32 devices in a mesh: row: 4 (over y, core), col: 8 (over z, x).
Axes of the slice: x: 2, y: 2, z: 4, core: 2. Of those that a mesh axis runs over, the one named last changes fastest.
Arguments:
- jac_tiles: bfloat16 [4096, 128, 128], P(('row', 'col')), may hold values from -0.0625 to 0.0625
- tile_pose: int32 [4096], P(('row', 'col')), may hold values from 0 to 63, as said below
- tile_point: int32 [4096], P(('row', 'col')), may hold values from 0 to 15
- tile_valid: int32 [4096], P(('row', 'col')), may hold values 0 or 1
- prior_weight: float32 [64, 128], P(('row', 'col')), may hold values from 0.1 to 1
- right_side: float32 [64, 128, 128], P(('row', 'col')), may hold values from -6 to 6
Outputs:
- solution: float32 [64, 128, 128], P(('row', 'col'))
- residual: float32 [64, 128, 128], P(('row', 'col'))
The draws below stay inside these ranges and needn't reach their ends.
Inputs may be any that keep to these rules, and one draw needn't show every extreme that they name: `tile_pose`: entry t belongs to device t // 128; pose block (a multi-camera rig's poses at one time step) k is held by device k // 2. On each device, all entries that name blocks of one holding device name the same one of its two blocks.
All inputs are finite; a program needn't handle non-finite values. No bound on the sum of `tile_valid` on one device may be relied on, other than what follows from the above.
Results may differ from the reference program's by a relative error of at most 0.0055.
Values may be sent and summed in bfloat16 or wider, within the bound.
No kernel may reach another device: no remote copies, remote signals or barrier semaphores. Data moves between devices by JAX's collectives and lax.ppermute only.
A program may use at most 128 MiB of HBM per device.

```python
import math
import jax
import jax.numpy as jnp
from jax import lax

BLK = 128
R = 128
TILES = 128
PT_DEV = 16
ITERS = 3
OWNERS = 32
POSES = 64
TILE_ROWS = 4096
N_ROW = 4
N_COL = 8


def draw_tile_pose(key, part):
    first_key, second_key = jax.random.split(jax.random.fold_in(key, 4711))
    count = OWNERS * TILES
    holders = jax.random.randint(first_key, (count,), 0, OWNERS)
    holders = holders.at[0].set(0).at[count - 1].set(OWNERS - 1)
    parity = jax.random.randint(second_key, (OWNERS, OWNERS), 0, 2)
    parity = parity.at[0, 0].set(0).at[OWNERS - 1, OWNERS - 1].set(1)
    device_of = jnp.arange(count) // TILES
    return (2 * holders + parity[device_of, holders]).astype(jnp.int32)


def touch_ends(values, rng, low, largest):
    dims = values.shape
    index_at = [jax.random.randint(jax.random.fold_in(rng, axis), (), 0, dims[axis]) for axis in range(len(dims))]
    values = values.at[tuple(index_at)].set(low)
    longest = dims.index(max(dims))
    index_at[longest] = (index_at[longest] + 1) % dims[longest]
    return values.at[tuple(index_at)].set(largest)


def level_of(rng, extent, cuts, smallest, largest):
    gain = 1.0
    for dim, shards_of in cuts:
        heights = jax.random.uniform(jax.random.fold_in(jax.random.fold_in(rng, 6), dim), (shards_of,), jnp.float32, smallest / len(cuts), largest / len(cuts))
        gain = gain * jnp.repeat(jnp.exp(heights), extent[dim] // shards_of).reshape((-1,) + (1,) * (len(extent) - 1 - dim))
    return gain


def normal_values(rng, extent, deviation, bound, shards=(), kind=jnp.bfloat16):
    array = jax.random.normal(rng, extent, jnp.float32) * deviation
    if len(shards) > 0:
        array = level_of(rng, extent, shards, -0.22, 0.18) * array
    return jnp.clip(array, min=-bound, max=bound).astype(kind)


def setup_inputs(seed: int = 0) -> dict:
    seeds = jax.random.split(jax.random.key(seed), 7)
    return {
        "jac_tiles": normal_values(seeds[0], (TILE_ROWS, BLK, BLK), (BLK * TILES // 2) ** -0.5, 0.0625, ((0, 32),)),
        "tile_pose": draw_tile_pose(jax.random.fold_in(seeds[6], 71), 0),
        "tile_point": touch_ends(jax.random.randint(seeds[2], (TILE_ROWS,), 0, PT_DEV), jax.random.fold_in(seeds[2], 1), 0, PT_DEV - 1).astype(jnp.int32),
        "tile_valid": touch_ends((jax.random.randint(seeds[3], (TILE_ROWS,), 0, 5) < 3).astype(jnp.int32), jax.random.fold_in(seeds[3], 1), 0, 1),
        "prior_weight": jnp.clip(jnp.exp(math.log(1.0) - 2.3025851 * jax.random.uniform(seeds[4], (POSES, BLK), jnp.float32) ** level_of(seeds[4], (POSES, BLK), ((0, 32),), -0.2, 0.2)), 0.1, 1.0),
        "right_side": normal_values(seeds[5], (POSES, BLK, R), 1.0, 6.0, ((0, 32),), jnp.float32),
    }


damping = 0.5
lowest = 0.5
highest = 8.0


def prior_term(field, prior_weight):
    owners = N_ROW * N_COL
    total = 2 * owners
    times = jnp.arange(total, dtype=jnp.int32)
    pos_of_time = jnp.where(times < owners, 2 * times, 2 * (total - 1 - times) + 1).astype(jnp.int32)
    positions = jnp.arange(total, dtype=jnp.int32)
    time_of = jnp.where(positions % 2 == 0, positions // 2, total - 1 - positions // 2).astype(jnp.int32)
    ordered = field[pos_of_time]
    weights = prior_weight[pos_of_time]
    flux = weights[:-1, :, None] * (ordered[1:] - ordered[:-1])
    zero_row = jnp.zeros((1,) + flux.shape[1:], jnp.float32)
    in_time = jnp.concatenate([zero_row, flux], axis=0) - jnp.concatenate([flux, zero_row], axis=0)
    return in_time[time_of]


def apply_operator(field, tiles, poses, points, valid, prior_weight):
    low = field.astype(jnp.bfloat16)

    def per_device(total, items):
        tile_block, pose_ids, point_ids, valid_ids = items
        masked = (tile_block * valid_ids.astype(jnp.bfloat16)[:, None, None]).astype(jnp.float32)
        rows = low[pose_ids].astype(jnp.float32)
        products = jnp.einsum("tij,tjk->tik", masked, rows, precision=lax.Precision.HIGHEST)
        sums = jax.ops.segment_sum(products, point_ids, num_segments=PT_DEV)
        sums = lax.optimization_barrier(sums.astype(jnp.bfloat16)).astype(jnp.float32)
        back = jnp.einsum("tij,tik->tjk", masked, sums[point_ids], precision=lax.Precision.HIGHEST)
        return total.at[pose_ids].add(back), None

    gram, _ = lax.scan(per_device, jnp.zeros(field.shape, jnp.float32), (tiles, poses, points, valid))
    return gram + prior_term(field, prior_weight) + damping * field


def reference(jac_tiles, tile_pose, tile_point, tile_valid, prior_weight, right_side):
    owners = N_ROW * N_COL
    tiles = jac_tiles.reshape(owners, TILES, BLK, BLK)
    poses = tile_pose.reshape(owners, TILES)
    points = tile_point.reshape(owners, TILES)
    valid = tile_valid.reshape(owners, TILES)
    theta = (highest + lowest) / 2.0
    delta = (highest - lowest) / 2.0
    sigma = theta / delta
    ratio = 1.0 / sigma
    step = right_side / theta
    solution = jnp.zeros(right_side.shape, jnp.float32)
    residual = right_side
    for turn in range(ITERS):
        if turn > 0:
            new_ratio = 1.0 / (2.0 * sigma - ratio)
            step = (new_ratio * ratio) * step + (2.0 * new_ratio / delta) * residual
            ratio = new_ratio
        solution = solution + step
        residual = residual - apply_operator(step, tiles, poses, points, valid, prior_weight)
    return solution, residual
```

```python
import functools

import jax
import jax.numpy as jnp
from jax import lax
from jax.experimental import pallas as pl
from jax.experimental.pallas import tpu as pltpu
from jax.sharding import PartitionSpec as P

PT_DEV = 16
ITERS = 3
UNROLL = 4

damping = 0.5
lowest = 0.5
highest = 8.0
BOTH = ("row", "col")


def pair_slots(key, groups, valid):
    tiles = key.shape[0]
    slots = -(-(tiles + groups) // (2 * UNROLL)) * 2 * UNROLL
    member = (key[:, None] == jnp.arange(groups, dtype=jnp.int32)[None, :]) & valid[:, None]
    counts = jnp.sum(member.astype(jnp.int32), axis=0)
    padded = (counts + 1) // 2 * 2
    ids = jnp.arange(groups, dtype=jnp.int32)
    start = jnp.sum(jnp.where(ids[None, :] < ids[:, None], padded[None, :], 0), axis=1)
    t = jnp.arange(tiles, dtype=jnp.int32)
    earlier = (key[None, :] == key[:, None]) & valid[None, :] & (t[None, :] < t[:, None])
    within = jnp.sum(earlier.astype(jnp.int32), axis=1)
    pos = jnp.sum(jnp.where(member, start[None, :], 0), axis=1) + within
    hit = (pos[None, :] == jnp.arange(slots, dtype=jnp.int32)[:, None]) & valid[None, :]
    pairs = (jnp.sum(padded) // 2).reshape(1)
    return hit, pairs


def pick(hit, values, empty=0):
    found = jnp.sum(jnp.where(hit, (values - empty)[None, :], 0), axis=1)
    return found + empty


def plan(tile_pose, tile_point, tile_valid, devices):
    valid = tile_valid > 0
    t = jnp.arange(tile_pose.shape[0], dtype=jnp.int32)
    hit, pairs = pair_slots(tile_point, PT_DEV, valid)
    fwd = [
        pairs,
        pick(hit, t),
        pick(hit, tile_pose),
        pick(hit, jnp.ones_like(t)),
        pick(hit, tile_point)[::2],
    ]
    hit, pairs = pair_slots(tile_pose // 2, devices, valid)
    bwd = [
        pairs,
        pick(hit, t),
        pick(hit, tile_point, PT_DEV),
        pick(hit, tile_pose)[::2],
    ]
    return jnp.concatenate(fwd), jnp.concatenate(bwd)


NT = (((1,), (1,)), ((), ()))
NN = (((1,), (0,)), ((), ()))


def gram_kernel(fwd_slots, bwd_slots, fwd, bwd, tiles, field, out, acc, low):
    acc[...] = jnp.zeros_like(acc)
    out[...] = jnp.zeros_like(out)

    def forward(i, _):
        for u in range(UNROLL):
            j = i * UNROLL + u
            tile = [fwd[1 + 2 * j + h] for h in range(2)]
            pose = [fwd[1 + fwd_slots + 2 * j + h] for h in range(2)]
            real = [fwd[1 + 2 * fwd_slots + 2 * j + h] for h in range(2)]
            point = fwd[1 + 3 * fwd_slots + j]
            left = field[pose[0]] * real[0].astype(jnp.float32).astype(jnp.bfloat16)
            right = field[pose[1]] * real[1].astype(jnp.float32).astype(jnp.bfloat16)
            acc[point] += lax.dot_general(
                jnp.concatenate([left, right], axis=1),
                jnp.concatenate([tiles[tile[0]], tiles[tile[1]]], axis=1),
                NT,
                preferred_element_type=jnp.float32,
            )
        return 0

    lax.fori_loop(0, (fwd[0] + UNROLL - 1) // UNROLL, forward, 0)
    low[: acc.shape[0]] = acc[...].astype(jnp.bfloat16)
    low[acc.shape[0]] = jnp.zeros(low.shape[1:], jnp.bfloat16)

    def backward(i, _):
        for u in range(UNROLL):
            j = i * UNROLL + u
            tile = [bwd[1 + 2 * j + h] for h in range(2)]
            point = [bwd[1 + bwd_slots + 2 * j + h] for h in range(2)]
            pose = bwd[1 + 2 * bwd_slots + j]
            out[pose] += lax.dot_general(
                jnp.concatenate([low[point[0]], low[point[1]]], axis=1),
                jnp.concatenate([tiles[tile[0]], tiles[tile[1]]], axis=0),
                NN,
                preferred_element_type=jnp.float32,
            )
        return 0

    lax.fori_loop(0, (bwd[0] + UNROLL - 1) // UNROLL, backward, 0)


def gram_product(fwd, bwd, tiles, field):
    blocks, rhs, params = field.shape
    points = tiles.shape[1]
    fwd_slots = (fwd.shape[0] - 1) * 2 // 7
    bwd_slots = (bwd.shape[0] - 1) * 2 // 5
    smem = pl.BlockSpec(memory_space=pltpu.SMEM)
    vmem = pl.BlockSpec(memory_space=pltpu.VMEM)
    return pl.pallas_call(
        functools.partial(gram_kernel, fwd_slots, bwd_slots),
        out_shape=jax.ShapeDtypeStruct((blocks, rhs, params), jnp.float32),
        in_specs=[smem, smem, vmem, vmem],
        out_specs=vmem,
        scratch_shapes=[
            pltpu.VMEM((PT_DEV, rhs, points), jnp.float32),
            pltpu.VMEM((PT_DEV + 1, rhs, points), jnp.bfloat16),
        ],
        compiler_params=pltpu.CompilerParams(vmem_limit_bytes=48 * 1024 * 1024),
        cost_estimate=pl.CostEstimate(
            flops=4 * tiles.shape[0] * rhs * params * points,
            bytes_accessed=tiles.size * 2 + field.size * 6,
            transcendentals=0,
        ),
    )(fwd, bwd, tiles, field)


def on_device(jac_tiles, tile_pose, tile_point, tile_valid, prior_weight, right_side):
    devices = lax.axis_size(BOTH)
    place = lax.axis_index(BOTH)
    is_first = place == 0
    is_last = place == devices - 1
    before = jnp.maximum(place - 1, 0)
    after = jnp.minimum(place + 1, devices - 1)
    fwd, bwd = plan(tile_pose, tile_point, tile_valid, devices)
    weights = lax.all_gather(prior_weight, BOTH, axis=0, tiled=True)
    left_weight = lax.dynamic_slice_in_dim(weights, 2 * before, 2, 0)
    right_weight = lax.dynamic_slice_in_dim(weights, 2 * after, 2, 0)
    zero = jnp.zeros_like(prior_weight[0])
    w_left = jnp.stack([jnp.where(is_first, zero, left_weight[0]), jnp.where(is_first, zero, prior_weight[1])])
    w_right = jnp.stack([prior_weight[0], jnp.where(is_last, prior_weight[0], right_weight[1])])
    w_left = w_left[:, None, :]
    w_right = w_right[:, None, :]

    theta = (highest + lowest) / 2.0
    delta = (highest - lowest) / 2.0
    sigma = theta / delta
    ratio = 1.0 / sigma
    right_side = jnp.swapaxes(right_side, 1, 2)
    step = right_side / theta
    solution = jnp.zeros(right_side.shape, jnp.float32)
    residual = right_side
    for turn in range(ITERS):
        if turn > 0:
            new_ratio = 1.0 / (2.0 * sigma - ratio)
            step = new_ratio * ratio * step + 2.0 * new_ratio / delta * residual
            ratio = new_ratio
        solution = solution + step
        field = lax.all_gather(step.astype(jnp.bfloat16), BOTH, axis=0, tiled=True)
        product = gram_product(fwd, bwd, jac_tiles, field)
        gram = lax.psum_scatter(product, BOTH, scatter_dimension=0, tiled=True)
        left = lax.dynamic_slice_in_dim(field, 2 * before, 2, 0).astype(jnp.float32)
        right = lax.dynamic_slice_in_dim(field, 2 * after, 2, 0).astype(jnp.float32)
        right = jnp.where(is_last, step[::-1], right)
        prior = w_left * (step - left) + w_right * (step - right)
        residual = residual - (gram + prior + damping * step)
    return jnp.swapaxes(solution, 1, 2), jnp.swapaxes(residual, 1, 2)


def solution(mesh):
    return jax.shard_map(
        on_device,
        mesh=mesh,
        in_specs=(
            P(BOTH, None, None),
            P(BOTH),
            P(BOTH),
            P(BOTH),
            P(BOTH, None),
            P(BOTH, None, None),
        ),
        out_specs=(P(BOTH, None, None), P(BOTH, None, None)),
        check_vma=False,
    )
```

```python
import functools

import jax
import jax.numpy as jnp
from jax import lax
from jax.experimental import pallas as pl
from jax.experimental.pallas import tpu as pltpu
from jax.sharding import PartitionSpec as P

PT_DEV = 16
ITERS = 3
UNROLL = 4

damping = 0.5
lowest = 0.5
highest = 8.0
BOTH = ("row", "col")


def pair_slots(key, groups, valid):
    tiles = key.shape[0]
    slots = -(-(tiles + groups) // (2 * UNROLL)) * 2 * UNROLL
    member = (key[:, None] == jnp.arange(groups, dtype=jnp.int32)[None, :]) & valid[:, None]
    counts = jnp.sum(member.astype(jnp.int32), axis=0)
    padded = (counts + 1) // 2 * 2
    ids = jnp.arange(groups, dtype=jnp.int32)
    start = jnp.sum(jnp.where(ids[None, :] < ids[:, None], padded[None, :], 0), axis=1)
    t = jnp.arange(tiles, dtype=jnp.int32)
    earlier = (key[None, :] == key[:, None]) & valid[None, :] & (t[None, :] < t[:, None])
    within = jnp.sum(earlier.astype(jnp.int32), axis=1)
    pos = jnp.sum(jnp.where(member, start[None, :], 0), axis=1) + within
    hit = (pos[None, :] == jnp.arange(slots, dtype=jnp.int32)[:, None]) & valid[None, :]
    pairs = (jnp.sum(padded) // 2).reshape(1)
    return hit, pairs


def pick(hit, values, empty=0):
    found = jnp.sum(jnp.where(hit, (values - empty)[None, :], 0), axis=1)
    return found + empty


def plan(tile_pose, tile_point, tile_valid, devices):
    valid = tile_valid > 0
    t = jnp.arange(tile_pose.shape[0], dtype=jnp.int32)
    hit, pairs = pair_slots(tile_point, PT_DEV, valid)
    fwd = [
        pairs,
        pick(hit, t),
        pick(hit, tile_pose // 2),
        pick(hit, jnp.ones_like(t)),
        pick(hit, tile_point)[::2],
    ]
    hit, pairs = pair_slots(tile_pose // 2, devices, valid)
    bwd = [
        pairs,
        pick(hit, t),
        pick(hit, tile_point, PT_DEV),
        pick(hit, tile_pose // 2)[::2],
    ]
    return jnp.concatenate(fwd), jnp.concatenate(bwd)


NT = (((1,), (1,)), ((), ()))
NN = (((1,), (0,)), ((), ()))


def gram_kernel(fwd_slots, bwd_slots, fwd, bwd, tiles, field, out, acc, low, total):
    acc[...] = jnp.zeros_like(acc)
    total[...] = jnp.zeros_like(total)

    def forward(i, _):
        for u in range(UNROLL):
            j = i * UNROLL + u
            tile = [fwd[1 + 2 * j + h] for h in range(2)]
            pose = [fwd[1 + fwd_slots + 2 * j + h] for h in range(2)]
            real = [fwd[1 + 2 * fwd_slots + 2 * j + h] for h in range(2)]
            point = fwd[1 + 3 * fwd_slots + j]
            left = field[pose[0]] * real[0].astype(jnp.float32).astype(jnp.bfloat16)
            right = field[pose[1]] * real[1].astype(jnp.float32).astype(jnp.bfloat16)
            acc[point] += lax.dot_general(
                jnp.concatenate([left, right], axis=1),
                jnp.concatenate([tiles[tile[0]], tiles[tile[1]]], axis=1),
                NT,
                preferred_element_type=jnp.float32,
            )
        return 0

    lax.fori_loop(0, (fwd[0] + UNROLL - 1) // UNROLL, forward, 0)
    low[: acc.shape[0]] = acc[...].astype(jnp.bfloat16)
    low[acc.shape[0]] = jnp.zeros(low.shape[1:], jnp.bfloat16)

    def backward(i, _):
        for u in range(UNROLL):
            j = i * UNROLL + u
            tile = [bwd[1 + 2 * j + h] for h in range(2)]
            point = [bwd[1 + bwd_slots + 2 * j + h] for h in range(2)]
            pose = bwd[1 + 2 * bwd_slots + j]
            total[pose] += lax.dot_general(
                jnp.concatenate([low[point[0]], low[point[1]]], axis=1),
                jnp.concatenate([tiles[tile[0]], tiles[tile[1]]], axis=0),
                NN,
                preferred_element_type=jnp.float32,
            )
        return 0

    lax.fori_loop(0, (bwd[0] + UNROLL - 1) // UNROLL, backward, 0)
    out[...] = total[...].astype(out.dtype)


def gram_product(fwd, bwd, tiles, field):
    blocks, rhs, params = field.shape
    points = tiles.shape[1]
    fwd_slots = (fwd.shape[0] - 1) * 2 // 7
    bwd_slots = (bwd.shape[0] - 1) * 2 // 5
    smem = pl.BlockSpec(memory_space=pltpu.SMEM)
    vmem = pl.BlockSpec(memory_space=pltpu.VMEM)
    return pl.pallas_call(
        functools.partial(gram_kernel, fwd_slots, bwd_slots),
        out_shape=jax.ShapeDtypeStruct((blocks, rhs, params), jnp.bfloat16),
        in_specs=[smem, smem, vmem, vmem],
        out_specs=vmem,
        scratch_shapes=[
            pltpu.VMEM((PT_DEV, rhs, points), jnp.float32),
            pltpu.VMEM((PT_DEV + 1, rhs, points), jnp.bfloat16),
            pltpu.VMEM((blocks, rhs, params), jnp.float32),
        ],
        compiler_params=pltpu.CompilerParams(vmem_limit_bytes=48 * 1024 * 1024),
        cost_estimate=pl.CostEstimate(
            flops=4 * tiles.shape[0] * rhs * params * points,
            bytes_accessed=tiles.size * 2 + field.size * 6,
            transcendentals=0,
        ),
    )(fwd, bwd, tiles, field)


def shifted(block, distance):
    devices = range(lax.axis_size(BOTH))
    route = [(i - distance, i) for i in devices if i - distance in devices]
    return lax.ppermute(block, BOTH, route)


def on_device(jac_tiles, tile_pose, tile_point, tile_valid, prior_weight, right_side):
    devices = lax.axis_size(BOTH)
    place = lax.axis_index(BOTH)
    is_first = place == 0
    is_last = place == devices - 1
    fwd, bwd = plan(tile_pose, tile_point, tile_valid, devices)
    left_weight = shifted(prior_weight, 1)
    right_weight = shifted(prior_weight, -1)
    needed = jnp.max(
        jnp.where(
            (tile_pose // 2)[None, :] == jnp.arange(devices, dtype=jnp.int32)[:, None],
            (tile_pose % 2)[None, :],
            0,
        ),
        axis=1,
    )
    wanted = lax.all_to_all(needed, BOTH, split_axis=0, concat_axis=0, tiled=True)
    first_wanted = (wanted == 0)[:, None, None]
    zero = jnp.zeros_like(prior_weight[0])
    w_left = jnp.stack([jnp.where(is_first, zero, left_weight[0]), jnp.where(is_first, zero, prior_weight[1])])
    w_right = jnp.stack([prior_weight[0], jnp.where(is_last, prior_weight[0], right_weight[1])])
    w_left = w_left[:, None, :]
    w_right = w_right[:, None, :]

    theta = (highest + lowest) / 2.0
    delta = (highest - lowest) / 2.0
    sigma = theta / delta
    ratio = 1.0 / sigma
    right_side = jnp.swapaxes(right_side, 1, 2)
    step = right_side / theta
    solution = jnp.zeros(right_side.shape, jnp.float32)
    residual = right_side
    for turn in range(ITERS):
        if turn > 0:
            new_ratio = 1.0 / (2.0 * sigma - ratio)
            step = new_ratio * ratio * step + 2.0 * new_ratio / delta * residual
            ratio = new_ratio
        solution = solution + step
        low = step.astype(jnp.bfloat16)
        outgoing = jnp.where(first_wanted, low[0], low[1])
        field = lax.all_to_all(outgoing, BOTH, split_axis=0, concat_axis=0, tiled=True)
        low, field = lax.optimization_barrier((low, field))
        left = shifted(low, 1).astype(jnp.float32)
        right = shifted(low, -1).astype(jnp.float32)
        product = gram_product(fwd, bwd, jac_tiles, field)
        product, left, right = lax.optimization_barrier((product, left, right))
        back = lax.all_to_all(product, BOTH, split_axis=0, concat_axis=0, tiled=True)
        back = back.astype(jnp.float32)
        gram = jnp.stack(
            [
                jnp.sum(jnp.where(first_wanted, back, 0.0), axis=0),
                jnp.sum(jnp.where(first_wanted, 0.0, back), axis=0),
            ]
        )
        right = jnp.where(is_last, step[::-1], right)
        prior = w_left * (step - left) + w_right * (step - right)
        residual = residual - (gram + prior + damping * step)
    return jnp.swapaxes(solution, 1, 2), jnp.swapaxes(residual, 1, 2)


def solution(mesh):
    return jax.shard_map(
        on_device,
        mesh=mesh,
        in_specs=(
            P(BOTH, None, None),
            P(BOTH),
            P(BOTH),
            P(BOTH),
            P(BOTH, None),
            P(BOTH, None, None),
        ),
        out_specs=(P(BOTH, None, None), P(BOTH, None, None)),
        check_vma=False,
    )
```

```python
import functools

import jax
import jax.numpy as jnp
from jax import lax
from jax.experimental import pallas as pl
from jax.experimental.pallas import tpu as pltpu
from jax.sharding import PartitionSpec as P

PT_DEV = 16
ITERS = 3
UNROLL = 4

damping = 0.5
lowest = 0.5
highest = 8.0
BOTH = ("row", "col")


class Grid:
    def __init__(self):
        rows = lax.axis_size("row")
        cols = lax.axis_size("col")
        self.sizes = {"y": rows // 2, "core": 2, "z": cols // 2, "x": 2}
        self.count = rows * cols

    def coords(self, device):
        cols = self.sizes["z"] * 2
        if isinstance(device, int):
            row, col = device // cols, device % cols
            return {"y": row // 2, "core": row % 2, "z": col // 2, "x": col % 2}
        row, col = lax.div(device, cols), lax.rem(device, cols)
        return {"y": lax.div(row, 2), "core": lax.rem(row, 2), "z": lax.div(col, 2), "x": lax.rem(col, 2)}

    def device(self, at):
        row = at["y"] * 2 + at["core"]
        col = at["z"] * 2 + at["x"]
        return row * self.sizes["z"] * 2 + col

    def slot(self, device, home):
        at, base = self.coords(device), self.coords(home)
        away = {a: lax.rem(at[a] - base[a] + n, n) for a, n in self.sizes.items()}
        plane = (away["core"] * self.sizes["y"] + away["y"]) * 2 + away["x"]
        return plane * self.sizes["z"] + away["z"]

    def send(self, block, axis, distance):
        route = []
        for source in range(self.count):
            at = self.coords(source)
            at[axis] = (at[axis] + distance) % self.sizes[axis]
            route.append((source, self.device(at)))
        return lax.ppermute(block, BOTH, route)

    def fetch(self, block, axis, distance):
        return self.send(block, axis, -distance)


def gather_field(grid, low):
    depth, wide = grid.sizes["z"], grid.sizes["y"]
    base = jnp.concatenate([low] + [grid.fetch(low, "z", r) for r in range(1, depth)])
    half = base.shape[0] // 2
    if wide == 2:
        over_x = grid.fetch(base, "x", 1)
        over_y = grid.fetch(base, "y", 1)
        corner = [grid.fetch(over_y[:half], "x", 1), grid.fetch(over_x[half:], "y", 1)]
        pieces = [base, over_x, over_y] + corner
    else:
        lines = [base] + [grid.fetch(base, "y", r) for r in range(1, wide)]
        pieces = []
        for line in lines:
            pieces += [line, grid.fetch(line, "x", 1)]
    return pieces + [grid.fetch(piece, "core", 1) for piece in pieces]


def scatter_sum(grid, own, other):
    depth, wide = grid.sizes["z"], grid.sizes["y"]
    arrived = grid.send(other, "core", 1)
    total = own.astype(jnp.float32) + arrived.astype(jnp.float32)
    total = total.reshape((wide, 2, 2 * depth) + total.shape[1:])

    def narrow(v):
        return v.astype(jnp.bfloat16)

    def widen(v):
        return v.astype(jnp.float32)

    if wide == 2:
        over_x = grid.send(narrow(total[1, 1, :depth]), "x", 1)
        over_y = grid.send(narrow(total[1, 1, depth:]), "y", 1)
        to_y = narrow(jnp.concatenate([total[1, 0, :depth] + widen(over_x), total[1, 0, depth:]]))
        to_x = narrow(jnp.concatenate([total[0, 1, :depth], total[0, 1, depth:] + widen(over_y)]))
        base = total[0, 0] + widen(grid.send(to_y, "y", 1)) + widen(grid.send(to_x, "x", 1))
    else:
        total = total[:, 0] + widen(grid.send(narrow(total[:, 1]), "x", 1))
        base = total[0]
        for r in range(1, wide):
            base = base + widen(grid.send(narrow(total[r]), "y", r))
    base = base.reshape((depth, 2) + base.shape[1:])
    gram = base[0]
    for r in range(1, depth):
        gram = gram + widen(grid.send(narrow(base[r]), "z", r))
    return gram


def pair_slots(key, groups, valid):
    tiles = key.shape[0]
    slots = -(-(tiles + groups) // (2 * UNROLL)) * 2 * UNROLL
    member = (key[:, None] == jnp.arange(groups, dtype=jnp.int32)[None, :]) & valid[:, None]
    counts = jnp.sum(member.astype(jnp.int32), axis=0)
    padded = (counts + 1) // 2 * 2
    ids = jnp.arange(groups, dtype=jnp.int32)
    start = jnp.sum(jnp.where(ids[None, :] < ids[:, None], padded[None, :], 0), axis=1)
    t = jnp.arange(tiles, dtype=jnp.int32)
    earlier = (key[None, :] == key[:, None]) & valid[None, :] & (t[None, :] < t[:, None])
    within = jnp.sum(earlier.astype(jnp.int32), axis=1)
    pos = jnp.sum(jnp.where(member, start[None, :], 0), axis=1) + within
    hit = (pos[None, :] == jnp.arange(slots, dtype=jnp.int32)[:, None]) & valid[None, :]
    pairs = (jnp.sum(padded) // 2).reshape(1)
    return hit, pairs


def pick(hit, values, empty=0):
    found = jnp.sum(jnp.where(hit, (values - empty)[None, :], 0), axis=1)
    return found + empty


def plan(grid, place, tile_pose, tile_point, tile_valid):
    valid = tile_valid > 0
    t = jnp.arange(tile_pose.shape[0], dtype=jnp.int32)
    holder = grid.slot(tile_pose // 2, place)
    pose = 2 * holder + tile_pose % 2
    before = jnp.maximum(place - 1, 0)
    after = jnp.minimum(place + 1, grid.count - 1)
    sides = jnp.stack([grid.slot(before, place), grid.slot(after, place)])
    hit, pairs = pair_slots(tile_point, PT_DEV, valid)
    fwd = [
        pairs,
        2 * sides,
        pick(hit, t),
        pick(hit, pose),
        pick(hit, jnp.ones_like(t)),
        pick(hit, tile_point)[::2],
    ]
    hit, pairs = pair_slots(holder, grid.count, valid)
    bwd = [
        pairs,
        pick(hit, t),
        pick(hit, tile_point, PT_DEV),
        pick(hit, pose)[::2],
    ]
    return jnp.concatenate(fwd), jnp.concatenate(bwd)


NT = (((1,), (1,)), ((), ()))
NN = (((1,), (0,)), ((), ()))


def gram_kernel(fwd_slots, bwd_slots, fwd, bwd, tiles, *refs):
    pieces, (own, other, sides, field, acc, low, total) = refs[:-7], refs[-7:]
    start = 0
    for piece in pieces:
        field[start : start + piece.shape[0]] = piece[...]
        start += piece.shape[0]
    for side in range(2):
        sides[side] = field[pl.ds(fwd[1 + side], 2)]
    acc[...] = jnp.zeros_like(acc)
    total[...] = jnp.zeros_like(total)

    def forward(i, _):
        for u in range(UNROLL):
            j = i * UNROLL + u
            tile = [fwd[3 + 2 * j + h] for h in range(2)]
            pose = [fwd[3 + fwd_slots + 2 * j + h] for h in range(2)]
            real = [fwd[3 + 2 * fwd_slots + 2 * j + h] for h in range(2)]
            point = fwd[3 + 3 * fwd_slots + j]
            left = field[pose[0]] * real[0].astype(jnp.float32).astype(jnp.bfloat16)
            right = field[pose[1]] * real[1].astype(jnp.float32).astype(jnp.bfloat16)
            acc[point] += lax.dot_general(
                jnp.concatenate([left, right], axis=1),
                jnp.concatenate([tiles[tile[0]], tiles[tile[1]]], axis=1),
                NT,
                preferred_element_type=jnp.float32,
            )
        return 0

    lax.fori_loop(0, (fwd[0] + UNROLL - 1) // UNROLL, forward, 0)
    low[: acc.shape[0]] = acc[...].astype(jnp.bfloat16)
    low[acc.shape[0]] = jnp.zeros(low.shape[1:], jnp.bfloat16)

    def backward(i, _):
        for u in range(UNROLL):
            j = i * UNROLL + u
            tile = [bwd[1 + 2 * j + h] for h in range(2)]
            point = [bwd[1 + bwd_slots + 2 * j + h] for h in range(2)]
            pose = bwd[1 + 2 * bwd_slots + j]
            total[pose] += lax.dot_general(
                jnp.concatenate([low[point[0]], low[point[1]]], axis=1),
                jnp.concatenate([tiles[tile[0]], tiles[tile[1]]], axis=0),
                NN,
                preferred_element_type=jnp.float32,
            )
        return 0

    lax.fori_loop(0, (bwd[0] + UNROLL - 1) // UNROLL, backward, 0)
    half = own.shape[0]
    other[...] = total[half:].astype(other.dtype)
    own[...] = total[:half].astype(own.dtype)


def gram_product(fwd, bwd, tiles, pieces):
    blocks = sum(piece.shape[0] for piece in pieces)
    rhs, params = pieces[0].shape[1:]
    points = tiles.shape[1]
    fwd_slots = (fwd.shape[0] - 3) * 2 // 7
    bwd_slots = (bwd.shape[0] - 1) * 2 // 5
    smem = pl.BlockSpec(memory_space=pltpu.SMEM)
    vmem = pl.BlockSpec(memory_space=pltpu.VMEM)
    return pl.pallas_call(
        functools.partial(gram_kernel, fwd_slots, bwd_slots),
        out_shape=[
            jax.ShapeDtypeStruct((blocks // 2, rhs, params), jnp.bfloat16),
            jax.ShapeDtypeStruct((blocks // 2, rhs, params), jnp.bfloat16),
            jax.ShapeDtypeStruct((2, 2, rhs, params), jnp.bfloat16),
        ],
        in_specs=[smem, smem, vmem] + [vmem] * len(pieces),
        out_specs=[vmem] * 3,
        scratch_shapes=[
            pltpu.VMEM((blocks, rhs, params), jnp.bfloat16),
            pltpu.VMEM((PT_DEV, rhs, points), jnp.float32),
            pltpu.VMEM((PT_DEV + 1, rhs, points), jnp.bfloat16),
            pltpu.VMEM((blocks, rhs, params), jnp.float32),
        ],
        compiler_params=pltpu.CompilerParams(vmem_limit_bytes=(7 * blocks // 32 + 8) * 1024 * 1024),
        cost_estimate=pl.CostEstimate(
            flops=4 * tiles.shape[0] * rhs * params * points,
            bytes_accessed=tiles.size * 2 + blocks * rhs * params * 4,
            transcendentals=0,
        ),
    )(fwd, bwd, tiles, *pieces)


def shifted(block, distance):
    devices = range(lax.axis_size(BOTH))
    route = [(i - distance, i) for i in devices if i - distance in devices]
    return lax.ppermute(block, BOTH, route)


def on_device(jac_tiles, tile_pose, tile_point, tile_valid, prior_weight, right_side):
    grid = Grid()
    place = lax.axis_index(BOTH)
    is_first = place == 0
    is_last = place == grid.count - 1
    fwd, bwd = plan(grid, place, tile_pose, tile_point, tile_valid)
    left_weight = shifted(prior_weight, 1)
    right_weight = shifted(prior_weight, -1)
    zero = jnp.zeros_like(prior_weight[0])
    w_left = jnp.stack([jnp.where(is_first, zero, left_weight[0]), jnp.where(is_first, zero, prior_weight[1])])
    w_right = jnp.stack([prior_weight[0], jnp.where(is_last, prior_weight[0], right_weight[1])])
    w_left = w_left[:, None, :]
    w_right = w_right[:, None, :]

    theta = (highest + lowest) / 2.0
    delta = (highest - lowest) / 2.0
    sigma = theta / delta
    ratio = 1.0 / sigma
    right_side = jnp.swapaxes(right_side, 1, 2)
    step = right_side / theta
    solution = jnp.zeros(right_side.shape, jnp.float32)
    residual = right_side
    for turn in range(ITERS):
        if turn > 0:
            new_ratio = 1.0 / (2.0 * sigma - ratio)
            step = new_ratio * ratio * step + 2.0 * new_ratio / delta * residual
            ratio = new_ratio
        solution = solution + step
        pieces = gather_field(grid, step.astype(jnp.bfloat16))
        own, other, sides = gram_product(fwd, bwd, jac_tiles, pieces)
        gram = scatter_sum(grid, own, other)
        left, right = sides.astype(jnp.float32)
        right = jnp.where(is_last, step[::-1], right)
        prior = w_left * (step - left) + w_right * (step - right)
        residual = residual - (gram + prior + damping * step)
    return jnp.swapaxes(solution, 1, 2), jnp.swapaxes(residual, 1, 2)


def solution(mesh):
    return jax.shard_map(
        on_device,
        mesh=mesh,
        in_specs=(
            P(BOTH, None, None),
            P(BOTH),
            P(BOTH),
            P(BOTH),
            P(BOTH, None),
            P(BOTH, None, None),
        ),
        out_specs=(P(BOTH, None, None), P(BOTH, None, None)),
        check_vma=False,
    )
```

```python
import functools

import jax
import jax.numpy as jnp
from jax import lax
from jax.experimental import pallas as pl
from jax.experimental.pallas import tpu as pltpu
from jax.sharding import PartitionSpec as P

PT_DEV = 16
ITERS = 3
UNROLL = 4

damping = 0.5
lowest = 0.5
highest = 8.0
BOTH = ("row", "col")


class Grid:
    def __init__(self):
        rows = lax.axis_size("row")
        cols = lax.axis_size("col")
        self.sizes = {"y": rows // 2, "core": 2, "z": cols // 2, "x": 2}
        self.count = rows * cols

    def coords(self, device):
        cols = self.sizes["z"] * 2
        if isinstance(device, int):
            row, col = device // cols, device % cols
            return {"y": row // 2, "core": row % 2, "z": col // 2, "x": col % 2}
        row, col = lax.div(device, cols), lax.rem(device, cols)
        return {"y": lax.div(row, 2), "core": lax.rem(row, 2), "z": lax.div(col, 2), "x": lax.rem(col, 2)}

    def device(self, at):
        row = at["y"] * 2 + at["core"]
        col = at["z"] * 2 + at["x"]
        return row * self.sizes["z"] * 2 + col

    def slot(self, device, home):
        at, base = self.coords(device), self.coords(home)
        away = {a: lax.rem(at[a] - base[a] + n, n) for a, n in self.sizes.items()}
        plane = (away["core"] * self.sizes["y"] + away["y"]) * 2 + away["x"]
        return plane * self.sizes["z"] + away["z"]

    def send(self, block, axis, distance):
        route = []
        for source in range(self.count):
            at = self.coords(source)
            for name in axis.split():
                at[name] = (at[name] + distance) % self.sizes[name]
            route.append((source, self.device(at)))
        return lax.ppermute(block, BOTH, route)

    def fetch(self, block, axis, distance):
        return self.send(block, axis, -distance)


def gather_field(grid, low):
    depth, wide = grid.sizes["z"], grid.sizes["y"]
    column = [low] + [grid.fetch(low, "z", r) for r in range(1, depth)]
    if wide == 2:
        corner = grid.fetch(low, "x y", 1)
        base = jnp.concatenate(column)
        far = [corner] + [grid.fetch(corner, "z", r) for r in range(1, depth)]
        over_x = grid.fetch(base, "x", 1)
        over_y = grid.fetch(base, "y", 1)
        pieces = [base, over_x, over_y, jnp.concatenate(far)]
    else:
        base = jnp.concatenate(column)
        lines = [base] + [grid.fetch(base, "y", r) for r in range(1, wide)]
        pieces = []
        for line in lines:
            pieces += [line, grid.fetch(line, "x", 1)]
    return pieces + [grid.fetch(piece, "core", 1) for piece in pieces]


def scatter_sum(grid, own, other):
    depth, wide = grid.sizes["z"], grid.sizes["y"]
    arrived = grid.send(other, "core", 1)
    total = own.astype(jnp.float32) + arrived.astype(jnp.float32)
    total = total.reshape((wide, 2, depth, 2) + total.shape[1:])

    def narrow(v):
        return v.astype(jnp.bfloat16)

    def widen(v):
        return v.astype(jnp.float32)

    if wide == 2:
        corner = total[1, 1, 0]
        for r in range(1, depth):
            corner = corner + widen(grid.send(narrow(total[1, 1, r]), "z", r))
        base = total[0, 0] + widen(grid.send(narrow(total[0, 1]), "x", 1))
        base = base + widen(grid.send(narrow(total[1, 0]), "y", 1))
        gram = base[0] + widen(grid.send(narrow(corner), "x y", 1))
    else:
        total = total[:, 0] + widen(grid.send(narrow(total[:, 1]), "x", 1))
        base = total[0]
        for r in range(1, wide):
            base = base + widen(grid.send(narrow(total[r]), "y", r))
        gram = base[0]
    for r in range(1, depth):
        gram = gram + widen(grid.send(narrow(base[r]), "z", r))
    return gram


def pair_slots(key, groups, valid):
    tiles = key.shape[0]
    slots = -(-(tiles + groups) // (2 * UNROLL)) * 2 * UNROLL
    member = (key[:, None] == jnp.arange(groups, dtype=jnp.int32)[None, :]) & valid[:, None]
    counts = jnp.sum(member.astype(jnp.int32), axis=0)
    padded = (counts + 1) // 2 * 2
    ids = jnp.arange(groups, dtype=jnp.int32)
    start = jnp.sum(jnp.where(ids[None, :] < ids[:, None], padded[None, :], 0), axis=1)
    t = jnp.arange(tiles, dtype=jnp.int32)
    earlier = (key[None, :] == key[:, None]) & valid[None, :] & (t[None, :] < t[:, None])
    within = jnp.sum(earlier.astype(jnp.int32), axis=1)
    pos = jnp.sum(jnp.where(member, start[None, :], 0), axis=1) + within
    hit = (pos[None, :] == jnp.arange(slots, dtype=jnp.int32)[:, None]) & valid[None, :]
    pairs = (jnp.sum(padded) // 2).reshape(1)
    return hit, pairs


def pick(hit, values, empty=0):
    found = jnp.sum(jnp.where(hit, (values - empty)[None, :], 0), axis=1)
    return found + empty


def plan(grid, place, tile_pose, tile_point, tile_valid):
    valid = tile_valid > 0
    t = jnp.arange(tile_pose.shape[0], dtype=jnp.int32)
    holder = grid.slot(tile_pose // 2, place)
    pose = 2 * holder + tile_pose % 2
    before = jnp.maximum(place - 1, 0)
    after = jnp.minimum(place + 1, grid.count - 1)
    sides = jnp.stack([grid.slot(before, place), grid.slot(after, place)])
    hit, pairs = pair_slots(tile_point, PT_DEV, valid)
    fwd = [
        pairs,
        2 * sides,
        pick(hit, t),
        pick(hit, pose),
        pick(hit, jnp.ones_like(t)),
        pick(hit, tile_point)[::2],
    ]
    hit, pairs = pair_slots(holder, grid.count, valid)
    bwd = [
        pairs,
        pick(hit, t),
        pick(hit, tile_point, PT_DEV),
        pick(hit, pose)[::2],
    ]
    return jnp.concatenate(fwd), jnp.concatenate(bwd)


NT = (((1,), (1,)), ((), ()))
NN = (((1,), (0,)), ((), ()))


def gram_kernel(fwd_slots, bwd_slots, fwd, bwd, tiles, *refs):
    pieces, (own, other, sides, field, acc, low, total) = refs[:-7], refs[-7:]
    start = 0
    for piece in pieces:
        field[start : start + piece.shape[0]] = piece[...]
        start += piece.shape[0]
    for side in range(2):
        sides[side] = field[pl.ds(fwd[1 + side], 2)]
    acc[...] = jnp.zeros_like(acc)
    total[...] = jnp.zeros_like(total)

    def forward(i, _):
        for u in range(UNROLL):
            j = i * UNROLL + u
            tile = [fwd[3 + 2 * j + h] for h in range(2)]
            pose = [fwd[3 + fwd_slots + 2 * j + h] for h in range(2)]
            real = [fwd[3 + 2 * fwd_slots + 2 * j + h] for h in range(2)]
            point = fwd[3 + 3 * fwd_slots + j]
            left = field[pose[0]] * real[0].astype(jnp.float32).astype(jnp.bfloat16)
            right = field[pose[1]] * real[1].astype(jnp.float32).astype(jnp.bfloat16)
            acc[point] += lax.dot_general(
                jnp.concatenate([left, right], axis=1),
                jnp.concatenate([tiles[tile[0]], tiles[tile[1]]], axis=1),
                NT,
                preferred_element_type=jnp.float32,
            )
        return 0

    lax.fori_loop(0, (fwd[0] + UNROLL - 1) // UNROLL, forward, 0)
    low[: acc.shape[0]] = acc[...].astype(jnp.bfloat16)
    low[acc.shape[0]] = jnp.zeros(low.shape[1:], jnp.bfloat16)

    def backward(i, _):
        for u in range(UNROLL):
            j = i * UNROLL + u
            tile = [bwd[1 + 2 * j + h] for h in range(2)]
            point = [bwd[1 + bwd_slots + 2 * j + h] for h in range(2)]
            pose = bwd[1 + 2 * bwd_slots + j]
            total[pose] += lax.dot_general(
                jnp.concatenate([low[point[0]], low[point[1]]], axis=1),
                jnp.concatenate([tiles[tile[0]], tiles[tile[1]]], axis=0),
                NN,
                preferred_element_type=jnp.float32,
            )
        return 0

    lax.fori_loop(0, (bwd[0] + UNROLL - 1) // UNROLL, backward, 0)
    half = own.shape[0]
    other[...] = total[half:].astype(other.dtype)
    own[...] = total[:half].astype(own.dtype)


def gram_product(fwd, bwd, tiles, pieces):
    blocks = sum(piece.shape[0] for piece in pieces)
    rhs, params = pieces[0].shape[1:]
    points = tiles.shape[1]
    fwd_slots = (fwd.shape[0] - 3) * 2 // 7
    bwd_slots = (bwd.shape[0] - 1) * 2 // 5
    smem = pl.BlockSpec(memory_space=pltpu.SMEM)
    vmem = pl.BlockSpec(memory_space=pltpu.VMEM)
    return pl.pallas_call(
        functools.partial(gram_kernel, fwd_slots, bwd_slots),
        out_shape=[
            jax.ShapeDtypeStruct((blocks // 2, rhs, params), jnp.bfloat16),
            jax.ShapeDtypeStruct((blocks // 2, rhs, params), jnp.bfloat16),
            jax.ShapeDtypeStruct((2, 2, rhs, params), jnp.bfloat16),
        ],
        in_specs=[smem, smem, vmem] + [vmem] * len(pieces),
        out_specs=[vmem] * 3,
        scratch_shapes=[
            pltpu.VMEM((blocks, rhs, params), jnp.bfloat16),
            pltpu.VMEM((PT_DEV, rhs, points), jnp.float32),
            pltpu.VMEM((PT_DEV + 1, rhs, points), jnp.bfloat16),
            pltpu.VMEM((blocks, rhs, params), jnp.float32),
        ],
        compiler_params=pltpu.CompilerParams(vmem_limit_bytes=(7 * blocks // 32 + 8) * 1024 * 1024),
        cost_estimate=pl.CostEstimate(
            flops=4 * tiles.shape[0] * rhs * params * points,
            bytes_accessed=tiles.size * 2 + blocks * rhs * params * 4,
            transcendentals=0,
        ),
    )(fwd, bwd, tiles, *pieces)


def shifted(block, distance):
    devices = range(lax.axis_size(BOTH))
    route = [(i - distance, i) for i in devices if i - distance in devices]
    return lax.ppermute(block, BOTH, route)


def on_device(jac_tiles, tile_pose, tile_point, tile_valid, prior_weight, right_side):
    grid = Grid()
    place = lax.axis_index(BOTH)
    is_first = place == 0
    is_last = place == grid.count - 1
    fwd, bwd = plan(grid, place, tile_pose, tile_point, tile_valid)
    left_weight = shifted(prior_weight, 1)
    right_weight = shifted(prior_weight, -1)
    zero = jnp.zeros_like(prior_weight[0])
    w_left = jnp.stack([jnp.where(is_first, zero, left_weight[0]), jnp.where(is_first, zero, prior_weight[1])])
    w_right = jnp.stack([prior_weight[0], jnp.where(is_last, prior_weight[0], right_weight[1])])
    w_left = w_left[:, None, :]
    w_right = w_right[:, None, :]

    theta = (highest + lowest) / 2.0
    delta = (highest - lowest) / 2.0
    sigma = theta / delta
    ratio = 1.0 / sigma
    right_side = jnp.swapaxes(right_side, 1, 2)
    step = right_side / theta
    solution = jnp.zeros(right_side.shape, jnp.float32)
    residual = right_side
    for turn in range(ITERS):
        if turn > 0:
            new_ratio = 1.0 / (2.0 * sigma - ratio)
            step = new_ratio * ratio * step + 2.0 * new_ratio / delta * residual
            ratio = new_ratio
        solution = solution + step
        pieces = gather_field(grid, step.astype(jnp.bfloat16))
        own, other, sides = gram_product(fwd, bwd, jac_tiles, pieces)
        gram = scatter_sum(grid, own, other)
        left, right = sides.astype(jnp.float32)
        right = jnp.where(is_last, step[::-1], right)
        prior = w_left * (step - left) + w_right * (step - right)
        residual = residual - (gram + prior + damping * step)
    return jnp.swapaxes(solution, 1, 2), jnp.swapaxes(residual, 1, 2)


def solution(mesh):
    return jax.shard_map(
        on_device,
        mesh=mesh,
        in_specs=(
            P(BOTH, None, None),
            P(BOTH),
            P(BOTH),
            P(BOTH),
            P(BOTH, None),
            P(BOTH, None, None),
        ),
        out_specs=(P(BOTH, None, None), P(BOTH, None, None)),
        check_vma=False,
    )
```

```python
import functools

import jax
import jax.numpy as jnp
from jax import lax
from jax.experimental import pallas as pl
from jax.experimental.pallas import tpu as pltpu
from jax.sharding import PartitionSpec as P

PT_DEV = 16
ITERS = 3
UNROLL = 4

damping = 0.5
lowest = 0.5
highest = 8.0
BOTH = ("row", "col")


class Grid:
    def __init__(self):
        rows = lax.axis_size("row")
        cols = lax.axis_size("col")
        self.sizes = {"y": rows // 2, "core": 2, "z": cols // 2, "x": 2}
        self.count = rows * cols

    def coords(self, device):
        cols = self.sizes["z"] * 2
        if isinstance(device, int):
            row, col = device // cols, device % cols
            return {"y": row // 2, "core": row % 2, "z": col // 2, "x": col % 2}
        row, col = lax.div(device, cols), lax.rem(device, cols)
        return {"y": lax.div(row, 2), "core": lax.rem(row, 2), "z": lax.div(col, 2), "x": lax.rem(col, 2)}

    def device(self, at):
        row = at["y"] * 2 + at["core"]
        col = at["z"] * 2 + at["x"]
        return row * self.sizes["z"] * 2 + col

    def slot(self, device, home):
        at, base = self.coords(device), self.coords(home)
        away = {a: lax.rem(at[a] - base[a] + n, n) for a, n in self.sizes.items()}
        away["z"] = at["z"]
        plane = (away["core"] * self.sizes["y"] + away["y"]) * 2 + away["x"]
        return plane * self.sizes["z"] + away["z"]

    def send(self, block, axis, distance):
        route = []
        for source in range(self.count):
            at = self.coords(source)
            for name in axis.split():
                at[name] = (at[name] + distance) % self.sizes[name]
            route.append((source, self.device(at)))
        return lax.ppermute(block, BOTH, route)

    def along_z(self, blocks):
        depth = self.sizes["z"]
        groups = [[2 * z + x for z in range(depth)] for x in range(2)]
        return lax.all_to_all(blocks, "col", 0, 0, axis_index_groups=groups, tiled=True)

    def fetch(self, block, axis, distance):
        return self.send(block, axis, -distance)


def gather_field(grid, low):
    depth, wide = grid.sizes["z"], grid.sizes["y"]
    base = grid.along_z(jnp.concatenate([low] * depth))
    if wide == 2:
        corner = grid.fetch(low, "x y", 1)
        base, corner = lax.optimization_barrier((base, corner))
        over_x = grid.fetch(base, "x", 1)
        over_y = grid.fetch(base, "y", 1)
        pieces = [base, over_x, over_y, grid.along_z(jnp.concatenate([corner] * depth))]
    else:
        lines = [base] + [grid.fetch(base, "y", r) for r in range(1, wide)]
        pieces = []
        for line in lines:
            pieces += [line, grid.fetch(line, "x", 1)]
    return pieces + [grid.fetch(piece, "core", 1) for piece in pieces]


def scatter_sum(grid, own, other):
    depth, wide = grid.sizes["z"], grid.sizes["y"]
    arrived = grid.send(other, "core", 1)
    total = own.astype(jnp.float32) + arrived.astype(jnp.float32)
    total = total.reshape((wide, 2, depth, 2) + total.shape[1:])

    def narrow(v):
        return v.astype(jnp.bfloat16)

    def widen(v):
        return v.astype(jnp.float32)

    if wide == 2:
        corner = jnp.sum(widen(grid.along_z(narrow(total[1, 1]))), axis=0)
        base = total[0, 0] + widen(grid.send(narrow(total[0, 1]), "x", 1))
        base = base + widen(grid.send(narrow(total[1, 0]), "y", 1))
        return jnp.sum(widen(grid.along_z(narrow(base))), axis=0) + widen(grid.send(narrow(corner), "x y", 1))
    total = total[:, 0] + widen(grid.send(narrow(total[:, 1]), "x", 1))
    base = total[0]
    for r in range(1, wide):
        base = base + widen(grid.send(narrow(total[r]), "y", r))
    return jnp.sum(widen(grid.along_z(narrow(base))), axis=0)


def pair_slots(key, groups, valid):
    tiles = key.shape[0]
    slots = -(-(tiles + groups) // (2 * UNROLL)) * 2 * UNROLL
    member = (key[:, None] == jnp.arange(groups, dtype=jnp.int32)[None, :]) & valid[:, None]
    counts = jnp.sum(member.astype(jnp.int32), axis=0)
    padded = (counts + 1) // 2 * 2
    ids = jnp.arange(groups, dtype=jnp.int32)
    start = jnp.sum(jnp.where(ids[None, :] < ids[:, None], padded[None, :], 0), axis=1)
    t = jnp.arange(tiles, dtype=jnp.int32)
    earlier = (key[None, :] == key[:, None]) & valid[None, :] & (t[None, :] < t[:, None])
    within = jnp.sum(earlier.astype(jnp.int32), axis=1)
    pos = jnp.sum(jnp.where(member, start[None, :], 0), axis=1) + within
    hit = (pos[None, :] == jnp.arange(slots, dtype=jnp.int32)[:, None]) & valid[None, :]
    pairs = (jnp.sum(padded) // 2).reshape(1)
    return hit, pairs


def pick(hit, values, empty=0):
    found = jnp.sum(jnp.where(hit, (values - empty)[None, :], 0), axis=1)
    return found + empty


def plan(grid, place, tile_pose, tile_point, tile_valid):
    valid = tile_valid > 0
    t = jnp.arange(tile_pose.shape[0], dtype=jnp.int32)
    holder = grid.slot(tile_pose // 2, place)
    pose = 2 * holder + tile_pose % 2
    before = jnp.maximum(place - 1, 0)
    after = jnp.minimum(place + 1, grid.count - 1)
    sides = jnp.stack([grid.slot(before, place), grid.slot(after, place)])
    hit, pairs = pair_slots(tile_point, PT_DEV, valid)
    fwd = [
        pairs,
        2 * sides,
        pick(hit, t),
        pick(hit, pose),
        pick(hit, jnp.ones_like(t)),
        pick(hit, tile_point)[::2],
    ]
    hit, pairs = pair_slots(holder, grid.count, valid)
    bwd = [
        pairs,
        pick(hit, t),
        pick(hit, tile_point, PT_DEV),
        pick(hit, pose)[::2],
    ]
    return jnp.concatenate(fwd), jnp.concatenate(bwd)


NT = (((1,), (1,)), ((), ()))
NN = (((1,), (0,)), ((), ()))


def gram_kernel(fwd_slots, bwd_slots, fwd, bwd, tiles, *refs):
    pieces, (own, other, sides, field, acc, low, total) = refs[:-7], refs[-7:]
    start = 0
    for piece in pieces:
        field[start : start + piece.shape[0]] = piece[...]
        start += piece.shape[0]
    for side in range(2):
        sides[side] = field[pl.ds(fwd[1 + side], 2)]
    acc[...] = jnp.zeros_like(acc)
    total[...] = jnp.zeros_like(total)

    def forward(i, _):
        for u in range(UNROLL):
            j = i * UNROLL + u
            tile = [fwd[3 + 2 * j + h] for h in range(2)]
            pose = [fwd[3 + fwd_slots + 2 * j + h] for h in range(2)]
            real = [fwd[3 + 2 * fwd_slots + 2 * j + h] for h in range(2)]
            point = fwd[3 + 3 * fwd_slots + j]
            left = field[pose[0]] * real[0].astype(jnp.float32).astype(jnp.bfloat16)
            right = field[pose[1]] * real[1].astype(jnp.float32).astype(jnp.bfloat16)
            acc[point] += lax.dot_general(
                jnp.concatenate([left, right], axis=1),
                jnp.concatenate([tiles[tile[0]], tiles[tile[1]]], axis=1),
                NT,
                preferred_element_type=jnp.float32,
            )
        return 0

    lax.fori_loop(0, (fwd[0] + UNROLL - 1) // UNROLL, forward, 0)
    low[: acc.shape[0]] = acc[...].astype(jnp.bfloat16)
    low[acc.shape[0]] = jnp.zeros(low.shape[1:], jnp.bfloat16)

    def backward(i, _):
        for u in range(UNROLL):
            j = i * UNROLL + u
            tile = [bwd[1 + 2 * j + h] for h in range(2)]
            point = [bwd[1 + bwd_slots + 2 * j + h] for h in range(2)]
            pose = bwd[1 + 2 * bwd_slots + j]
            total[pose] += lax.dot_general(
                jnp.concatenate([low[point[0]], low[point[1]]], axis=1),
                jnp.concatenate([tiles[tile[0]], tiles[tile[1]]], axis=0),
                NN,
                preferred_element_type=jnp.float32,
            )
        return 0

    lax.fori_loop(0, (bwd[0] + UNROLL - 1) // UNROLL, backward, 0)
    half = own.shape[0]
    other[...] = total[half:].astype(other.dtype)
    own[...] = total[:half].astype(own.dtype)


def gram_product(fwd, bwd, tiles, pieces):
    blocks = sum(piece.shape[0] for piece in pieces)
    rhs, params = pieces[0].shape[1:]
    points = tiles.shape[1]
    fwd_slots = (fwd.shape[0] - 3) * 2 // 7
    bwd_slots = (bwd.shape[0] - 1) * 2 // 5
    smem = pl.BlockSpec(memory_space=pltpu.SMEM)
    vmem = pl.BlockSpec(memory_space=pltpu.VMEM)
    return pl.pallas_call(
        functools.partial(gram_kernel, fwd_slots, bwd_slots),
        out_shape=[
            jax.ShapeDtypeStruct((blocks // 2, rhs, params), jnp.bfloat16),
            jax.ShapeDtypeStruct((blocks // 2, rhs, params), jnp.bfloat16),
            jax.ShapeDtypeStruct((2, 2, rhs, params), jnp.bfloat16),
        ],
        in_specs=[smem, smem, vmem] + [vmem] * len(pieces),
        out_specs=[vmem] * 3,
        scratch_shapes=[
            pltpu.VMEM((blocks, rhs, params), jnp.bfloat16),
            pltpu.VMEM((PT_DEV, rhs, points), jnp.float32),
            pltpu.VMEM((PT_DEV + 1, rhs, points), jnp.bfloat16),
            pltpu.VMEM((blocks, rhs, params), jnp.float32),
        ],
        compiler_params=pltpu.CompilerParams(vmem_limit_bytes=(7 * blocks // 32 + 8) * 1024 * 1024),
        cost_estimate=pl.CostEstimate(
            flops=4 * tiles.shape[0] * rhs * params * points,
            bytes_accessed=tiles.size * 2 + blocks * rhs * params * 4,
            transcendentals=0,
        ),
    )(fwd, bwd, tiles, *pieces)


def shifted(block, distance):
    devices = range(lax.axis_size(BOTH))
    route = [(i - distance, i) for i in devices if i - distance in devices]
    return lax.ppermute(block, BOTH, route)


def on_device(jac_tiles, tile_pose, tile_point, tile_valid, prior_weight, right_side):
    grid = Grid()
    place = lax.axis_index(BOTH)
    is_first = place == 0
    is_last = place == grid.count - 1
    fwd, bwd = plan(grid, place, tile_pose, tile_point, tile_valid)
    left_weight = shifted(prior_weight, 1)
    right_weight = shifted(prior_weight, -1)
    zero = jnp.zeros_like(prior_weight[0])
    w_left = jnp.stack([jnp.where(is_first, zero, left_weight[0]), jnp.where(is_first, zero, prior_weight[1])])
    w_right = jnp.stack([prior_weight[0], jnp.where(is_last, prior_weight[0], right_weight[1])])
    w_left = w_left[:, None, :]
    w_right = w_right[:, None, :]

    theta = (highest + lowest) / 2.0
    delta = (highest - lowest) / 2.0
    sigma = theta / delta
    ratio = 1.0 / sigma
    right_side = jnp.swapaxes(right_side, 1, 2)
    step = right_side / theta
    solution = jnp.zeros(right_side.shape, jnp.float32)
    residual = right_side
    for turn in range(ITERS):
        if turn > 0:
            new_ratio = 1.0 / (2.0 * sigma - ratio)
            step = new_ratio * ratio * step + 2.0 * new_ratio / delta * residual
            ratio = new_ratio
        solution = solution + step
        low = step.astype(jnp.bfloat16)
        if turn == 0:
            low, w_left, w_right = lax.optimization_barrier((low, w_left, w_right))
        pieces = gather_field(grid, low)
        own, other, sides = gram_product(fwd, bwd, jac_tiles, pieces)
        gram = scatter_sum(grid, own, other)
        left, right = sides.astype(jnp.float32)
        right = jnp.where(is_last, step[::-1], right)
        prior = w_left * (step - left) + w_right * (step - right)
        residual = residual - (gram + prior + damping * step)
    return jnp.swapaxes(solution, 1, 2), jnp.swapaxes(residual, 1, 2)


def solution(mesh):
    return jax.shard_map(
        on_device,
        mesh=mesh,
        in_specs=(
            P(BOTH, None, None),
            P(BOTH),
            P(BOTH),
            P(BOTH),
            P(BOTH, None),
            P(BOTH, None, None),
        ),
        out_specs=(P(BOTH, None, None), P(BOTH, None, None)),
        check_vma=False,
    )
```

```python
import math

import jax
import jax.numpy as jnp
from jax import lax
from jax.experimental import pallas as pl
from jax.experimental.pallas import tpu as pltpu
from jax.sharding import PartitionSpec as P

PT_DEV = 16
ITERS = 3
UNROLL = 8

damping = 0.5
lowest = 0.5
highest = 8.0
BOTH = ("row", "col")


class Grid:
    def __init__(self):
        rows = lax.axis_size("row")
        cols = lax.axis_size("col")
        self.sizes = {"y": rows // 2, "core": 2, "z": cols // 2, "x": 2}
        self.count = rows * cols

    def coords(self, device):
        cols = self.sizes["z"] * 2
        if isinstance(device, int):
            row, col = device // cols, device % cols
            return {"y": row // 2, "core": row % 2, "z": col // 2, "x": col % 2}
        row, col = lax.div(device, cols), lax.rem(device, cols)
        return {"y": lax.div(row, 2), "core": lax.rem(row, 2), "z": lax.div(col, 2), "x": lax.rem(col, 2)}

    def device(self, at):
        row = at["y"] * 2 + at["core"]
        col = at["z"] * 2 + at["x"]
        return row * self.sizes["z"] * 2 + col

    def slot(self, device, home):
        at, base = self.coords(device), self.coords(home)
        away = {a: lax.rem(at[a] - base[a] + n, n) for a, n in self.sizes.items()}
        return away["core"], (away["y"] * 2 + away["x"]) * self.sizes["z"] + away["z"]

    def send(self, block, axis, distance):
        route = []
        for source in range(self.count):
            at = self.coords(source)
            for name in axis.split():
                at[name] = (at[name] + distance) % self.sizes[name]
            route.append((source, self.device(at)))
        return lax.ppermute(block, BOTH, route)

    def fetch(self, block, axis, distance):
        return self.send(block, axis, -distance)


def gather_field(grid, low, *early):
    depth, wide = grid.sizes["z"], grid.sizes["y"]
    column = [low] + [grid.fetch(low, "z", r) for r in range(1, depth)]
    if wide == 2:
        corner = grid.fetch(low, "x y", 1)
        base, corner, *early = lax.optimization_barrier((jnp.concatenate(column), corner, *early))
        far = [corner] + [grid.fetch(corner, "z", r) for r in range(1, depth)]
        over_x = grid.fetch(base, "x", 1)
        over_y = grid.fetch(base, "y", 1)
        base, over_x = lax.optimization_barrier((base, over_x))
        pieces = [base, over_x, over_y, jnp.concatenate(far)]
    else:
        base = jnp.concatenate(column)
        lines = [base] + [grid.fetch(base, "y", r) for r in range(1, wide)]
        pieces = []
        for line in lines:
            pieces += [line, grid.fetch(line, "x", 1)]
    return pieces, [grid.fetch(piece, "core", 1) for piece in pieces], early


def scatter_sum(grid, own, arrived):
    depth, wide = grid.sizes["z"], grid.sizes["y"]
    total = own + arrived.astype(jnp.float32)
    total = total.reshape((wide, 2, depth, 2) + total.shape[1:])

    def narrow(v):
        return v.astype(jnp.bfloat16)

    def widen(v):
        return v.astype(jnp.float32)

    if wide == 2:
        corner = total[1, 1, 0]
        for r in range(1, depth):
            corner = corner + widen(grid.send(narrow(total[1, 1, r]), "z", r))
        base = total[0, 0] + widen(grid.send(narrow(total[0, 1]), "x", 1))
        base = base + widen(grid.send(narrow(total[1, 0]), "y", 1))
        gram = base[0] + widen(grid.send(narrow(corner), "x y", 1))
    else:
        total = total[:, 0] + widen(grid.send(narrow(total[:, 1]), "x", 1))
        base = total[0]
        for r in range(1, wide):
            base = base + widen(grid.send(narrow(total[r]), "y", r))
        gram = base[0]
    for r in range(1, depth):
        gram = gram + widen(grid.send(narrow(base[r]), "z", r))
    return gram


def plan_kernel(core, pose, point, valid, out):
    tiles, slots = core.shape[1], out.shape[1]
    row_id = lax.broadcasted_iota(jnp.int32, (tiles, tiles), 0)
    col_id = lax.broadcasted_iota(jnp.int32, (tiles, tiles), 1)
    lane = lax.broadcasted_iota(jnp.int32, (tiles, slots), 1)

    def column(row):
        return jnp.sum(jnp.where(row_id == col_id, row, 0.0), axis=1, keepdims=True)

    def half_up(v, unit):
        whole = v.astype(jnp.int32) + (unit - 1)
        return (whole & ~(unit - 1)).astype(jnp.float32)

    def arrange(key, phase):
        key_col, phase_col = column(key), column(phase)
        same = jnp.where((key_col == key) & (real_col > 0.0) & (real > 0.0), 1.0, 0.0)
        count = jnp.sum(same, axis=0, keepdims=True)
        rank = jnp.sum(jnp.where(row_id < col_id, same, 0.0), axis=0, keepdims=True)
        rank_col = jnp.sum(jnp.where(col_id < row_id, same, 0.0), axis=1, keepdims=True)
        room = jnp.where((rank == 0.0) & (real > 0.0), half_up(count, 2), 0.0)
        start = jnp.sum(jnp.where(key < key_col, room, 0.0), axis=1, keepdims=True)
        first = jnp.sum(jnp.where(phase == 0.0, room, 0.0), axis=1, keepdims=True)
        second = jnp.sum(jnp.where(phase == 0.0, 0.0, room), axis=1, keepdims=True)
        padded = half_up(first, 2 * UNROLL)
        place = start + rank_col + jnp.where(phase_col == 0.0, 0.0, padded - first)
        place = jnp.where(real_col > 0.0, place, -1.0)
        hit = jnp.where(place.astype(jnp.int32) == lane, 1.0, 0.0)
        return hit, padded, padded + half_up(second, 2 * UNROLL)

    def pick(hit, values):
        return jnp.sum(hit * values, axis=0, keepdims=True)

    real = valid[...].astype(jnp.float32)
    real_col = column(real)
    core_row = core[...].astype(jnp.float32)
    pose_row = pose[...].astype(jnp.float32)
    point_row = point[...].astype(jnp.float32)
    pose_col, point_col = column(pose_row), column(point_row)
    tile_col = column(col_id[:1].astype(jnp.float32))
    hit, first, last = arrange(core_row * PT_DEV + point_row, core_row)
    rows = [
        pick(hit, tile_col),
        pick(hit, pose_col),
        pick(hit, jnp.ones_like(tile_col)),
        pick(hit, point_col),
    ]
    ends = [first, last]
    other = 1.0 - core_row
    hit, first, last = arrange(other * 65536.0 + pose_row, other)
    rows += [
        pick(hit, tile_col),
        pick(hit, point_col - PT_DEV) + PT_DEV,
        pick(hit, pose_col),
    ]
    ends += [first, last]
    spot = lane[:1]
    tail = jnp.zeros_like(rows[0])
    for k, end in enumerate(ends):
        tail = jnp.where(spot == k, end * (0.5 / UNROLL), tail)
    for k, row in enumerate(rows + [tail]):
        out[k : k + 1] = row.astype(jnp.int32)


def make_plan(grid, place, tile_pose, tile_point, tile_valid):
    tiles = tile_pose.shape[0]
    core, chip = grid.slot(lax.div(tile_pose, 2), place)
    pose = 2 * chip + lax.rem(tile_pose, 2)
    slots = tiles + max(2 * PT_DEV, min(tiles, grid.count)) + 4 * UNROLL
    slots = -(-slots // 128) * 128
    rows = [v.reshape(1, tiles) for v in (core, pose, tile_point, tile_valid)]
    return pl.pallas_call(
        plan_kernel,
        out_shape=jax.ShapeDtypeStruct((8, slots), jnp.int32),
        in_specs=[pl.BlockSpec(memory_space=pltpu.VMEM)] * 4,
        out_specs=pl.BlockSpec(memory_space=pltpu.VMEM),
    )(*rows)


NT = (((1,), (1,)), ((), ()))
NN = (((1,), (0,)), ((), ()))
F_TILE, F_POSE, F_REAL, F_POINT, B_TILE, B_POINT, B_POSE, ENDS = range(8)


def forward(plan, tiles, field, acc, begin, end):
    def body(i, _):
        for u in range(UNROLL):
            j = 2 * (i * UNROLL + u)
            block = [
                field[plan[F_POSE, j + h]]
                * plan[F_REAL, j + h].astype(jnp.float32).astype(jnp.bfloat16)
                for h in range(2)
            ]
            tile = [tiles[plan[F_TILE, j + h]] for h in range(2)]
            acc[plan[F_POINT, j]] += lax.dot_general(
                jnp.concatenate(block, axis=1),
                jnp.concatenate(tile, axis=1),
                NT,
                preferred_element_type=jnp.float32,
            )
        return 0

    lax.fori_loop(begin, end, body, 0)


def backward(plan, tiles, low, total, begin, end):
    def body(i, _):
        for u in range(UNROLL):
            j = 2 * (i * UNROLL + u)
            block = [low[plan[B_POINT, j + h]] for h in range(2)]
            tile = [tiles[plan[B_TILE, j + h]] for h in range(2)]
            total[plan[B_POSE, j]] += lax.dot_general(
                jnp.concatenate(block, axis=1),
                jnp.concatenate(tile, axis=0),
                NN,
                preferred_element_type=jnp.float32,
            )
        return 0

    lax.fori_loop(begin, end, body, 0)


def assemble(pieces, field):
    start = 0
    for piece in pieces:
        field[start : start + piece.shape[0]] = piece[...]
        start += piece.shape[0]


def own_forward(plan, near, tiles, *refs):
    pieces, (acc, sides, field) = refs[:-3], refs[-3:]
    assemble(pieces, field)
    for side in range(2):
        sides[side] = field[pl.ds(near[2 * side + 1], 2)]
    acc[...] = jnp.zeros_like(acc)
    forward(plan, tiles, field, acc, 0, plan[ENDS, 0])


def other_both(plan, near, tiles, part, own_sides, *refs):
    pieces, (other, low, sides, field, acc, total) = refs[:-6], refs[-6:]
    assemble(pieces, field)
    for side in range(2):

        @pl.when(near[2 * side] == 0)
        def _():
            sides[side] = own_sides[side]

        @pl.when(near[2 * side] != 0)
        def _():
            sides[side] = field[pl.ds(near[2 * side + 1], 2)]

    acc[...] = part[...]
    total[...] = jnp.zeros_like(total)
    forward(plan, tiles, field, acc, plan[ENDS, 0], plan[ENDS, 1])
    points = acc.shape[0]
    low[:points] = acc[...].astype(jnp.bfloat16)
    low[points] = jnp.zeros(low.shape[1:], jnp.bfloat16)
    backward(plan, tiles, low, total, 0, plan[ENDS, 2])
    other[...] = total[...].astype(other.dtype)


def own_backward(plan, tiles, low, own):
    own[...] = jnp.zeros_like(own)
    backward(plan, tiles, low, own, plan[ENDS, 2], plan[ENDS, 3])


def call(kernel, outs, scratch, args, kinds, tiles, share):
    place = {
        "s": pl.BlockSpec(memory_space=pltpu.SMEM),
        "v": pl.BlockSpec(memory_space=pltpu.VMEM),
    }
    size = sum(math.prod(v.shape) * v.dtype.itemsize for v in [*outs, *args])
    size += sum(math.prod(v.shape) * jnp.dtype(v.dtype).itemsize for v in scratch)
    return pl.pallas_call(
        kernel,
        out_shape=outs,
        in_specs=[place[kind] for kind in kinds],
        out_specs=[place["v"]] * len(outs),
        scratch_shapes=scratch,
        compiler_params=pltpu.CompilerParams(vmem_limit_bytes=size + 2 * 1024 * 1024),
        cost_estimate=pl.CostEstimate(
            flops=int(share * 4 * tiles.size * 128),
            bytes_accessed=tiles.size * 2,
            transcendentals=0,
        ),
    )(*args)


def gram_product(grid, plan, near, tiles, own_pieces, other_pieces):
    rhs, params = own_pieces[0].shape[1:]
    points = tiles.shape[1]
    blocks = grid.count

    def array(lead, kind):
        return jax.ShapeDtypeStruct((*lead, rhs, params), kind)

    field = pltpu.VMEM((blocks, rhs, params), jnp.bfloat16)
    acc = jax.ShapeDtypeStruct((PT_DEV, rhs, points), jnp.float32)
    part, own_sides = call(
        own_forward,
        [acc, array((2, 2), jnp.bfloat16)],
        [field],
        [plan, near, tiles, *own_pieces],
        "ssv" + "v" * len(own_pieces),
        tiles,
        0.25,
    )
    other, low, sides = call(
        other_both,
        [
            array((blocks,), jnp.bfloat16),
            jax.ShapeDtypeStruct((PT_DEV + 1, rhs, points), jnp.bfloat16),
            array((2, 2), jnp.bfloat16),
        ],
        [
            field,
            pltpu.VMEM((PT_DEV, rhs, points), jnp.float32),
            pltpu.VMEM((blocks, rhs, params), jnp.float32),
        ],
        [plan, near, tiles, part, own_sides, *other_pieces],
        "ssvvv" + "v" * len(other_pieces),
        tiles,
        0.5,
    )
    arrived = grid.send(other, "core", 1)
    (own,) = call(
        own_backward,
        [array((blocks,), jnp.float32)],
        [],
        [plan, tiles, low],
        "svv",
        tiles,
        0.25,
    )
    return own, arrived, sides


def shifted(block, distance):
    devices = range(lax.axis_size(BOTH))
    route = [(i - distance, i) for i in devices if i - distance in devices]
    return lax.ppermute(block, BOTH, route)


def on_device(jac_tiles, tile_pose, tile_point, tile_valid, prior_weight, right_side):
    grid = Grid()
    place = lax.axis_index(BOTH)
    is_first = place == 0
    is_last = place == grid.count - 1
    plan = make_plan(grid, place, tile_pose, tile_point, tile_valid)
    before = grid.slot(jnp.maximum(place - 1, 0), place)
    after = grid.slot(jnp.minimum(place + 1, grid.count - 1), place)
    near = jnp.stack([before[0], 2 * before[1], after[0], 2 * after[1]])
    left_weight = shifted(prior_weight, 1)
    right_weight = shifted(prior_weight, -1)
    zero = jnp.zeros_like(prior_weight[0])
    w_left = jnp.stack([jnp.where(is_first, zero, left_weight[0]), jnp.where(is_first, zero, prior_weight[1])])
    w_right = jnp.stack([prior_weight[0], jnp.where(is_last, prior_weight[0], right_weight[1])])
    w_left = w_left[:, None, :]
    w_right = w_right[:, None, :]

    theta = (highest + lowest) / 2.0
    delta = (highest - lowest) / 2.0
    sigma = theta / delta
    ratio = 1.0 / sigma
    right_side = jnp.swapaxes(right_side, 1, 2)
    step = right_side / theta
    solution = jnp.zeros(right_side.shape, jnp.float32)
    residual = right_side
    for turn in range(ITERS):
        if turn > 0:
            new_ratio = 1.0 / (2.0 * sigma - ratio)
            step = new_ratio * ratio * step + 2.0 * new_ratio / delta * residual
            ratio = new_ratio
        solution = solution + step
        low = step.astype(jnp.bfloat16)
        if turn == 0:
            low, w_left, w_right = lax.optimization_barrier((low, w_left, w_right))
        pieces, swapped, (plan, near) = gather_field(grid, low, plan, near)
        own, arrived, sides = gram_product(grid, plan, near, jac_tiles, pieces, swapped)
        gram = scatter_sum(grid, own, arrived)
        left, right = sides.astype(jnp.float32)
        right = jnp.where(is_last, step[::-1], right)
        prior = w_left * (step - left) + w_right * (step - right)
        residual = residual - (gram + prior + damping * step)
    return jnp.swapaxes(solution, 1, 2), jnp.swapaxes(residual, 1, 2)


def solution(mesh):
    return jax.shard_map(
        on_device,
        mesh=mesh,
        in_specs=(
            P(BOTH, None, None),
            P(BOTH),
            P(BOTH),
            P(BOTH),
            P(BOTH, None),
            P(BOTH, None, None),
        ),
        out_specs=(P(BOTH, None, None), P(BOTH, None, None)),
        check_vma=False,
    )
```

```python
import math

import jax
import jax.numpy as jnp
from jax import lax
from jax.experimental import pallas as pl
from jax.experimental.pallas import tpu as pltpu
from jax.sharding import PartitionSpec as P

PT_DEV = 16
ITERS = 3
UNROLL = 8

damping = 0.5
lowest = 0.5
highest = 8.0
BOTH = ("row", "col")


class Grid:
    def __init__(self):
        rows = lax.axis_size("row")
        cols = lax.axis_size("col")
        self.sizes = {"y": rows // 2, "core": 2, "z": cols // 2, "x": 2}
        self.count = rows * cols

    def coords(self, device):
        cols = self.sizes["z"] * 2
        if isinstance(device, int):
            row, col = device // cols, device % cols
            return {"y": row // 2, "core": row % 2, "z": col // 2, "x": col % 2}
        row, col = lax.div(device, cols), lax.rem(device, cols)
        return {"y": lax.div(row, 2), "core": lax.rem(row, 2), "z": lax.div(col, 2), "x": lax.rem(col, 2)}

    def device(self, at):
        row = at["y"] * 2 + at["core"]
        col = at["z"] * 2 + at["x"]
        return row * self.sizes["z"] * 2 + col

    def slot(self, device, home):
        at, base = self.coords(device), self.coords(home)
        sign = 1 - 2 * at["core"]
        away = {a: lax.rem((at[a] - base[a]) * sign + n, n) for a, n in self.sizes.items()}
        x, y = away["x"], away["y"]
        if self.sizes["y"] == 2:
            swap = at["core"] == 1
            x, y = jnp.where(swap, y, x), jnp.where(swap, x, y)
        return away["core"], (y * 2 + x) * self.sizes["z"] + away["z"]

    def send(self, block, axes, distance):
        route = []
        for source in range(self.count):
            at = self.coords(source)
            sign = 1 - 2 * at["core"]
            names = axes if isinstance(axes, str) else axes[at["core"]]
            for name in names.split():
                at[name] = (at[name] + sign * distance) % self.sizes[name]
            route.append((source, self.device(at)))
        return lax.ppermute(block, BOTH, route)

    def fetch(self, block, axes, distance):
        return self.send(block, axes, -distance)


PLANE = (("x", "y"), ("y", "x"), "x y")


def gather_field(grid, low, *early):
    depth, wide = grid.sizes["z"], grid.sizes["y"]
    column = [low] + [grid.fetch(low, "z", r) for r in range(1, depth)]
    base, *early = lax.optimization_barrier((jnp.concatenate(column), *early))
    if wide == 2:
        pieces = [base] + [grid.fetch(base, axes, 1) for axes in PLANE]
    else:
        lines = [base] + [grid.fetch(base, "y", r) for r in range(1, wide)]
        pieces = []
        for line in lines:
            pieces += [line, grid.fetch(line, "x", 1)]
    return pieces, [grid.fetch(piece, "core", 1) for piece in pieces], early


def scatter_sum(grid, own, arrived):
    depth, wide = grid.sizes["z"], grid.sizes["y"]
    total = own + arrived.astype(jnp.float32)
    total = total.reshape((wide, 2, depth, 2) + total.shape[1:])

    def narrow(v):
        return v.astype(jnp.bfloat16)

    def widen(v):
        return v.astype(jnp.float32)

    if wide == 2:
        base = total[0, 0]
        for k, axes in enumerate(PLANE):
            base = base + widen(grid.send(narrow(total[(k + 1) // 2, (k + 1) % 2]), axes, 1))
    else:
        total = total[:, 0] + widen(grid.send(narrow(total[:, 1]), "x", 1))
        base = total[0]
        for r in range(1, wide):
            base = base + widen(grid.send(narrow(total[r]), "y", r))
    gram = base[0]
    for r in range(1, depth):
        gram = gram + widen(grid.send(narrow(base[r]), "z", r))
    return gram


def plan_kernel(core, pose, point, valid, jac, out):
    tiles, slots = core.shape[1], out.shape[1]
    row_id = lax.broadcasted_iota(jnp.int32, (tiles, tiles), 0)
    col_id = lax.broadcasted_iota(jnp.int32, (tiles, tiles), 1)
    lane = lax.broadcasted_iota(jnp.int32, (tiles, slots), 1)

    def column(row):
        return jnp.sum(jnp.where(row_id == col_id, row, 0.0), axis=1, keepdims=True)

    def half_up(v, unit):
        whole = v.astype(jnp.int32) + (unit - 1)
        return (whole & ~(unit - 1)).astype(jnp.float32)

    def arrange(key, phase):
        key_col, phase_col = column(key), column(phase)
        same = jnp.where((key_col == key) & (real_col > 0.0) & (real > 0.0), 1.0, 0.0)
        count = jnp.sum(same, axis=0, keepdims=True)
        rank = jnp.sum(jnp.where(row_id < col_id, same, 0.0), axis=0, keepdims=True)
        rank_col = jnp.sum(jnp.where(col_id < row_id, same, 0.0), axis=1, keepdims=True)
        room = jnp.where((rank == 0.0) & (real > 0.0), half_up(count, 2), 0.0)
        start = jnp.sum(jnp.where(key < key_col, room, 0.0), axis=1, keepdims=True)
        first = jnp.sum(jnp.where(phase == 0.0, room, 0.0), axis=1, keepdims=True)
        second = jnp.sum(jnp.where(phase == 0.0, 0.0, room), axis=1, keepdims=True)
        padded = half_up(first, 2 * UNROLL)
        place = start + rank_col + jnp.where(phase_col == 0.0, 0.0, padded - first)
        place = jnp.where(real_col > 0.0, place, -1.0)
        hit = jnp.where(place.astype(jnp.int32) == lane, 1.0, 0.0)
        return hit, padded, padded + half_up(second, 2 * UNROLL)

    def pick(hit, values):
        return jnp.sum(hit * values, axis=0, keepdims=True)

    real = valid[...].astype(jnp.float32)
    real_col = column(real)
    core_row = core[...].astype(jnp.float32)
    pose_row = pose[...].astype(jnp.float32)
    point_row = point[...].astype(jnp.float32)
    pose_col, point_col = column(pose_row), column(point_row)
    tile_col = column(col_id[:1].astype(jnp.float32))
    hit, first, last = arrange(core_row * PT_DEV + point_row, core_row)
    rows = [
        pick(hit, tile_col),
        pick(hit, pose_col),
        pick(hit, jnp.ones_like(tile_col)),
        pick(hit, point_col),
    ]
    ends = [first, last]
    other = 1.0 - core_row
    hit, first, last = arrange(other * 65536.0 + pose_row, other)
    rows += [
        pick(hit, tile_col),
        pick(hit, point_col - PT_DEV) + PT_DEV,
        pick(hit, pose_col),
    ]
    ends += [first, last]
    spot = lane[:1]
    tail = jnp.zeros_like(rows[0])
    for k, end in enumerate(ends):
        tail = jnp.where(spot == k, end * (0.5 / UNROLL), tail)
    for k, row in enumerate(rows + [tail]):
        out[k : k + 1] = row.astype(jnp.int32)


def make_plan(grid, place, tile_pose, tile_point, tile_valid, jac):
    tiles = tile_pose.shape[0]
    core, chip = grid.slot(lax.div(tile_pose, 2), place)
    pose = 2 * chip + lax.rem(tile_pose, 2)
    slots = tiles + max(2 * PT_DEV, min(tiles, grid.count)) + 4 * UNROLL
    slots = -(-slots // 128) * 128
    rows = [v.reshape(1, tiles) for v in (core, pose, tile_point, tile_valid)]
    return pl.pallas_call(
        plan_kernel,
        out_shape=jax.ShapeDtypeStruct((8, slots), jnp.int32),
        in_specs=[pl.BlockSpec(memory_space=pltpu.VMEM)] * 5,
        out_specs=pl.BlockSpec(memory_space=pltpu.VMEM),
    )(*rows, jac)


NT = (((1,), (1,)), ((), ()))
NN = (((1,), (0,)), ((), ()))
F_TILE, F_POSE, F_REAL, F_POINT, B_TILE, B_POINT, B_POSE, ENDS = range(8)


def forward(plan, tiles, field, acc, begin, end):
    def body(i, _):
        for u in range(UNROLL):
            j = 2 * (i * UNROLL + u)
            block = [
                field[plan[F_POSE, j + h]]
                * plan[F_REAL, j + h].astype(jnp.float32).astype(jnp.bfloat16)
                for h in range(2)
            ]
            tile = [tiles[plan[F_TILE, j + h]] for h in range(2)]
            acc[plan[F_POINT, j]] += lax.dot_general(
                jnp.concatenate(block, axis=1),
                jnp.concatenate(tile, axis=1),
                NT,
                preferred_element_type=jnp.float32,
            )
        return 0

    lax.fori_loop(begin, end, body, 0)


def backward(plan, tiles, low, total, begin, end):
    def body(i, _):
        for u in range(UNROLL):
            j = 2 * (i * UNROLL + u)
            block = [low[plan[B_POINT, j + h]] for h in range(2)]
            tile = [tiles[plan[B_TILE, j + h]] for h in range(2)]
            total[plan[B_POSE, j]] += lax.dot_general(
                jnp.concatenate(block, axis=1),
                jnp.concatenate(tile, axis=0),
                NN,
                preferred_element_type=jnp.float32,
            )
        return 0

    lax.fori_loop(begin, end, body, 0)


def assemble(pieces, field):
    start = 0
    for piece in pieces:
        field[start : start + piece.shape[0]] = piece[...]
        start += piece.shape[0]


def own_forward(plan, near, tiles, *refs):
    pieces, (acc, sides, field) = refs[:-3], refs[-3:]
    assemble(pieces, field)
    for side in range(2):
        sides[side] = field[pl.ds(near[2 * side + 1], 2)]
    acc[...] = jnp.zeros_like(acc)
    forward(plan, tiles, field, acc, 0, plan[ENDS, 0])


def other_both(plan, near, tiles, part, own_sides, *refs):
    pieces, (other, low, sides, field, acc, total) = refs[:-6], refs[-6:]
    assemble(pieces, field)
    for side in range(2):

        @pl.when(near[2 * side] == 0)
        def _():
            sides[side] = own_sides[side]

        @pl.when(near[2 * side] != 0)
        def _():
            sides[side] = field[pl.ds(near[2 * side + 1], 2)]

    acc[...] = part[...]
    total[...] = jnp.zeros_like(total)
    forward(plan, tiles, field, acc, plan[ENDS, 0], plan[ENDS, 1])
    points = acc.shape[0]
    low[:points] = acc[...].astype(jnp.bfloat16)
    low[points] = jnp.zeros(low.shape[1:], jnp.bfloat16)
    backward(plan, tiles, low, total, 0, plan[ENDS, 2])
    other[...] = total[...].astype(other.dtype)


def own_backward(plan, tiles, low, own):
    own[...] = jnp.zeros_like(own)
    backward(plan, tiles, low, own, plan[ENDS, 2], plan[ENDS, 3])


def call(kernel, outs, scratch, args, kinds, tiles, share):
    place = {
        "s": pl.BlockSpec(memory_space=pltpu.SMEM),
        "v": pl.BlockSpec(memory_space=pltpu.VMEM),
    }
    size = sum(math.prod(v.shape) * v.dtype.itemsize for v in [*outs, *args])
    size += sum(math.prod(v.shape) * jnp.dtype(v.dtype).itemsize for v in scratch)
    return pl.pallas_call(
        kernel,
        out_shape=outs,
        in_specs=[place[kind] for kind in kinds],
        out_specs=[place["v"]] * len(outs),
        scratch_shapes=scratch,
        compiler_params=pltpu.CompilerParams(vmem_limit_bytes=size + 2 * 1024 * 1024),
        cost_estimate=pl.CostEstimate(
            flops=int(share * 4 * tiles.size * 128),
            bytes_accessed=tiles.size * 2,
            transcendentals=0,
        ),
    )(*args)


def gram_product(grid, plan, near, tiles, own_pieces, other_pieces):
    rhs, params = own_pieces[0].shape[1:]
    points = tiles.shape[1]
    blocks = grid.count

    def array(lead, kind):
        return jax.ShapeDtypeStruct((*lead, rhs, params), kind)

    field = pltpu.VMEM((blocks, rhs, params), jnp.bfloat16)
    acc = jax.ShapeDtypeStruct((PT_DEV, rhs, points), jnp.float32)
    part, own_sides = call(
        own_forward,
        [acc, array((2, 2), jnp.bfloat16)],
        [field],
        [plan, near, tiles, *own_pieces],
        "ssv" + "v" * len(own_pieces),
        tiles,
        0.25,
    )
    other, low, sides = call(
        other_both,
        [
            array((blocks,), jnp.bfloat16),
            jax.ShapeDtypeStruct((PT_DEV + 1, rhs, points), jnp.bfloat16),
            array((2, 2), jnp.bfloat16),
        ],
        [
            field,
            pltpu.VMEM((PT_DEV, rhs, points), jnp.float32),
            pltpu.VMEM((blocks, rhs, params), jnp.float32),
        ],
        [plan, near, tiles, part, own_sides, *other_pieces],
        "ssvvv" + "v" * len(other_pieces),
        tiles,
        0.5,
    )
    arrived = grid.send(other, "core", 1)
    (own,) = call(
        own_backward,
        [array((blocks,), jnp.float32)],
        [],
        [plan, tiles, low],
        "svv",
        tiles,
        0.25,
    )
    return own, arrived, sides


def shifted(block, distance):
    devices = range(lax.axis_size(BOTH))
    route = [(i - distance, i) for i in devices if i - distance in devices]
    return lax.ppermute(block, BOTH, route)


def edge_weights(prior_weight, is_first, is_last):
    left_weight = shifted(prior_weight, 1)
    right_weight = shifted(prior_weight, -1)
    zero = jnp.zeros_like(prior_weight[0])
    w_left = jnp.stack([jnp.where(is_first, zero, left_weight[0]), jnp.where(is_first, zero, prior_weight[1])])
    w_right = jnp.stack([prior_weight[0], jnp.where(is_last, prior_weight[0], right_weight[1])])
    w_left = w_left[:, None, :]
    w_right = w_right[:, None, :]
    return w_left, w_right


def on_device(jac_tiles, tile_pose, tile_point, tile_valid, prior_weight, right_side):
    grid = Grid()
    place = lax.axis_index(BOTH)
    is_first = place == 0
    is_last = place == grid.count - 1
    plan = make_plan(grid, place, tile_pose, tile_point, tile_valid, jac_tiles)
    before = grid.slot(jnp.maximum(place - 1, 0), place)
    after = grid.slot(jnp.minimum(place + 1, grid.count - 1), place)
    near = jnp.stack([before[0], 2 * before[1], after[0], 2 * after[1]])
    theta = (highest + lowest) / 2.0
    delta = (highest - lowest) / 2.0
    sigma = theta / delta
    ratio = 1.0 / sigma
    right_side = jnp.swapaxes(right_side, 1, 2)
    step = right_side / theta
    solution = jnp.zeros(right_side.shape, jnp.float32)
    residual = right_side
    for turn in range(ITERS):
        if turn > 0:
            new_ratio = 1.0 / (2.0 * sigma - ratio)
            step = new_ratio * ratio * step + 2.0 * new_ratio / delta * residual
            ratio = new_ratio
        solution = solution + step
        low = step.astype(jnp.bfloat16)
        pieces, swapped, (plan, near) = gather_field(grid, low, plan, near)
        if turn == 0:
            pieces[1], later = lax.optimization_barrier((pieces[1], prior_weight))
            w_left, w_right = edge_weights(later, is_first, is_last)
        own, arrived, sides = gram_product(grid, plan, near, jac_tiles, pieces, swapped)
        gram = scatter_sum(grid, own, arrived)
        left, right = sides.astype(jnp.float32)
        right = jnp.where(is_last, step[::-1], right)
        prior = w_left * (step - left) + w_right * (step - right)
        residual = residual - (gram + prior + damping * step)
    return jnp.swapaxes(solution, 1, 2), jnp.swapaxes(residual, 1, 2)


def solution(mesh):
    return jax.shard_map(
        on_device,
        mesh=mesh,
        in_specs=(
            P(BOTH, None, None),
            P(BOTH),
            P(BOTH),
            P(BOTH),
            P(BOTH, None),
            P(BOTH, None, None),
        ),
        out_specs=(P(BOTH, None, None), P(BOTH, None, None)),
        check_vma=False,
    )
```

```python
import math

import jax
import jax.numpy as jnp
from jax import lax
from jax.experimental import pallas as pl
from jax.experimental.pallas import tpu as pltpu
from jax.sharding import PartitionSpec as P

PT_DEV = 16
ITERS = 3
UNROLL = 8

damping = 0.5
lowest = 0.5
highest = 8.0
BOTH = ("row", "col")


class Grid:
    def __init__(self):
        rows = lax.axis_size("row")
        cols = lax.axis_size("col")
        self.sizes = {"y": rows // 2, "core": 2, "z": cols // 2, "x": 2}
        self.count = rows * cols

    def coords(self, device):
        cols = self.sizes["z"] * 2
        if isinstance(device, int):
            row, col = device // cols, device % cols
            return {"y": row // 2, "core": row % 2, "z": col // 2, "x": col % 2}
        row, col = lax.div(device, cols), lax.rem(device, cols)
        return {"y": lax.div(row, 2), "core": lax.rem(row, 2), "z": lax.div(col, 2), "x": lax.rem(col, 2)}

    def device(self, at):
        row = at["y"] * 2 + at["core"]
        col = at["z"] * 2 + at["x"]
        return row * self.sizes["z"] * 2 + col

    def slot(self, device, home):
        at, base = self.coords(device), self.coords(home)
        away = {a: lax.rem(at[a] - base[a] + n, n) for a, n in self.sizes.items()}
        away["z"] = at["z"] ^ base["z"]
        x, y = away["x"], away["y"]
        if self.sizes["y"] == 2:
            swap = at["core"] == 1
            x, y = jnp.where(swap, y, x), jnp.where(swap, x, y)
        return away["core"], (y * 2 + x) * self.sizes["z"] + away["z"]

    def send(self, block, axes, distance):
        route = []
        for source in range(self.count):
            at = self.coords(source)
            names = axes if isinstance(axes, str) else axes[at["core"]]
            for name in names.split():
                moved = (at[name] + distance) % self.sizes[name]
                at[name] = at[name] ^ distance if name == "z" else moved
            route.append((source, self.device(at)))
        return lax.ppermute(block, BOTH, route)

    def fetch(self, block, axes, distance):
        return self.send(block, axes, -distance)


ONE, TWO, BOTH_AXES = ("x", "y"), ("y", "x"), "x y"


def z_order(depth):
    return sorted(range(1, depth), key=lambda r: (r >= depth // 2, -r))


def gather_field(grid, low, *early):
    depth, wide = grid.sizes["z"], grid.sizes["y"]
    column = {0: low} | {r: grid.send(low, "z", r) for r in z_order(depth)}
    column = [column[r] for r in range(depth)]
    base, *early = lax.optimization_barrier((jnp.concatenate(column), *early))
    if wide == 2:
        pieces = [base] + [grid.send(base, axes, 1) for axes in (ONE, TWO, BOTH_AXES)]
    else:
        lines = [base] + [grid.fetch(base, "y", r) for r in range(1, wide)]
        pieces = []
        for line in lines:
            pieces += [line, grid.fetch(line, "x", 1)]
    return pieces, [grid.fetch(piece, "core", 1) for piece in pieces], early


def scatter_sum(grid, own, arrived):
    depth, wide = grid.sizes["z"], grid.sizes["y"]
    total = own + arrived.astype(jnp.float32)
    total = total.reshape((wide, 2, depth, 2) + total.shape[1:])

    def narrow(v):
        return v.astype(jnp.bfloat16)

    def widen(v):
        return v.astype(jnp.float32)

    if wide == 2:
        half = depth // 2
        corner = narrow(total[1, 1])
        via_one = widen(grid.send(corner[:half], ONE, 1))
        via_two = widen(grid.send(corner[half:], TWO, 1))
        one = narrow(jnp.concatenate([total[0, 1, :half], total[0, 1, half:] + via_two]))
        two = narrow(jnp.concatenate([total[1, 0, :half] + via_one, total[1, 0, half:]]))
        base = total[0, 0] + widen(grid.send(one, ONE, 1)) + widen(grid.send(two, TWO, 1))
    else:
        total = total[:, 0] + widen(grid.send(narrow(total[:, 1]), "x", 1))
        base = total[0]
        for r in range(1, wide):
            base = base + widen(grid.send(narrow(total[r]), "y", r))
    gram = base[0]
    for r in z_order(depth):
        gram = gram + widen(grid.send(narrow(base[r]), "z", r))
    return gram


def plan_kernel(core, pose, point, valid, jac, out, jac_copy, sem):
    copy = pltpu.make_async_copy(jac, jac_copy, sem)
    copy.start()
    tiles, slots = core.shape[1], out.shape[1]
    row_id = lax.broadcasted_iota(jnp.int32, (tiles, tiles), 0)
    col_id = lax.broadcasted_iota(jnp.int32, (tiles, tiles), 1)
    lane = lax.broadcasted_iota(jnp.int32, (tiles, slots), 1)

    def column(row):
        return jnp.sum(jnp.where(row_id == col_id, row, 0.0), axis=1, keepdims=True)

    def half_up(v, unit):
        whole = v.astype(jnp.int32) + (unit - 1)
        return (whole & ~(unit - 1)).astype(jnp.float32)

    def arrange(key, phase):
        key_col, phase_col = column(key), column(phase)
        same = jnp.where((key_col == key) & (real_col > 0.0) & (real > 0.0), 1.0, 0.0)
        count = jnp.sum(same, axis=0, keepdims=True)
        rank = jnp.sum(jnp.where(row_id < col_id, same, 0.0), axis=0, keepdims=True)
        rank_col = jnp.sum(jnp.where(col_id < row_id, same, 0.0), axis=1, keepdims=True)
        room = jnp.where((rank == 0.0) & (real > 0.0), half_up(count, 2), 0.0)
        start = jnp.sum(jnp.where(key < key_col, room, 0.0), axis=1, keepdims=True)
        first = jnp.sum(jnp.where(phase == 0.0, room, 0.0), axis=1, keepdims=True)
        second = jnp.sum(jnp.where(phase == 0.0, 0.0, room), axis=1, keepdims=True)
        padded = half_up(first, 2 * UNROLL)
        place = start + rank_col + jnp.where(phase_col == 0.0, 0.0, padded - first)
        place = jnp.where(real_col > 0.0, place, -1.0)
        hit = jnp.where(place.astype(jnp.int32) == lane, 1.0, 0.0)
        return hit, padded, padded + half_up(second, 2 * UNROLL)

    def pick(hit, values):
        return jnp.sum(hit * values, axis=0, keepdims=True)

    real = valid[...].astype(jnp.float32)
    real_col = column(real)
    core_row = core[...].astype(jnp.float32)
    pose_row = pose[...].astype(jnp.float32)
    point_row = point[...].astype(jnp.float32)
    pose_col, point_col = column(pose_row), column(point_row)
    tile_col = column(col_id[:1].astype(jnp.float32))
    hit, first, last = arrange(core_row * PT_DEV + point_row, core_row)
    rows = [
        pick(hit, tile_col),
        pick(hit, pose_col),
        pick(hit, jnp.ones_like(tile_col)),
        pick(hit, point_col),
    ]
    ends = [first, last]
    other = 1.0 - core_row
    hit, first, last = arrange(other * 65536.0 + pose_row, other)
    rows += [
        pick(hit, tile_col),
        pick(hit, point_col - PT_DEV) + PT_DEV,
        pick(hit, pose_col),
    ]
    ends += [first, last]
    spot = lane[:1]
    tail = jnp.zeros_like(rows[0])
    for k, end in enumerate(ends):
        tail = jnp.where(spot == k, end * (0.5 / UNROLL), tail)
    for k, row in enumerate(rows + [tail]):
        out[k : k + 1] = row.astype(jnp.int32)
    copy.wait()


def make_plan(grid, place, tile_pose, tile_point, tile_valid, jac):
    tiles = tile_pose.shape[0]
    core, chip = grid.slot(lax.div(tile_pose, 2), place)
    pose = 2 * chip + lax.rem(tile_pose, 2)
    slots = tiles + max(2 * PT_DEV, min(tiles, grid.count)) + 4 * UNROLL
    slots = -(-slots // 128) * 128
    rows = [v.reshape(1, tiles) for v in (core, pose, tile_point, tile_valid)]
    vmem = pl.BlockSpec(memory_space=pltpu.VMEM)
    return pl.pallas_call(
        plan_kernel,
        out_shape=[
            jax.ShapeDtypeStruct((8, slots), jnp.int32),
            jax.ShapeDtypeStruct(jac.shape, jac.dtype),
        ],
        in_specs=[vmem] * 4 + [pl.BlockSpec(memory_space=pl.ANY)],
        out_specs=[vmem] * 2,
        scratch_shapes=[pltpu.SemaphoreType.DMA],
        compiler_params=pltpu.CompilerParams(vmem_limit_bytes=jac.size * 2 + 4 * 1024 * 1024),
    )(*rows, jac)


NT = (((1,), (1,)), ((), ()))
NN = (((1,), (0,)), ((), ()))
F_TILE, F_POSE, F_REAL, F_POINT, B_TILE, B_POINT, B_POSE, ENDS = range(8)


def forward(plan, tiles, field, acc, begin, end):
    def body(i, _):
        for u in range(UNROLL):
            j = 2 * (i * UNROLL + u)
            block = [
                field[plan[F_POSE, j + h], : acc.shape[1]]
                * plan[F_REAL, j + h].astype(jnp.float32).astype(jnp.bfloat16)
                for h in range(2)
            ]
            tile = [tiles[plan[F_TILE, j + h]] for h in range(2)]
            acc[plan[F_POINT, j]] += lax.dot_general(
                jnp.concatenate(block, axis=1),
                jnp.concatenate(tile, axis=1),
                NT,
                preferred_element_type=jnp.float32,
            )
        return 0

    lax.fori_loop(begin, end, body, 0)


def backward(plan, tiles, low, total, begin, end):
    def body(i, _):
        for u in range(UNROLL):
            j = 2 * (i * UNROLL + u)
            block = [low[plan[B_POINT, j + h]] for h in range(2)]
            tile = [tiles[plan[B_TILE, j + h]] for h in range(2)]
            total[plan[B_POSE, j]] += lax.dot_general(
                jnp.concatenate(block, axis=1),
                jnp.concatenate(tile, axis=0),
                NN,
                preferred_element_type=jnp.float32,
            )
        return 0

    lax.fori_loop(begin, end, body, 0)


def assemble(pieces, field):
    start = 0
    for piece in pieces:
        field[start : start + piece.shape[0]] = piece[...]
        start += piece.shape[0]


def own_forward(plan, near, tiles, *refs):
    pieces, (acc, sides, field) = refs[:-3], refs[-3:]
    assemble(pieces, field)
    for side in range(2):
        sides[side] = field[pl.ds(near[2 * side + 1], 2)]
    acc[...] = jnp.zeros_like(acc)
    forward(plan, tiles, field, acc, 0, plan[ENDS, 0])


def other_both(plan, near, tiles, part, own_sides, *refs):
    pieces, (other, low, sides, field, acc, total) = refs[:-6], refs[-6:]
    assemble(pieces, field)
    for side in range(2):

        @pl.when(near[2 * side] == 0)
        def _():
            sides[side] = own_sides[side]

        @pl.when(near[2 * side] != 0)
        def _():
            sides[side] = field[pl.ds(near[2 * side + 1], 2)]

    acc[...] = part[...]
    total[...] = jnp.zeros_like(total)
    forward(plan, tiles, field, acc, plan[ENDS, 0], plan[ENDS, 1])
    points = acc.shape[0]
    low[:points] = acc[...].astype(jnp.bfloat16)
    low[points] = jnp.zeros(low.shape[1:], jnp.bfloat16)
    backward(plan, tiles, low, total, 0, plan[ENDS, 2])
    other[...] = total[...].astype(other.dtype)


def own_backward(plan, tiles, low, own):
    own[...] = jnp.zeros_like(own)
    backward(plan, tiles, low, own, plan[ENDS, 2], plan[ENDS, 3])


def call(kernel, outs, scratch, args, kinds, tiles, share):
    place = {
        "s": pl.BlockSpec(memory_space=pltpu.SMEM),
        "v": pl.BlockSpec(memory_space=pltpu.VMEM),
    }
    size = sum(math.prod(v.shape) * v.dtype.itemsize for v in [*outs, *args])
    size += sum(math.prod(v.shape) * jnp.dtype(v.dtype).itemsize for v in scratch)
    return pl.pallas_call(
        kernel,
        out_shape=outs,
        in_specs=[place[kind] for kind in kinds],
        out_specs=[place["v"]] * len(outs),
        scratch_shapes=scratch,
        compiler_params=pltpu.CompilerParams(vmem_limit_bytes=size + 2 * 1024 * 1024),
        cost_estimate=pl.CostEstimate(
            flops=int(share * 4 * tiles.size * 128),
            bytes_accessed=tiles.size * 2,
            transcendentals=0,
        ),
    )(*args)


def gram_product(grid, plan, near, tiles, rhs, own_pieces, other_pieces):
    rows, params = own_pieces[0].shape[1:]
    points = tiles.shape[1]
    blocks = grid.count

    def array(lead, kind):
        return jax.ShapeDtypeStruct((*lead, rhs, params), kind)

    field = pltpu.VMEM((blocks, rows, params), jnp.bfloat16)
    beside = jax.ShapeDtypeStruct((2, 2, rows, params), jnp.bfloat16)
    acc = jax.ShapeDtypeStruct((PT_DEV, rhs, points), jnp.float32)
    part, own_sides = call(
        own_forward,
        [acc, beside],
        [field],
        [plan, near, tiles, *own_pieces],
        "ssv" + "v" * len(own_pieces),
        tiles,
        0.25,
    )
    other, low, sides = call(
        other_both,
        [
            array((blocks,), jnp.bfloat16),
            jax.ShapeDtypeStruct((PT_DEV + 1, rhs, points), jnp.bfloat16),
            beside,
        ],
        [
            field,
            pltpu.VMEM((PT_DEV, rhs, points), jnp.float32),
            pltpu.VMEM((blocks, rhs, params), jnp.float32),
        ],
        [plan, near, tiles, part, own_sides, *other_pieces],
        "ssvvv" + "v" * len(other_pieces),
        tiles,
        0.5,
    )
    arrived = grid.send(other, "core", 1)
    (own,) = call(
        own_backward,
        [array((blocks,), jnp.float32)],
        [],
        [plan, tiles, low],
        "svv",
        tiles,
        0.25,
    )
    return own, arrived, sides


def edge_weights(prior_weight, left_weight, right_weight, is_first, is_last):
    zero = jnp.zeros_like(prior_weight[0])
    w_left = jnp.stack([jnp.where(is_first, zero, left_weight[0]), jnp.where(is_first, zero, prior_weight[1])])
    w_right = jnp.stack([prior_weight[0], jnp.where(is_last, prior_weight[0], right_weight[1])])
    return w_left[:, None, :], w_right[:, None, :]


def on_device(jac_tiles, tile_pose, tile_point, tile_valid, prior_weight, right_side):
    grid = Grid()
    place = lax.axis_index(BOTH)
    is_first = place == 0
    is_last = place == grid.count - 1
    plan, tiles = make_plan(grid, place, tile_pose, tile_point, tile_valid, jac_tiles)
    before = grid.slot(jnp.maximum(place - 1, 0), place)
    after = grid.slot(jnp.minimum(place + 1, grid.count - 1), place)
    near = jnp.stack([before[0], 2 * before[1], after[0], 2 * after[1]])
    theta = (highest + lowest) / 2.0
    delta = (highest - lowest) / 2.0
    sigma = theta / delta
    ratio = 1.0 / sigma
    right_side = jnp.swapaxes(right_side, 1, 2)
    step = right_side / theta
    solution = jnp.zeros(right_side.shape, jnp.float32)
    residual = right_side
    for turn in range(ITERS):
        if turn > 0:
            new_ratio = 1.0 / (2.0 * sigma - ratio)
            step = new_ratio * ratio * step + 2.0 * new_ratio / delta * residual
            ratio = new_ratio
        solution = solution + step
        low = step.astype(jnp.bfloat16)
        if turn == 0:
            extra = jnp.broadcast_to(prior_weight[:, None, :], (2, 16, prior_weight.shape[1]))
            low = jnp.concatenate([low, extra.astype(jnp.bfloat16)], axis=1)
        pieces, swapped, (plan, near, tiles, result) = gather_field(
            grid, low, plan, near, tiles, jnp.swapaxes(solution, 1, 2)
        )
        own, arrived, sides = gram_product(grid, plan, near, tiles, step.shape[1], pieces, swapped)
        sides = sides.astype(jnp.float32)
        if turn == 0:
            w_left, w_right = edge_weights(prior_weight, *sides[:, :, step.shape[1]], is_first, is_last)
        gram = scatter_sum(grid, own, arrived)
        left, right = sides[:, :, : step.shape[1]]
        right = jnp.where(is_last, step[::-1], right)
        prior = w_left * (step - left) + w_right * (step - right)
        residual = residual - (gram + prior + damping * step)
    return result, jnp.swapaxes(residual, 1, 2)


def solution(mesh):
    return jax.shard_map(
        on_device,
        mesh=mesh,
        in_specs=(
            P(BOTH, None, None),
            P(BOTH),
            P(BOTH),
            P(BOTH),
            P(BOTH, None),
            P(BOTH, None, None),
        ),
        out_specs=(P(BOTH, None, None), P(BOTH, None, None)),
        check_vma=False,
    )
```

```python
import math

import jax
import jax.numpy as jnp
from jax import lax
from jax.experimental import pallas as pl
from jax.experimental.pallas import tpu as pltpu
from jax.sharding import PartitionSpec as P

PT_DEV = 16
ITERS = 3
UNROLL = 8

damping = 0.5
lowest = 0.5
highest = 8.0
BOTH = ("row", "col")


class Grid:
    def __init__(self):
        rows = lax.axis_size("row")
        cols = lax.axis_size("col")
        self.sizes = {"y": rows // 2, "core": 2, "z": cols // 2, "x": 2}
        self.count = rows * cols

    def coords(self, device):
        cols = self.sizes["z"] * 2
        if isinstance(device, int):
            row, col = device // cols, device % cols
            return {"y": row // 2, "core": row % 2, "z": col // 2, "x": col % 2}
        row, col = lax.div(device, cols), lax.rem(device, cols)
        return {"y": lax.div(row, 2), "core": lax.rem(row, 2), "z": lax.div(col, 2), "x": lax.rem(col, 2)}

    def device(self, at):
        row = at["y"] * 2 + at["core"]
        col = at["z"] * 2 + at["x"]
        return row * self.sizes["z"] * 2 + col

    def slot(self, device, home):
        at, base = self.coords(device), self.coords(home)
        away = {a: lax.rem(at[a] - base[a] + n, n) for a, n in self.sizes.items()}
        away["z"] = at["z"] ^ base["z"]
        x, y = away["x"], away["y"]
        if self.sizes["y"] == 2:
            swap = at["core"] == 1
            x, y = jnp.where(swap, y, x), jnp.where(swap, x, y)
        return away["core"], (y * 2 + x) * self.sizes["z"] + away["z"]

    def send(self, block, axes, distance):
        route = []
        for source in range(self.count):
            at = self.coords(source)
            names = axes if isinstance(axes, str) else axes[at["core"]]
            for name in names.split():
                moved = (at[name] + distance) % self.sizes[name]
                at[name] = at[name] ^ distance if name == "z" else moved
            route.append((source, self.device(at)))
        return lax.ppermute(block, BOTH, route)

    def fetch(self, block, axes, distance):
        return self.send(block, axes, -distance)


ONE, TWO, BOTH_AXES = ("x", "y"), ("y", "x"), "x y"


def z_order(depth):
    return sorted(range(1, depth), key=lambda r: (r >= depth // 2, -r))


def gather_field(grid, low, *early):
    depth, wide = grid.sizes["z"], grid.sizes["y"]
    column = {0: low} | {r: grid.send(low, "z", r) for r in z_order(depth)}
    column = [column[r] for r in range(depth)]
    base, *early = lax.optimization_barrier((jnp.concatenate(column), *early))
    if wide == 2:
        pieces = [base] + [grid.send(base, axes, 1) for axes in (ONE, TWO, BOTH_AXES)]
    else:
        lines = [base] + [grid.fetch(base, "y", r) for r in range(1, wide)]
        pieces = []
        for line in lines:
            pieces += [line, grid.fetch(line, "x", 1)]
    return pieces, [grid.fetch(piece, "core", 1) for piece in pieces], early


def scatter_sum(grid, own, arrived):
    depth, wide = grid.sizes["z"], grid.sizes["y"]
    total = own + arrived.astype(jnp.float32)
    total = total.reshape((wide, 2, depth, 2) + total.shape[1:])

    def narrow(v):
        return v.astype(jnp.bfloat16)

    def widen(v):
        return v.astype(jnp.float32)

    if wide == 2:
        half = depth // 2
        corner_a, corner_b = narrow(total[1, 1, half:]), narrow(total[1, 1, :half])
        one_a, two_b = narrow(total[0, 1, half:]), narrow(total[1, 0, :half])
        corner_a, corner_b, one_a, two_b = lax.optimization_barrier((corner_a, corner_b, one_a, two_b))
        one_a = grid.send(one_a, ONE, 1)
        two_b = grid.send(two_b, TWO, 1)
        two_a = total[1, 0, half:] + widen(grid.send(corner_a, ONE, 1))
        one_b = total[0, 1, :half] + widen(grid.send(corner_b, TWO, 1))
        two_a = grid.send(lax.optimization_barrier(narrow(two_a)), TWO, 1)
        one_b = grid.send(lax.optimization_barrier(narrow(one_b)), ONE, 1)
        one_a, one_b, two_a, two_b = lax.optimization_barrier((one_a, one_b, two_a, two_b))
        base_a = total[0, 0, half:] + widen(one_a) + widen(two_a)
        base_b = total[0, 0, :half] + widen(one_b) + widen(two_b)
        base = jnp.concatenate([base_b, base_a])
    else:
        total = total[:, 0] + widen(grid.send(narrow(total[:, 1]), "x", 1))
        base = total[0]
        for r in range(1, wide):
            base = base + widen(grid.send(narrow(total[r]), "y", r))
    order = range(depth - 1, 0, -1)
    parts = lax.optimization_barrier([narrow(base[r]) for r in order])
    gram = base[0]
    for r, part in zip(order, parts):
        gram = gram + widen(grid.send(part, "z", r))
    return gram


def plan_kernel(core, pose, point, valid, jac, out, jac_copy, sem):
    copy = pltpu.make_async_copy(jac, jac_copy, sem)
    copy.start()
    tiles, slots = core.shape[1], out.shape[1]
    row_id = lax.broadcasted_iota(jnp.int32, (tiles, tiles), 0)
    col_id = lax.broadcasted_iota(jnp.int32, (tiles, tiles), 1)
    lane = lax.broadcasted_iota(jnp.int32, (tiles, slots), 1)

    def column(row):
        return jnp.sum(jnp.where(row_id == col_id, row, 0.0), axis=1, keepdims=True)

    def half_up(v, unit):
        whole = v.astype(jnp.int32) + (unit - 1)
        return (whole & ~(unit - 1)).astype(jnp.float32)

    def arrange(key, phase):
        key_col, phase_col = column(key), column(phase)
        same = jnp.where((key_col == key) & (real_col > 0.0) & (real > 0.0), 1.0, 0.0)
        count = jnp.sum(same, axis=0, keepdims=True)
        rank = jnp.sum(jnp.where(row_id < col_id, same, 0.0), axis=0, keepdims=True)
        rank_col = jnp.sum(jnp.where(col_id < row_id, same, 0.0), axis=1, keepdims=True)
        room = jnp.where((rank == 0.0) & (real > 0.0), half_up(count, 2), 0.0)
        start = jnp.sum(jnp.where(key < key_col, room, 0.0), axis=1, keepdims=True)
        first = jnp.sum(jnp.where(phase == 0.0, room, 0.0), axis=1, keepdims=True)
        second = jnp.sum(jnp.where(phase == 0.0, 0.0, room), axis=1, keepdims=True)
        padded = half_up(first, 2 * UNROLL)
        place = start + rank_col + jnp.where(phase_col == 0.0, 0.0, padded - first)
        place = jnp.where(real_col > 0.0, place, -1.0)
        hit = jnp.where(place.astype(jnp.int32) == lane, 1.0, 0.0)
        return hit, padded, padded + half_up(second, 2 * UNROLL)

    def pick(hit, values):
        return jnp.sum(hit * values, axis=0, keepdims=True)

    real = valid[...].astype(jnp.float32)
    real_col = column(real)
    core_row = core[...].astype(jnp.float32)
    pose_row = pose[...].astype(jnp.float32)
    point_row = point[...].astype(jnp.float32)
    pose_col, point_col = column(pose_row), column(point_row)
    tile_col = column(col_id[:1].astype(jnp.float32))
    hit, first, last = arrange(core_row * PT_DEV + point_row, core_row)
    rows = [
        pick(hit, tile_col),
        pick(hit, pose_col),
        pick(hit, jnp.ones_like(tile_col)),
        pick(hit, point_col),
    ]
    ends = [first, last]
    other = 1.0 - core_row
    hit, first, last = arrange(other * 65536.0 + pose_row, other)
    rows += [
        pick(hit, tile_col),
        pick(hit, point_col - PT_DEV) + PT_DEV,
        pick(hit, pose_col),
    ]
    ends += [first, last]
    spot = lane[:1]
    tail = jnp.zeros_like(rows[0])
    for k, end in enumerate(ends):
        tail = jnp.where(spot == k, end * (0.5 / UNROLL), tail)
    for k, row in enumerate(rows + [tail]):
        out[k : k + 1] = row.astype(jnp.int32)
    copy.wait()


def make_plan(grid, place, tile_pose, tile_point, tile_valid, jac):
    tiles = tile_pose.shape[0]
    core, chip = grid.slot(lax.div(tile_pose, 2), place)
    pose = 2 * chip + lax.rem(tile_pose, 2)
    slots = tiles + max(2 * PT_DEV, min(tiles, grid.count)) + 4 * UNROLL
    slots = -(-slots // 128) * 128
    rows = [v.reshape(1, tiles) for v in (core, pose, tile_point, tile_valid)]
    vmem = pl.BlockSpec(memory_space=pltpu.VMEM)
    return pl.pallas_call(
        plan_kernel,
        out_shape=[
            jax.ShapeDtypeStruct((8, slots), jnp.int32),
            jax.ShapeDtypeStruct(jac.shape, jac.dtype),
        ],
        in_specs=[vmem] * 4 + [pl.BlockSpec(memory_space=pl.ANY)],
        out_specs=[vmem] * 2,
        scratch_shapes=[pltpu.SemaphoreType.DMA],
        compiler_params=pltpu.CompilerParams(vmem_limit_bytes=jac.size * 2 + 4 * 1024 * 1024),
    )(*rows, jac)


NT = (((1,), (1,)), ((), ()))
NN = (((1,), (0,)), ((), ()))
F_TILE, F_POSE, F_REAL, F_POINT, B_TILE, B_POINT, B_POSE, ENDS = range(8)


def forward(plan, tiles, field, acc, begin, end):
    def body(i, _):
        for u in range(UNROLL):
            j = 2 * (i * UNROLL + u)
            block = [
                field[plan[F_POSE, j + h], : acc.shape[1]]
                * plan[F_REAL, j + h].astype(jnp.float32).astype(jnp.bfloat16)
                for h in range(2)
            ]
            tile = [tiles[plan[F_TILE, j + h]] for h in range(2)]
            acc[plan[F_POINT, j]] += lax.dot_general(
                jnp.concatenate(block, axis=1),
                jnp.concatenate(tile, axis=1),
                NT,
                preferred_element_type=jnp.float32,
            )
        return 0

    lax.fori_loop(begin, end, body, 0)


def backward(plan, tiles, low, total, begin, end):
    def body(i, _):
        for u in range(UNROLL):
            j = 2 * (i * UNROLL + u)
            block = [low[plan[B_POINT, j + h]] for h in range(2)]
            tile = [tiles[plan[B_TILE, j + h]] for h in range(2)]
            total[plan[B_POSE, j]] += lax.dot_general(
                jnp.concatenate(block, axis=1),
                jnp.concatenate(tile, axis=0),
                NN,
                preferred_element_type=jnp.float32,
            )
        return 0

    lax.fori_loop(begin, end, body, 0)


def assemble(pieces, field):
    start = 0
    for piece in pieces:
        field[start : start + piece.shape[0]] = piece[...]
        start += piece.shape[0]


def own_forward(plan, near, tiles, *refs):
    pieces, (acc, sides, field) = refs[:-3], refs[-3:]
    assemble(pieces, field)
    for side in range(2):
        sides[side] = field[pl.ds(near[2 * side + 1], 2)]
    acc[...] = jnp.zeros_like(acc)
    forward(plan, tiles, field, acc, 0, plan[ENDS, 0])


def other_both(plan, near, tiles, part, own_sides, *refs):
    pieces, (other, low, sides, field, acc, total) = refs[:-6], refs[-6:]
    assemble(pieces, field)
    for side in range(2):

        @pl.when(near[2 * side] == 0)
        def _():
            sides[side] = own_sides[side]

        @pl.when(near[2 * side] != 0)
        def _():
            sides[side] = field[pl.ds(near[2 * side + 1], 2)]

    acc[...] = part[...]
    total[...] = jnp.zeros_like(total)
    forward(plan, tiles, field, acc, plan[ENDS, 0], plan[ENDS, 1])
    points = acc.shape[0]
    low[:points] = acc[...].astype(jnp.bfloat16)
    low[points] = jnp.zeros(low.shape[1:], jnp.bfloat16)
    backward(plan, tiles, low, total, 0, plan[ENDS, 2])
    other[...] = total[...].astype(other.dtype)


def own_backward(plan, tiles, low, own):
    own[...] = jnp.zeros_like(own)
    backward(plan, tiles, low, own, plan[ENDS, 2], plan[ENDS, 3])


def call(kernel, outs, scratch, args, kinds, tiles, share):
    place = {
        "s": pl.BlockSpec(memory_space=pltpu.SMEM),
        "v": pl.BlockSpec(memory_space=pltpu.VMEM),
    }
    size = sum(math.prod(v.shape) * v.dtype.itemsize for v in [*outs, *args])
    size += sum(math.prod(v.shape) * jnp.dtype(v.dtype).itemsize for v in scratch)
    return pl.pallas_call(
        kernel,
        out_shape=outs,
        in_specs=[place[kind] for kind in kinds],
        out_specs=[place["v"]] * len(outs),
        scratch_shapes=scratch,
        compiler_params=pltpu.CompilerParams(vmem_limit_bytes=size + 2 * 1024 * 1024),
        cost_estimate=pl.CostEstimate(
            flops=int(share * 4 * tiles.size * 128),
            bytes_accessed=tiles.size * 2,
            transcendentals=0,
        ),
    )(*args)


def gram_product(grid, plan, near, tiles, rhs, own_pieces, other_pieces):
    rows, params = own_pieces[0].shape[1:]
    points = tiles.shape[1]
    blocks = grid.count

    def array(lead, kind):
        return jax.ShapeDtypeStruct((*lead, rhs, params), kind)

    field = pltpu.VMEM((blocks, rows, params), jnp.bfloat16)
    beside = jax.ShapeDtypeStruct((2, 2, rows, params), jnp.bfloat16)
    acc = jax.ShapeDtypeStruct((PT_DEV, rhs, points), jnp.float32)
    part, own_sides = call(
        own_forward,
        [acc, beside],
        [field],
        [plan, near, tiles, *own_pieces],
        "ssv" + "v" * len(own_pieces),
        tiles,
        0.25,
    )
    other, low, sides = call(
        other_both,
        [
            array((blocks,), jnp.bfloat16),
            jax.ShapeDtypeStruct((PT_DEV + 1, rhs, points), jnp.bfloat16),
            beside,
        ],
        [
            field,
            pltpu.VMEM((PT_DEV, rhs, points), jnp.float32),
            pltpu.VMEM((blocks, rhs, params), jnp.float32),
        ],
        [plan, near, tiles, part, own_sides, *other_pieces],
        "ssvvv" + "v" * len(other_pieces),
        tiles,
        0.5,
    )
    arrived = grid.send(other, "core", 1)
    (own,) = call(
        own_backward,
        [array((blocks,), jnp.float32)],
        [],
        [plan, tiles, low],
        "svv",
        tiles,
        0.25,
    )
    return own, arrived, sides


def edge_weights(prior_weight, left_weight, right_weight, is_first, is_last):
    zero = jnp.zeros_like(prior_weight[0])
    w_left = jnp.stack([jnp.where(is_first, zero, left_weight[0]), jnp.where(is_first, zero, prior_weight[1])])
    w_right = jnp.stack([prior_weight[0], jnp.where(is_last, prior_weight[0], right_weight[1])])
    return w_left[:, None, :], w_right[:, None, :]


def on_device(jac_tiles, tile_pose, tile_point, tile_valid, prior_weight, right_side):
    grid = Grid()
    place = lax.axis_index(BOTH)
    is_first = place == 0
    is_last = place == grid.count - 1
    plan, tiles = make_plan(grid, place, tile_pose, tile_point, tile_valid, jac_tiles)
    before = grid.slot(jnp.maximum(place - 1, 0), place)
    after = grid.slot(jnp.minimum(place + 1, grid.count - 1), place)
    near = jnp.stack([before[0], 2 * before[1], after[0], 2 * after[1]])
    theta = (highest + lowest) / 2.0
    delta = (highest - lowest) / 2.0
    sigma = theta / delta
    ratio = 1.0 / sigma
    right_side = jnp.swapaxes(right_side, 1, 2)
    step = right_side / theta
    solution = jnp.zeros(right_side.shape, jnp.float32)
    residual = right_side
    for turn in range(ITERS):
        if turn > 0:
            new_ratio = 1.0 / (2.0 * sigma - ratio)
            step = new_ratio * ratio * step + 2.0 * new_ratio / delta * residual
            ratio = new_ratio
        solution = solution + step
        low = step.astype(jnp.bfloat16)
        if turn == 0:
            extra = jnp.broadcast_to(prior_weight[:, None, :], (2, 16, prior_weight.shape[1]))
            low = jnp.concatenate([low, extra.astype(jnp.bfloat16)], axis=1)
        pieces, swapped, (plan, near, tiles, result) = gather_field(
            grid, low, plan, near, tiles, jnp.swapaxes(solution, 1, 2)
        )
        own, arrived, sides = gram_product(grid, plan, near, tiles, step.shape[1], pieces, swapped)
        sides = sides.astype(jnp.float32)
        if turn == 0:
            w_left, w_right = edge_weights(prior_weight, *sides[:, :, step.shape[1]], is_first, is_last)
        gram = scatter_sum(grid, own, arrived)
        left, right = sides[:, :, : step.shape[1]]
        right = jnp.where(is_last, step[::-1], right)
        prior = w_left * (step - left) + w_right * (step - right)
        residual = residual - (gram + prior + damping * step)
    return result, jnp.swapaxes(residual, 1, 2)


def solution(mesh):
    return jax.shard_map(
        on_device,
        mesh=mesh,
        in_specs=(
            P(BOTH, None, None),
            P(BOTH),
            P(BOTH),
            P(BOTH),
            P(BOTH, None),
            P(BOTH, None, None),
        ),
        out_specs=(P(BOTH, None, None), P(BOTH, None, None)),
        check_vma=False,
    )
```

```python
import math

import jax
import jax.numpy as jnp
from jax import lax
from jax.experimental import pallas as pl
from jax.experimental.pallas import tpu as pltpu
from jax.sharding import PartitionSpec as P

PT_DEV = 16
ITERS = 3
UNROLL = 8

damping = 0.5
lowest = 0.5
highest = 8.0
BOTH = ("row", "col")


class Grid:
    def __init__(self):
        rows = lax.axis_size("row")
        cols = lax.axis_size("col")
        self.sizes = {"y": rows // 2, "core": 2, "z": cols // 2, "x": 2}
        self.count = rows * cols

    def coords(self, device):
        cols = self.sizes["z"] * 2
        if isinstance(device, int):
            row, col = device // cols, device % cols
            return {"y": row // 2, "core": row % 2, "z": col // 2, "x": col % 2}
        row, col = lax.div(device, cols), lax.rem(device, cols)
        return {"y": lax.div(row, 2), "core": lax.rem(row, 2), "z": lax.div(col, 2), "x": lax.rem(col, 2)}

    def device(self, at):
        row = at["y"] * 2 + at["core"]
        col = at["z"] * 2 + at["x"]
        return row * self.sizes["z"] * 2 + col

    def slot(self, device, home):
        at, base = self.coords(device), self.coords(home)
        away = {a: lax.rem(at[a] - base[a] + n, n) for a, n in self.sizes.items()}
        away["z"] = at["z"] ^ base["z"]
        x, y = away["x"], away["y"]
        if self.sizes["y"] == 2:
            swap = at["core"] == 1
            x, y = jnp.where(swap, y, x), jnp.where(swap, x, y)
        return away["core"], (y * 2 + x) * self.sizes["z"] + away["z"]

    def send(self, block, axes, distance):
        route = []
        for source in range(self.count):
            at = self.coords(source)
            names = axes if isinstance(axes, str) else axes[at["core"]]
            for name in names.split():
                moved = (at[name] + distance) % self.sizes[name]
                at[name] = at[name] ^ distance if name == "z" else moved
            route.append((source, self.device(at)))
        return lax.ppermute(block, BOTH, route)

    def fetch(self, block, axes, distance):
        return self.send(block, axes, -distance)


ONE, TWO, BOTH_AXES = ("x", "y"), ("y", "x"), "x y"


def along_z(grid, block):
    depth = grid.sizes["z"]
    moved = [grid.send(block, "z", r) for r in range(depth - 1, 0, -1)]
    return jnp.concatenate([block] + moved[::-1])


def gather_field(grid, low, *early):
    wide = grid.sizes["y"]
    base = along_z(grid, low)
    if wide == 2:
        corner = grid.send(low, BOTH_AXES, 1)
        base, corner, *early = lax.optimization_barrier((base, corner, *early))
        far = along_z(grid, corner)
        over = [grid.send(base, axes, 1) for axes in (ONE, TWO)]
        base, far = lax.optimization_barrier((base, far))
        pieces = [base, *over, far]
    else:
        base, *early = lax.optimization_barrier((base, *early))
        lines = [base] + [grid.fetch(base, "y", r) for r in range(1, wide)]
        pieces = []
        for line in lines:
            pieces += [line, grid.fetch(line, "x", 1)]
    return pieces, [grid.fetch(piece, "core", 1) for piece in pieces], early


def scatter_sum(grid, own, arrived):
    depth, wide = grid.sizes["z"], grid.sizes["y"]
    total = own + arrived.astype(jnp.float32)
    total = total.reshape((wide, 2, depth, 2) + total.shape[1:])
    order = range(depth - 1, 0, -1)

    def narrow(v):
        return v.astype(jnp.bfloat16)

    def widen(v):
        return v.astype(jnp.float32)

    diagonal = 0.0
    if wide == 2:
        parts = [narrow(total[1, 1, r]) for r in order] + [narrow(total[0, 1]), narrow(total[1, 0])]
        parts = lax.optimization_barrier(parts)
        one, two = grid.send(parts[-2], ONE, 1), grid.send(parts[-1], TWO, 1)
        parts = [grid.send(part, "z", r) for r, part in zip(order, parts)]
        parts = lax.optimization_barrier(parts + [one, two])
        base = total[0, 0] + widen(parts[-2]) + widen(parts[-1])
        corner = narrow(total[1, 1, 0] + sum(widen(part) for part in parts[:-2]))
    else:
        total = total[:, 0] + widen(grid.send(narrow(total[:, 1]), "x", 1))
        base = total[0]
        for r in range(1, wide):
            base = base + widen(grid.send(narrow(total[r]), "y", r))
        corner = None
    parts = [narrow(base[r]) for r in order]
    if corner is not None:
        *parts, corner = lax.optimization_barrier(parts + [corner])
        diagonal = widen(grid.send(corner, BOTH_AXES, 1))
    gram = base[0] + diagonal
    for r, part in zip(order, parts):
        gram = gram + widen(grid.send(part, "z", r))
    return gram


def plan_kernel(core, pose, point, valid, jac, out, jac_copy, sem):
    copy = pltpu.make_async_copy(jac, jac_copy, sem)
    copy.start()
    tiles, slots = core.shape[1], out.shape[1]
    row_id = lax.broadcasted_iota(jnp.int32, (tiles, tiles), 0)
    col_id = lax.broadcasted_iota(jnp.int32, (tiles, tiles), 1)
    lane = lax.broadcasted_iota(jnp.int32, (tiles, slots), 1)

    def column(row):
        return jnp.sum(jnp.where(row_id == col_id, row, 0.0), axis=1, keepdims=True)

    def half_up(v, unit):
        whole = v.astype(jnp.int32) + (unit - 1)
        return (whole & ~(unit - 1)).astype(jnp.float32)

    def arrange(key, phase):
        key_col, phase_col = column(key), column(phase)
        same = jnp.where((key_col == key) & (real_col > 0.0) & (real > 0.0), 1.0, 0.0)
        count = jnp.sum(same, axis=0, keepdims=True)
        rank = jnp.sum(jnp.where(row_id < col_id, same, 0.0), axis=0, keepdims=True)
        rank_col = jnp.sum(jnp.where(col_id < row_id, same, 0.0), axis=1, keepdims=True)
        room = jnp.where((rank == 0.0) & (real > 0.0), half_up(count, 2), 0.0)
        start = jnp.sum(jnp.where(key < key_col, room, 0.0), axis=1, keepdims=True)
        first = jnp.sum(jnp.where(phase == 0.0, room, 0.0), axis=1, keepdims=True)
        second = jnp.sum(jnp.where(phase == 0.0, 0.0, room), axis=1, keepdims=True)
        padded = half_up(first, 2 * UNROLL)
        place = start + rank_col + jnp.where(phase_col == 0.0, 0.0, padded - first)
        place = jnp.where(real_col > 0.0, place, -1.0)
        hit = jnp.where(place.astype(jnp.int32) == lane, 1.0, 0.0)
        return hit, padded, padded + half_up(second, 2 * UNROLL)

    def pick(hit, values):
        return jnp.sum(hit * values, axis=0, keepdims=True)

    real = valid[...].astype(jnp.float32)
    real_col = column(real)
    core_row = core[...].astype(jnp.float32)
    pose_row = pose[...].astype(jnp.float32)
    point_row = point[...].astype(jnp.float32)
    pose_col, point_col = column(pose_row), column(point_row)
    tile_col = column(col_id[:1].astype(jnp.float32))
    hit, first, last = arrange(core_row * PT_DEV + point_row, core_row)
    rows = [
        pick(hit, tile_col),
        pick(hit, pose_col),
        pick(hit, jnp.ones_like(tile_col)),
        pick(hit, point_col),
    ]
    ends = [first, last]
    other = 1.0 - core_row
    hit, first, last = arrange(other * 65536.0 + pose_row, other)
    rows += [
        pick(hit, tile_col),
        pick(hit, point_col - PT_DEV) + PT_DEV,
        pick(hit, pose_col),
    ]
    ends += [first, last]
    spot = lane[:1]
    tail = jnp.zeros_like(rows[0])
    for k, end in enumerate(ends):
        tail = jnp.where(spot == k, end * (0.5 / UNROLL), tail)
    for k, row in enumerate(rows + [tail]):
        out[k : k + 1] = row.astype(jnp.int32)
    copy.wait()


def make_plan(grid, place, tile_pose, tile_point, tile_valid, jac):
    tiles = tile_pose.shape[0]
    core, chip = grid.slot(lax.div(tile_pose, 2), place)
    pose = 2 * chip + lax.rem(tile_pose, 2)
    slots = tiles + max(2 * PT_DEV, min(tiles, grid.count)) + 4 * UNROLL
    slots = -(-slots // 128) * 128
    rows = [v.reshape(1, tiles) for v in (core, pose, tile_point, tile_valid)]
    vmem = pl.BlockSpec(memory_space=pltpu.VMEM)
    return pl.pallas_call(
        plan_kernel,
        out_shape=[
            jax.ShapeDtypeStruct((8, slots), jnp.int32),
            jax.ShapeDtypeStruct(jac.shape, jac.dtype),
        ],
        in_specs=[vmem] * 4 + [pl.BlockSpec(memory_space=pl.ANY)],
        out_specs=[vmem] * 2,
        scratch_shapes=[pltpu.SemaphoreType.DMA],
        compiler_params=pltpu.CompilerParams(vmem_limit_bytes=jac.size * 2 + 4 * 1024 * 1024),
    )(*rows, jac)


NT = (((1,), (1,)), ((), ()))
NN = (((1,), (0,)), ((), ()))
F_TILE, F_POSE, F_REAL, F_POINT, B_TILE, B_POINT, B_POSE, ENDS = range(8)


def forward(plan, tiles, field, acc, begin, end):
    def body(i, _):
        for u in range(UNROLL):
            j = 2 * (i * UNROLL + u)
            block = [
                field[plan[F_POSE, j + h], : acc.shape[1]]
                * plan[F_REAL, j + h].astype(jnp.float32).astype(jnp.bfloat16)
                for h in range(2)
            ]
            tile = [tiles[plan[F_TILE, j + h]] for h in range(2)]
            acc[plan[F_POINT, j]] += lax.dot_general(
                jnp.concatenate(block, axis=1),
                jnp.concatenate(tile, axis=1),
                NT,
                preferred_element_type=jnp.float32,
            )
        return 0

    lax.fori_loop(begin, end, body, 0)


def backward(plan, tiles, low, total, begin, end):
    def body(i, _):
        for u in range(UNROLL):
            j = 2 * (i * UNROLL + u)
            block = [low[plan[B_POINT, j + h]] for h in range(2)]
            tile = [tiles[plan[B_TILE, j + h]] for h in range(2)]
            total[plan[B_POSE, j]] += lax.dot_general(
                jnp.concatenate(block, axis=1),
                jnp.concatenate(tile, axis=0),
                NN,
                preferred_element_type=jnp.float32,
            )
        return 0

    lax.fori_loop(begin, end, body, 0)


def assemble(pieces, field):
    start = 0
    for piece in pieces:
        field[start : start + piece.shape[0]] = piece[...]
        start += piece.shape[0]


def own_forward(plan, near, tiles, *refs):
    pieces, (acc, sides, field) = refs[:-3], refs[-3:]
    assemble(pieces, field)
    for side in range(2):
        sides[side] = field[pl.ds(near[2 * side + 1], 2)]
    acc[...] = jnp.zeros_like(acc)
    forward(plan, tiles, field, acc, 0, plan[ENDS, 0])


def other_both(plan, near, tiles, part, own_sides, *refs):
    pieces, (other, low, sides, field, acc, total) = refs[:-6], refs[-6:]
    assemble(pieces, field)
    for side in range(2):

        @pl.when(near[2 * side] == 0)
        def _():
            sides[side] = own_sides[side]

        @pl.when(near[2 * side] != 0)
        def _():
            sides[side] = field[pl.ds(near[2 * side + 1], 2)]

    acc[...] = part[...]
    total[...] = jnp.zeros_like(total)
    forward(plan, tiles, field, acc, plan[ENDS, 0], plan[ENDS, 1])
    points = acc.shape[0]
    low[:points] = acc[...].astype(jnp.bfloat16)
    low[points] = jnp.zeros(low.shape[1:], jnp.bfloat16)
    backward(plan, tiles, low, total, 0, plan[ENDS, 2])
    other[...] = total[...].astype(other.dtype)


def own_backward(plan, tiles, low, own):
    own[...] = jnp.zeros_like(own)
    backward(plan, tiles, low, own, plan[ENDS, 2], plan[ENDS, 3])


def call(kernel, outs, scratch, args, kinds, tiles, share):
    place = {
        "s": pl.BlockSpec(memory_space=pltpu.SMEM),
        "v": pl.BlockSpec(memory_space=pltpu.VMEM),
    }
    size = sum(math.prod(v.shape) * v.dtype.itemsize for v in [*outs, *args])
    size += sum(math.prod(v.shape) * jnp.dtype(v.dtype).itemsize for v in scratch)
    return pl.pallas_call(
        kernel,
        out_shape=outs,
        in_specs=[place[kind] for kind in kinds],
        out_specs=[place["v"]] * len(outs),
        scratch_shapes=scratch,
        compiler_params=pltpu.CompilerParams(vmem_limit_bytes=size + 2 * 1024 * 1024),
        cost_estimate=pl.CostEstimate(
            flops=int(share * 4 * tiles.size * 128),
            bytes_accessed=tiles.size * 2,
            transcendentals=0,
        ),
    )(*args)


def gram_product(grid, plan, near, tiles, rhs, own_pieces, other_pieces):
    rows, params = own_pieces[0].shape[1:]
    points = tiles.shape[1]
    blocks = grid.count

    def array(lead, kind):
        return jax.ShapeDtypeStruct((*lead, rhs, params), kind)

    field = pltpu.VMEM((blocks, rows, params), jnp.bfloat16)
    beside = jax.ShapeDtypeStruct((2, 2, rows, params), jnp.bfloat16)
    acc = jax.ShapeDtypeStruct((PT_DEV, rhs, points), jnp.float32)
    part, own_sides = call(
        own_forward,
        [acc, beside],
        [field],
        [plan, near, tiles, *own_pieces],
        "ssv" + "v" * len(own_pieces),
        tiles,
        0.25,
    )
    other, low, sides = call(
        other_both,
        [
            array((blocks,), jnp.bfloat16),
            jax.ShapeDtypeStruct((PT_DEV + 1, rhs, points), jnp.bfloat16),
            beside,
        ],
        [
            field,
            pltpu.VMEM((PT_DEV, rhs, points), jnp.float32),
            pltpu.VMEM((blocks, rhs, params), jnp.float32),
        ],
        [plan, near, tiles, part, own_sides, *other_pieces],
        "ssvvv" + "v" * len(other_pieces),
        tiles,
        0.5,
    )
    arrived = grid.send(other, "core", 1)
    (own,) = call(
        own_backward,
        [array((blocks,), jnp.float32)],
        [],
        [plan, tiles, low],
        "svv",
        tiles,
        0.25,
    )
    return own, arrived, sides


def edge_weights(prior_weight, left_weight, right_weight, is_first, is_last):
    zero = jnp.zeros_like(prior_weight[0])
    w_left = jnp.stack([jnp.where(is_first, zero, left_weight[0]), jnp.where(is_first, zero, prior_weight[1])])
    w_right = jnp.stack([prior_weight[0], jnp.where(is_last, prior_weight[0], right_weight[1])])
    return w_left[:, None, :], w_right[:, None, :]


def on_device(jac_tiles, tile_pose, tile_point, tile_valid, prior_weight, right_side):
    grid = Grid()
    place = lax.axis_index(BOTH)
    is_first = place == 0
    is_last = place == grid.count - 1
    plan, tiles = make_plan(grid, place, tile_pose, tile_point, tile_valid, jac_tiles)
    before = grid.slot(jnp.maximum(place - 1, 0), place)
    after = grid.slot(jnp.minimum(place + 1, grid.count - 1), place)
    near = jnp.stack([before[0], 2 * before[1], after[0], 2 * after[1]])
    theta = (highest + lowest) / 2.0
    delta = (highest - lowest) / 2.0
    sigma = theta / delta
    ratio = 1.0 / sigma
    right_side = jnp.swapaxes(right_side, 1, 2)
    step = right_side / theta
    solution = jnp.zeros(right_side.shape, jnp.float32)
    residual = right_side
    for turn in range(ITERS):
        if turn > 0:
            new_ratio = 1.0 / (2.0 * sigma - ratio)
            step = new_ratio * ratio * step + 2.0 * new_ratio / delta * residual
            ratio = new_ratio
        solution = solution + step
        low = step.astype(jnp.bfloat16)
        if turn == 0:
            extra = jnp.broadcast_to(prior_weight[:, None, :], (2, 16, prior_weight.shape[1]))
            low = jnp.concatenate([low, extra.astype(jnp.bfloat16)], axis=1)
        pieces, swapped, (plan, near, tiles, result) = gather_field(
            grid, low, plan, near, tiles, jnp.swapaxes(solution, 1, 2)
        )
        own, arrived, sides = gram_product(grid, plan, near, tiles, step.shape[1], pieces, swapped)
        sides = sides.astype(jnp.float32)
        if turn == 0:
            w_left, w_right = edge_weights(prior_weight, *sides[:, :, step.shape[1]], is_first, is_last)
        gram = scatter_sum(grid, own, arrived)
        left, right = sides[:, :, : step.shape[1]]
        right = jnp.where(is_last, step[::-1], right)
        prior = w_left * (step - left) + w_right * (step - right)
        residual = residual - (gram + prior + damping * step)
    return result, jnp.swapaxes(residual, 1, 2)


def solution(mesh):
    return jax.shard_map(
        on_device,
        mesh=mesh,
        in_specs=(
            P(BOTH, None, None),
            P(BOTH),
            P(BOTH),
            P(BOTH),
            P(BOTH, None),
            P(BOTH, None, None),
        ),
        out_specs=(P(BOTH, None, None), P(BOTH, None, None)),
        check_vma=False,
    )
```

```python
import math

import jax
import jax.numpy as jnp
from jax import lax
from jax.experimental import pallas as pl
from jax.experimental.pallas import tpu as pltpu
from jax.sharding import PartitionSpec as P

PT_DEV = 16
ITERS = 3
UNROLL = 8

damping = 0.5
lowest = 0.5
highest = 8.0
BOTH = ("row", "col")


class Grid:
    def __init__(self):
        rows = lax.axis_size("row")
        cols = lax.axis_size("col")
        self.sizes = {"y": rows // 2, "core": 2, "z": cols // 2, "x": 2}
        self.count = rows * cols

    def coords(self, device):
        cols = self.sizes["z"] * 2
        if isinstance(device, int):
            row, col = device // cols, device % cols
            return {"y": row // 2, "core": row % 2, "z": col // 2, "x": col % 2}
        row, col = lax.div(device, cols), lax.rem(device, cols)
        return {"y": lax.div(row, 2), "core": lax.rem(row, 2), "z": lax.div(col, 2), "x": lax.rem(col, 2)}

    def device(self, at):
        row = at["y"] * 2 + at["core"]
        col = at["z"] * 2 + at["x"]
        return row * self.sizes["z"] * 2 + col

    def slot(self, device, home):
        at, base = self.coords(device), self.coords(home)
        away = {a: lax.rem(at[a] - base[a] + n, n) for a, n in self.sizes.items()}
        away["z"] = at["z"] ^ base["z"]
        x, y = away["x"], away["y"]
        if self.sizes["y"] == 2:
            swap = at["core"] == 1
            x, y = jnp.where(swap, y, x), jnp.where(swap, x, y)
        return away["core"], (y * 2 + x) * self.sizes["z"] + away["z"]

    def send(self, block, axes, distance):
        route = []
        for source in range(self.count):
            at = self.coords(source)
            names = axes if isinstance(axes, str) else axes[at["core"]]
            for name in names.split():
                moved = (at[name] + distance) % self.sizes[name]
                at[name] = at[name] ^ distance if name == "z" else moved
            route.append((source, self.device(at)))
        return lax.ppermute(block, BOTH, route)

    def fetch(self, block, axes, distance):
        return self.send(block, axes, -distance)


ONE, TWO, BOTH_AXES = ("x", "y"), ("y", "x"), "x y"


def along_z(grid, block):
    depth = grid.sizes["z"]
    moved = [grid.send(block, "z", r) for r in range(depth - 1, 0, -1)]
    return jnp.concatenate([block] + moved[::-1])


def gather_field(grid, low, *early):
    wide = grid.sizes["y"]
    base = along_z(grid, low)
    if wide == 2:
        corner = grid.send(low, BOTH_AXES, 1)
        base, corner, *early = lax.optimization_barrier((base, corner, *early))
        far = along_z(grid, corner)
        over = [grid.send(base, axes, 1) for axes in (ONE, TWO)]
        base, far = lax.optimization_barrier((base, far))
        pieces = [base, *over, far]
    else:
        base, *early = lax.optimization_barrier((base, *early))
        lines = [base] + [grid.fetch(base, "y", r) for r in range(1, wide)]
        pieces = []
        for line in lines:
            pieces += [line, grid.fetch(line, "x", 1)]
    return pieces, [grid.fetch(piece, "core", 1) for piece in pieces], early


def scatter_sum(grid, own, arrived):
    depth, wide = grid.sizes["z"], grid.sizes["y"]
    total = own + arrived.astype(jnp.float32)
    total = total.reshape((wide, 2, depth, 2) + total.shape[1:])
    order = range(depth - 1, 0, -1)

    def narrow(v):
        return v.astype(jnp.bfloat16)

    def widen(v):
        return v.astype(jnp.float32)

    diagonal = 0.0
    if wide == 2:
        parts = [narrow(total[1, 1, r]) for r in order] + [narrow(total[0, 1]), narrow(total[1, 0])]
        parts = lax.optimization_barrier(parts)
        one, two = grid.send(parts[-2], ONE, 1), grid.send(parts[-1], TWO, 1)
        parts = [grid.send(part, "z", r) for r, part in zip(order, parts)]
        parts = lax.optimization_barrier(parts + [one, two])
        base = total[0, 0] + widen(parts[-2]) + widen(parts[-1])
        corner = narrow(total[1, 1, 0] + sum(widen(part) for part in parts[:-2]))
    else:
        total = total[:, 0] + widen(grid.send(narrow(total[:, 1]), "x", 1))
        base = total[0]
        for r in range(1, wide):
            base = base + widen(grid.send(narrow(total[r]), "y", r))
        corner = None
    parts = [narrow(base[r]) for r in order]
    if corner is not None:
        *parts, corner = lax.optimization_barrier(parts + [corner])
        diagonal = widen(grid.send(corner, BOTH_AXES, 1))
    gram = base[0] + diagonal
    for r, part in zip(order, parts):
        gram = gram + widen(grid.send(part, "z", r))
    return gram


def plan_kernel(near, core, pose, point, valid, jac, out, jac_copy, sem):
    copy = pltpu.make_async_copy(jac, jac_copy, sem)
    copy.start()
    tiles, slots = core.shape[1], out.shape[1]
    row_id = lax.broadcasted_iota(jnp.int32, (tiles, tiles), 0)
    col_id = lax.broadcasted_iota(jnp.int32, (tiles, tiles), 1)
    lane = lax.broadcasted_iota(jnp.int32, (tiles, slots), 1)

    def column(row):
        return jnp.sum(jnp.where(row_id == col_id, row, 0.0), axis=1, keepdims=True)

    def half_up(v, unit):
        whole = v.astype(jnp.int32) + (unit - 1)
        return (whole & ~(unit - 1)).astype(jnp.float32)

    def arrange(key, phase):
        key_col, phase_col = column(key), column(phase)
        same = jnp.where((key_col == key) & (real_col > 0.0) & (real > 0.0), 1.0, 0.0)
        count = jnp.sum(same, axis=0, keepdims=True)
        rank = jnp.sum(jnp.where(row_id < col_id, same, 0.0), axis=0, keepdims=True)
        rank_col = jnp.sum(jnp.where(col_id < row_id, same, 0.0), axis=1, keepdims=True)
        room = jnp.where((rank == 0.0) & (real > 0.0), half_up(count, 2), 0.0)
        start = jnp.sum(jnp.where(key < key_col, room, 0.0), axis=1, keepdims=True)
        first = jnp.sum(jnp.where(phase == 0.0, room, 0.0), axis=1, keepdims=True)
        second = jnp.sum(jnp.where(phase == 0.0, 0.0, room), axis=1, keepdims=True)
        padded = half_up(first, 2 * UNROLL)
        place = start + rank_col + jnp.where(phase_col == 0.0, 0.0, padded - first)
        place = jnp.where(real_col > 0.0, place, -1.0)
        hit = jnp.where(place.astype(jnp.int32) == lane, 1.0, 0.0)
        return hit, padded, padded + half_up(second, 2 * UNROLL)

    def pick(hit, values):
        return jnp.sum(hit * values, axis=0, keepdims=True)

    real = valid[...].astype(jnp.float32)
    real_col = column(real)
    core_row = core[...].astype(jnp.float32)
    pose_row = pose[...].astype(jnp.float32)
    point_row = point[...].astype(jnp.float32)
    pose_col, point_col = column(pose_row), column(point_row)
    tile_col = column(col_id[:1].astype(jnp.float32))
    hit, first, last = arrange(core_row * PT_DEV + point_row, core_row)
    rows = [
        pick(hit, tile_col),
        pick(hit, pose_col),
        pick(hit, jnp.ones_like(tile_col)),
        pick(hit, point_col),
    ]
    ends = [first, last]
    other = 1.0 - core_row
    hit, first, last = arrange(other * 65536.0 + pose_row, other)
    rows += [
        pick(hit, tile_col),
        pick(hit, point_col - PT_DEV) + PT_DEV,
        pick(hit, pose_col),
    ]
    ends += [first, last]
    spot = lane[:1]
    tail = jnp.zeros_like(rows[0])
    for k, end in enumerate(ends):
        tail = jnp.where(spot == k, end * (0.5 / UNROLL), tail)
    for k in range(4):
        tail = jnp.where(spot == NEAR + k, near[k].astype(jnp.float32), tail)
    for k, row in enumerate(rows + [tail]):
        out[k : k + 1] = row.astype(jnp.int32)
    copy.wait()


def make_plan(grid, place, near, tile_pose, tile_point, tile_valid, jac):
    tiles = tile_pose.shape[0]
    core, chip = grid.slot(lax.div(tile_pose, 2), place)
    pose = 2 * chip + lax.rem(tile_pose, 2)
    slots = tiles + max(2 * PT_DEV, min(tiles, grid.count)) + 4 * UNROLL
    slots = -(-slots // 128) * 128
    rows = [v.reshape(1, tiles) for v in (core, pose, tile_point, tile_valid)]
    vmem = pl.BlockSpec(memory_space=pltpu.VMEM)
    return pl.pallas_call(
        plan_kernel,
        out_shape=[
            jax.ShapeDtypeStruct((8, slots), jnp.int32),
            jax.ShapeDtypeStruct(jac.shape, jac.dtype),
        ],
        in_specs=[pl.BlockSpec(memory_space=pltpu.SMEM)] + [vmem] * 4 + [pl.BlockSpec(memory_space=pl.ANY)],
        out_specs=[vmem] * 2,
        scratch_shapes=[pltpu.SemaphoreType.DMA],
        compiler_params=pltpu.CompilerParams(vmem_limit_bytes=jac.size * 2 + 4 * 1024 * 1024),
    )(near, *rows, jac)


NT = (((1,), (1,)), ((), ()))
NN = (((1,), (0,)), ((), ()))
NEAR = 4
F_TILE, F_POSE, F_REAL, F_POINT, B_TILE, B_POINT, B_POSE, ENDS = range(8)


def forward(plan, tiles, field, acc, begin, end):
    def body(i, _):
        for u in range(UNROLL):
            j = 2 * (i * UNROLL + u)
            block = [
                field[plan[F_POSE, j + h], : acc.shape[1]]
                * plan[F_REAL, j + h].astype(jnp.float32).astype(jnp.bfloat16)
                for h in range(2)
            ]
            tile = [tiles[plan[F_TILE, j + h]] for h in range(2)]
            acc[plan[F_POINT, j]] += lax.dot_general(
                jnp.concatenate(block, axis=1),
                jnp.concatenate(tile, axis=1),
                NT,
                preferred_element_type=jnp.float32,
            )
        return 0

    lax.fori_loop(begin, end, body, 0)


def backward(plan, tiles, low, total, begin, end):
    def body(i, _):
        for u in range(UNROLL):
            j = 2 * (i * UNROLL + u)
            block = [low[plan[B_POINT, j + h]] for h in range(2)]
            tile = [tiles[plan[B_TILE, j + h]] for h in range(2)]
            total[plan[B_POSE, j]] += lax.dot_general(
                jnp.concatenate(block, axis=1),
                jnp.concatenate(tile, axis=0),
                NN,
                preferred_element_type=jnp.float32,
            )
        return 0

    lax.fori_loop(begin, end, body, 0)


def assemble(pieces, field):
    start = 0
    for piece in pieces:
        field[start : start + piece.shape[0]] = piece[...]
        start += piece.shape[0]


def near_side(plan, field, sides, side, core):
    spot = NEAR + 2 * side

    @pl.when(plan[ENDS, spot] == core)
    def _():
        sides[side] = field[pl.ds(plan[ENDS, spot + 1], 2)]


def own_forward(plan_in, tiles, *refs):
    pieces, (acc, sides, field, plan, sem) = refs[:-5], refs[-5:]
    copy = pltpu.make_async_copy(plan_in, plan, sem)
    copy.start()
    assemble(pieces, field)
    acc[...] = jnp.zeros_like(acc)
    sides[...] = jnp.zeros_like(sides)
    copy.wait()
    for side in range(2):
        near_side(plan, field, sides, side, 0)
    forward(plan, tiles, field, acc, 0, plan[ENDS, 0])


def other_both(plan_in, tiles, part, own_sides, *refs):
    pieces, (other, low, sides, acc, field, total, plan, sem) = refs[:-8], refs[-8:]
    copy = pltpu.make_async_copy(plan_in, plan, sem)
    copy.start()
    assemble(pieces, field)
    sides[...] = own_sides[...]
    total[...] = jnp.zeros_like(total)
    points = acc.shape[0]
    low[points] = jnp.zeros(low.shape[1:], jnp.bfloat16)
    copy.wait()
    for side in range(2):
        near_side(plan, field, sides, side, 1)
    forward(plan, tiles, field, acc, plan[ENDS, 0], plan[ENDS, 1])
    low[:points] = acc[...].astype(jnp.bfloat16)
    backward(plan, tiles, low, total, 0, plan[ENDS, 2])
    other[...] = total[...].astype(other.dtype)


def own_backward(plan_in, tiles, low, own, plan, sem):
    copy = pltpu.make_async_copy(plan_in, plan, sem)
    copy.start()
    own[...] = jnp.zeros_like(own)
    copy.wait()
    backward(plan, tiles, low, own, plan[ENDS, 2], plan[ENDS, 3])


def call(kernel, outs, scratch, args, kinds, tiles, share, aliases={}):
    place = {
        "a": pl.BlockSpec(memory_space=pl.ANY),
        "v": pl.BlockSpec(memory_space=pltpu.VMEM),
    }
    size = sum(math.prod(v.shape) * v.dtype.itemsize for v in [*outs, *args])
    size += sum(math.prod(v.shape) * jnp.dtype(v.dtype).itemsize for v in scratch)
    scratch = scratch + [pltpu.SMEM(args[0].shape, jnp.int32), pltpu.SemaphoreType.DMA]
    return pl.pallas_call(
        kernel,
        out_shape=outs,
        in_specs=[place[kind] for kind in kinds],
        out_specs=[place["v"]] * len(outs),
        scratch_shapes=scratch,
        input_output_aliases=aliases,
        compiler_params=pltpu.CompilerParams(vmem_limit_bytes=size + 2 * 1024 * 1024),
        cost_estimate=pl.CostEstimate(
            flops=int(share * 4 * tiles.size * 128),
            bytes_accessed=tiles.size * 2,
            transcendentals=0,
        ),
    )(*args)


def gram_product(grid, plan, tiles, rhs, own_pieces, other_pieces):
    rows, params = own_pieces[0].shape[1:]
    points = tiles.shape[1]
    blocks = grid.count

    def array(lead, kind):
        return jax.ShapeDtypeStruct((*lead, rhs, params), kind)

    field = pltpu.VMEM((blocks, rows, params), jnp.bfloat16)
    beside = jax.ShapeDtypeStruct((2, 2, rows, params), jnp.bfloat16)
    acc = jax.ShapeDtypeStruct((PT_DEV, rhs, points), jnp.float32)
    part, own_sides = call(
        own_forward,
        [acc, beside],
        [field],
        [plan, tiles, *own_pieces],
        "av" + "v" * len(own_pieces),
        tiles,
        0.25,
    )
    other, low, sides, _ = call(
        other_both,
        [
            array((blocks,), jnp.bfloat16),
            jax.ShapeDtypeStruct((PT_DEV + 1, rhs, points), jnp.bfloat16),
            beside,
            acc,
        ],
        [
            field,
            pltpu.VMEM((blocks, rhs, params), jnp.float32),
        ],
        [plan, tiles, part, own_sides, *other_pieces],
        "avvv" + "v" * len(other_pieces),
        tiles,
        0.5,
        {2: 3},
    )
    arrived = grid.send(other, "core", 1)
    (own,) = call(
        own_backward,
        [array((blocks,), jnp.float32)],
        [],
        [plan, tiles, low],
        "avv",
        tiles,
        0.25,
    )
    return own, arrived, sides


def edge_weights(prior_weight, left_weight, right_weight, is_first, is_last):
    zero = jnp.zeros_like(prior_weight[0])
    w_left = jnp.stack([jnp.where(is_first, zero, left_weight[0]), jnp.where(is_first, zero, prior_weight[1])])
    w_right = jnp.stack([prior_weight[0], jnp.where(is_last, prior_weight[0], right_weight[1])])
    return w_left[:, None, :], w_right[:, None, :]


def on_device(jac_tiles, tile_pose, tile_point, tile_valid, prior_weight, right_side):
    grid = Grid()
    place = lax.axis_index(BOTH)
    is_first = place == 0
    is_last = place == grid.count - 1
    before = grid.slot(jnp.maximum(place - 1, 0), place)
    after = grid.slot(jnp.minimum(place + 1, grid.count - 1), place)
    near = jnp.stack([before[0], 2 * before[1], after[0], 2 * after[1]])
    plan, tiles = make_plan(grid, place, near, tile_pose, tile_point, tile_valid, jac_tiles)
    theta = (highest + lowest) / 2.0
    delta = (highest - lowest) / 2.0
    sigma = theta / delta
    ratio = 1.0 / sigma
    right_side = jnp.swapaxes(right_side, 1, 2)
    step = right_side / theta
    solution = jnp.zeros(right_side.shape, jnp.float32)
    residual = right_side
    for turn in range(ITERS):
        if turn > 0:
            new_ratio = 1.0 / (2.0 * sigma - ratio)
            step = new_ratio * ratio * step + 2.0 * new_ratio / delta * residual
            ratio = new_ratio
        solution = solution + step
        low = step.astype(jnp.bfloat16)
        if turn == 0:
            extra = jnp.broadcast_to(prior_weight[:, None, :], (2, 16, prior_weight.shape[1]))
            low = jnp.concatenate([low, extra.astype(jnp.bfloat16)], axis=1)
        pieces, swapped, (plan, tiles, result) = gather_field(
            grid, low, plan, tiles, jnp.swapaxes(solution, 1, 2)
        )
        own, arrived, sides = gram_product(grid, plan, tiles, step.shape[1], pieces, swapped)
        sides = sides.astype(jnp.float32)
        if turn == 0:
            w_left, w_right = edge_weights(prior_weight, *sides[:, :, step.shape[1]], is_first, is_last)
        gram = scatter_sum(grid, own, arrived)
        left, right = sides[:, :, : step.shape[1]]
        right = jnp.where(is_last, step[::-1], right)
        prior = w_left * (step - left) + w_right * (step - right)
        residual = residual - (gram + prior + damping * step)
    return result, jnp.swapaxes(residual, 1, 2)


def solution(mesh):
    return jax.shard_map(
        on_device,
        mesh=mesh,
        in_specs=(
            P(BOTH, None, None),
            P(BOTH),
            P(BOTH),
            P(BOTH),
            P(BOTH, None),
            P(BOTH, None, None),
        ),
        out_specs=(P(BOTH, None, None), P(BOTH, None, None)),
        check_vma=False,
    )
```

```python
import math

import jax
import jax.numpy as jnp
from jax import lax
from jax.experimental import pallas as pl
from jax.experimental.pallas import tpu as pltpu
from jax.sharding import PartitionSpec as P

PT_DEV = 16
ITERS = 3
UNROLL = 8
AREAS = 3
NEAR = 2 * AREAS

damping = 0.5
lowest = 0.5
highest = 8.0
BOTH = ("row", "col")


class Grid:
    def __init__(self):
        rows = lax.axis_size("row")
        cols = lax.axis_size("col")
        self.sizes = {"y": rows // 2, "core": 2, "z": cols // 2, "x": 2}
        self.count = rows * cols

    def coords(self, device):
        cols = self.sizes["z"] * 2
        if isinstance(device, int):
            row, col = device // cols, device % cols
            return {"y": row // 2, "core": row % 2, "z": col // 2, "x": col % 2}
        row, col = lax.div(device, cols), lax.rem(device, cols)
        return {"y": lax.div(row, 2), "core": lax.rem(row, 2), "z": lax.div(col, 2), "x": lax.rem(col, 2)}

    def device(self, at):
        row = at["y"] * 2 + at["core"]
        col = at["z"] * 2 + at["x"]
        return row * self.sizes["z"] * 2 + col

    def slot(self, device, home):
        at, base = self.coords(device), self.coords(home)
        away = {a: lax.rem(at[a] - base[a] + n, n) for a, n in self.sizes.items()}
        away["z"] = at["z"] ^ base["z"]
        x, y = away["x"], away["y"]
        if self.sizes["y"] == 2:
            swap = at["core"] == 1
            x, y = jnp.where(swap, y, x), jnp.where(swap, x, y)
        return away["core"], (y * 2 + x) * self.sizes["z"] + away["z"]

    def send(self, block, axes, distance):
        route = []
        for source in range(self.count):
            at = self.coords(source)
            names = axes if isinstance(axes, str) else axes[at["core"]]
            for name in names.split():
                moved = (at[name] + distance) % self.sizes[name]
                at[name] = at[name] ^ distance if name == "z" else moved
            route.append((source, self.device(at)))
        return lax.ppermute(block, BOTH, route)

    def fetch(self, block, axes, distance):
        return self.send(block, axes, -distance)


ONE, TWO, BOTH_AXES = ("x", "y"), ("y", "x"), "x y"


def along_z(grid, block, *beside):
    depth = grid.sizes["z"]
    order = range(1, depth) if beside else range(depth - 1, 0, -1)
    moved = {r: grid.send(block, "z", r) for r in order}
    if beside:
        moved, beside = lax.optimization_barrier((moved, beside[0]))
    return jnp.concatenate([block] + [moved[r] for r in range(1, depth)]), beside


def gather_field(grid, low, plan, tiles, rhs):
    wide = grid.sizes["y"]
    base, _ = along_z(grid, low)
    if wide == 2:
        corner = grid.send(low, BOTH_AXES, 1)
        base, corner, plan, tiles = lax.optimization_barrier((base, corner, plan, tiles))
        sums = base_product(grid, plan, tiles, rhs, base)
        over = [grid.send(base, axes, 1) for axes in (ONE, TWO)]
        far, _ = along_z(grid, corner)
        far, *sums = lax.optimization_barrier((far, *sums))
        held, over[0] = lax.optimization_barrier((base, over[0]))
        pieces = [held, *over, far]
    else:
        base, plan, tiles = lax.optimization_barrier((base, plan, tiles))
        sums = base_product(grid, plan, tiles, rhs, base)
        lines = [base] + [grid.fetch(base, "y", r) for r in range(1, wide)]
        pieces = []
        for line in lines:
            pieces += [line, grid.fetch(line, "x", 1)]
    return sums, pieces, [grid.send(piece, "core", 1) for piece in pieces], plan, tiles


def scatter_sum(grid, plan, tiles, rest, low):
    depth, wide = grid.sizes["z"], grid.sizes["y"]
    rest = rest.reshape((2 * wide - 1, depth, 2) + rest.shape[1:])
    order = range(depth - 1, 0, -1)

    def narrow(v):
        return v.astype(jnp.bfloat16)

    def widen(v):
        return v.astype(jnp.float32)

    diagonal = 0.0
    if wide == 2:
        parts = [narrow(rest[2, r]) for r in order] + [narrow(rest[0]), narrow(rest[1])]
        parts = lax.optimization_barrier(parts)
        one, two = grid.send(parts[-2], ONE, 1), grid.send(parts[-1], TWO, 1)
        parts = [grid.send(part, "z", r) for r, part in zip(order, parts)]
        parts[0], low = lax.optimization_barrier((parts[0], low))
        own_base, other_base = base_return(grid, plan, tiles, low)
        *parts, own_base = lax.optimization_barrier((*parts, one, two, own_base))
        base = base_total(grid, own_base, other_base) + widen(parts[-2]) + widen(parts[-1])
        corner = narrow(rest[2, 0] + sum(widen(part) for part in parts[:-2]))
    else:
        base = base_total(grid, *base_return(grid, plan, tiles, low))
        total = jnp.concatenate([base[None], rest]).reshape((wide, 2) + base.shape)
        total = total[:, 0] + widen(grid.send(narrow(total[:, 1]), "x", 1))
        base = total[0]
        for r in range(1, wide):
            base = base + widen(grid.send(narrow(total[r]), "y", r))
        corner = None
    parts = [narrow(base[r]) for r in order]
    if corner is not None:
        *parts, corner = lax.optimization_barrier(parts + [corner])
        diagonal = widen(grid.send(corner, BOTH_AXES, 1))
    gram = base[0] + diagonal
    for r, part in zip(order, parts):
        gram = gram + widen(grid.send(part, "z", r))
    return gram


def plan_kernel(near, area, pose, back_area, back_pose, point, valid, jac, out, jac_copy, sem):
    copy = pltpu.make_async_copy(jac, jac_copy, sem)
    copy.start()
    tiles, slots = area.shape[1], out.shape[1]
    row_id = lax.broadcasted_iota(jnp.int32, (tiles, tiles), 0)
    col_id = lax.broadcasted_iota(jnp.int32, (tiles, tiles), 1)
    lane = lax.broadcasted_iota(jnp.int32, (tiles, slots), 1)

    def column(row):
        return jnp.sum(jnp.where(row_id == col_id, row, 0.0), axis=1, keepdims=True)

    def half_up(v, unit):
        whole = v.astype(jnp.int32) + (unit - 1)
        return (whole & ~(unit - 1)).astype(jnp.float32)

    def arrange(key, phase):
        key_col, phase_col = column(key), column(phase)
        same = jnp.where((key_col == key) & (real_col > 0.0) & (real > 0.0), 1.0, 0.0)
        count = jnp.sum(same, axis=0, keepdims=True)
        rank = jnp.sum(jnp.where(row_id < col_id, same, 0.0), axis=0, keepdims=True)
        rank_col = jnp.sum(jnp.where(col_id < row_id, same, 0.0), axis=1, keepdims=True)
        room = jnp.where((rank == 0.0) & (real > 0.0), half_up(count, 2), 0.0)
        place = jnp.sum(jnp.where(key < key_col, room, 0.0), axis=1, keepdims=True) + rank_col
        end, gap, bounds = 0.0, 0.0, []
        for k in range(AREAS):
            used = jnp.sum(jnp.where(phase == k, room, 0.0), axis=1, keepdims=True)
            place = place + jnp.where(phase_col == k, gap, 0.0)
            padded = half_up(used, 2 * UNROLL)
            end, gap = end + padded, gap + padded - used
            bounds.append(end)
        place = jnp.where(real_col > 0.0, place, -1.0)
        return jnp.where(place.astype(jnp.int32) == lane, 1.0, 0.0), bounds

    def pick(hit, values):
        return jnp.sum(hit * values, axis=0, keepdims=True)

    real = valid[...].astype(jnp.float32)
    real_col = column(real)
    area_row = area[...].astype(jnp.float32)
    pose_row = pose[...].astype(jnp.float32)
    point_row = point[...].astype(jnp.float32)
    pose_col, point_col = column(pose_row), column(point_row)
    tile_col = column(col_id[:1].astype(jnp.float32))
    hit, ends = arrange(area_row * PT_DEV + point_row, area_row)
    rows = [
        pick(hit, tile_col),
        pick(hit, pose_col),
        pick(hit, jnp.ones_like(tile_col)),
        pick(hit, point_col),
    ]
    area_row = back_area[...].astype(jnp.float32)
    pose_row = back_pose[...].astype(jnp.float32)
    hit, bounds = arrange(area_row * 65536.0 + pose_row, area_row)
    rows += [
        pick(hit, tile_col),
        pick(hit, point_col - PT_DEV) + PT_DEV,
        pick(hit, column(pose_row)),
    ]
    ends += bounds
    spot = lane[:1]
    tail = jnp.zeros_like(rows[0])
    for k, end in enumerate(ends):
        tail = jnp.where(spot == k, end * (0.5 / UNROLL), tail)
    for k in range(4):
        tail = jnp.where(spot == NEAR + k, near[k].astype(jnp.float32), tail)
    for k, row in enumerate(rows + [tail]):
        out[k : k + 1] = row.astype(jnp.int32)
    copy.wait()


def spots(grid, pose, place):
    core, chip = grid.slot(lax.div(pose, 2), place)
    spot = 2 * chip + lax.rem(pose, 2)
    plane = 2 * grid.sizes["z"]
    in_base = spot < plane
    own_rest = jnp.logical_and(core == 0, jnp.logical_not(in_base))
    out = jnp.where(core == 1, 2, jnp.where(in_base, 0, 1)), spot - jnp.where(own_rest, plane, 0)
    back = jnp.where(in_base, 2, 1 - core), spot + jnp.where(in_base, core * plane, -plane)
    return out, back


def make_plan(grid, place, near, tile_pose, tile_point, tile_valid, jac):
    tiles = tile_pose.shape[0]
    (area, pose), (back_area, back_pose) = spots(grid, tile_pose, place)
    slots = tiles + max(AREAS * PT_DEV, min(tiles, grid.count)) + 2 * AREAS * UNROLL
    slots = -(-slots // 128) * 128
    rows = [v.reshape(1, tiles) for v in (area, pose, back_area, back_pose, tile_point, tile_valid)]
    vmem = pl.BlockSpec(memory_space=pltpu.VMEM)
    return pl.pallas_call(
        plan_kernel,
        out_shape=[
            jax.ShapeDtypeStruct((8, slots), jnp.int32),
            jax.ShapeDtypeStruct(jac.shape, jac.dtype),
        ],
        in_specs=[pl.BlockSpec(memory_space=pltpu.SMEM)] + [vmem] * 6 + [pl.BlockSpec(memory_space=pl.ANY)],
        out_specs=[vmem] * 2,
        scratch_shapes=[pltpu.SemaphoreType.DMA],
        compiler_params=pltpu.CompilerParams(vmem_limit_bytes=jac.size * 2 + 4 * 1024 * 1024),
    )(near, *rows, jac)


NT = (((1,), (1,)), ((), ()))
NN = (((1,), (0,)), ((), ()))
F_TILE, F_POSE, F_REAL, F_POINT, B_TILE, B_POINT, B_POSE, ENDS = range(8)


def forward(plan, tiles, field, acc, begin, end):
    def body(i, _):
        for u in range(UNROLL):
            j = 2 * (i * UNROLL + u)
            block = [
                field[plan[F_POSE, j + h], : acc.shape[1]]
                * plan[F_REAL, j + h].astype(jnp.float32).astype(jnp.bfloat16)
                for h in range(2)
            ]
            tile = [tiles[plan[F_TILE, j + h]] for h in range(2)]
            acc[plan[F_POINT, j]] += lax.dot_general(
                jnp.concatenate(block, axis=1),
                jnp.concatenate(tile, axis=1),
                NT,
                preferred_element_type=jnp.float32,
            )
        return 0

    lax.fori_loop(begin, end, body, 0)


def backward(plan, tiles, low, total, begin, end):
    def body(i, _):
        for u in range(UNROLL):
            j = 2 * (i * UNROLL + u)
            block = [low[plan[B_POINT, j + h]] for h in range(2)]
            tile = [tiles[plan[B_TILE, j + h]] for h in range(2)]
            total[plan[B_POSE, j]] += lax.dot_general(
                jnp.concatenate(block, axis=1),
                jnp.concatenate(tile, axis=0),
                NN,
                preferred_element_type=jnp.float32,
            )
        return 0

    lax.fori_loop(begin, end, body, 0)


def assemble(pieces, field):
    start = 0
    for piece in pieces:
        field[start : start + piece.shape[0]] = piece[...]
        start += piece.shape[0]


def near_side(plan, field, sides, area):
    for side in range(2):
        spot = NEAR + 2 * side

        @pl.when(plan[ENDS, spot] == area)
        def _():
            sides[side] = field[pl.ds(plan[ENDS, spot + 1], 2)]


def base_forward(plan_in, tiles, field, acc, sides, plan, sem):
    copy = pltpu.make_async_copy(plan_in, plan, sem)
    copy.start()
    acc[...] = jnp.zeros_like(acc)
    sides[...] = jnp.zeros_like(sides)
    copy.wait()
    near_side(plan, field, sides, 0)
    forward(plan, tiles, field, acc, 0, plan[ENDS, 0])


def own_forward(plan_in, tiles, part, sides_in, *refs):
    pieces, (acc, sides, field, plan, sem) = refs[:-5], refs[-5:]
    copy = pltpu.make_async_copy(plan_in, plan, sem)
    copy.start()
    assemble(pieces, field)
    copy.wait()
    near_side(plan, field, sides, 1)
    forward(plan, tiles, field, acc, plan[ENDS, 0], plan[ENDS, 1])


def other_both(plan_in, tiles, part, sides_in, *refs):
    pieces, (acc, sides, other, low, field, total, plan, sem) = refs[:-8], refs[-8:]
    copy = pltpu.make_async_copy(plan_in, plan, sem)
    copy.start()
    assemble(pieces, field)
    total[...] = jnp.zeros_like(total)
    points = acc.shape[0]
    low[points] = jnp.zeros(low.shape[1:], jnp.bfloat16)
    copy.wait()
    near_side(plan, field, sides, 2)
    forward(plan, tiles, field, acc, plan[ENDS, 1], plan[ENDS, 2])
    low[:points] = acc[...].astype(jnp.bfloat16)
    backward(plan, tiles, low, total, 0, plan[ENDS, AREAS])
    other[...] = total[...].astype(other.dtype)


def own_backward(plan_in, tiles, low, own, plan, sem):
    copy = pltpu.make_async_copy(plan_in, plan, sem)
    copy.start()
    own[...] = jnp.zeros_like(own)
    copy.wait()
    backward(plan, tiles, low, own, plan[ENDS, AREAS], plan[ENDS, AREAS + 1])


def base_backward(plan_in, tiles, low, own, other, total, plan, sem):
    copy = pltpu.make_async_copy(plan_in, plan, sem)
    copy.start()
    total[...] = jnp.zeros_like(total)
    copy.wait()
    backward(plan, tiles, low, total, plan[ENDS, AREAS + 1], plan[ENDS, AREAS + 2])
    plane = own.shape[0]
    own[...] = total[:plane]
    other[...] = total[plane:].astype(other.dtype)


def call(kernel, outs, scratch, args, kinds, tiles, share, aliases={}):
    place = {
        "a": pl.BlockSpec(memory_space=pl.ANY),
        "v": pl.BlockSpec(memory_space=pltpu.VMEM),
    }
    size = sum(math.prod(v.shape) * v.dtype.itemsize for v in [*outs, *args])
    size += sum(math.prod(v.shape) * jnp.dtype(v.dtype).itemsize for v in scratch)
    scratch = scratch + [pltpu.SMEM(args[0].shape, jnp.int32), pltpu.SemaphoreType.DMA]
    return pl.pallas_call(
        kernel,
        out_shape=outs,
        in_specs=[place[kind] for kind in kinds],
        out_specs=[place["v"]] * len(outs),
        scratch_shapes=scratch,
        input_output_aliases=aliases,
        compiler_params=pltpu.CompilerParams(vmem_limit_bytes=size + 2 * 1024 * 1024),
        cost_estimate=pl.CostEstimate(
            flops=int(share * 4 * tiles.size * 128),
            bytes_accessed=tiles.size * 2,
            transcendentals=0,
        ),
    )(*args)


def array(lead, rows, params, kind):
    return jax.ShapeDtypeStruct((lead, rows, params), kind)


def field(lead, pieces):
    return pltpu.VMEM((lead, *pieces[0].shape[1:]), jnp.bfloat16)


def base_product(grid, plan, tiles, rhs, base):
    return call(
        base_forward,
        [
            jax.ShapeDtypeStruct((PT_DEV, rhs, tiles.shape[1]), jnp.float32),
            jax.ShapeDtypeStruct((2, 2, *base.shape[1:]), jnp.bfloat16),
        ],
        [],
        [plan, tiles, base],
        "avv",
        tiles,
        0.125,
    )


def rest_product(grid, plan, tiles, rhs, sums, own_pieces, other_pieces):
    params = tiles.shape[2]
    rest = grid.count - 2 * grid.sizes["z"]
    shapes = [jax.ShapeDtypeStruct(v.shape, v.dtype) for v in sums]
    sums = call(
        own_forward,
        shapes,
        [field(rest, own_pieces)],
        [plan, tiles, *sums, *own_pieces[1:]],
        "avvv" + "v" * len(own_pieces[1:]),
        tiles,
        0.1875,
        {2: 0, 3: 1},
    )
    _, sides, other, low = call(
        other_both,
        [
            *shapes,
            array(rest, rhs, params, jnp.bfloat16),
            array(PT_DEV + 1, rhs, tiles.shape[1], jnp.bfloat16),
        ],
        [field(grid.count, other_pieces), pltpu.VMEM((rest, rhs, params), jnp.float32)],
        [plan, tiles, *sums, *other_pieces],
        "avvv" + "v" * len(other_pieces),
        tiles,
        0.375,
        {2: 0, 3: 1},
    )
    arrived = grid.send(other, "core", 1)
    (own,) = call(
        own_backward,
        [array(rest, rhs, params, jnp.float32)],
        [],
        [plan, tiles, low],
        "avv",
        tiles,
        0.1875,
    )
    return own + arrived.astype(jnp.float32), low, sides


def base_return(grid, plan, tiles, low):
    rhs, params = low.shape[1], tiles.shape[2]
    plane = 2 * grid.sizes["z"]
    return call(
        base_backward,
        [array(plane, rhs, params, jnp.float32), array(plane, rhs, params, jnp.bfloat16)],
        [pltpu.VMEM((2 * plane, rhs, params), jnp.float32)],
        [plan, tiles, low],
        "avv",
        tiles,
        0.125,
    )


def base_total(grid, own, other):
    base = own + grid.send(other, "core", 1).astype(jnp.float32)
    return base.reshape((grid.sizes["z"], 2) + base.shape[1:])


def edge_weights(prior_weight, left_weight, right_weight, is_first, is_last):
    zero = jnp.zeros_like(prior_weight[0])
    w_left = jnp.stack([jnp.where(is_first, zero, left_weight[0]), jnp.where(is_first, zero, prior_weight[1])])
    w_right = jnp.stack([prior_weight[0], jnp.where(is_last, prior_weight[0], right_weight[1])])
    return w_left[:, None, :], w_right[:, None, :]


def on_device(jac_tiles, tile_pose, tile_point, tile_valid, prior_weight, right_side):
    grid = Grid()
    place = lax.axis_index(BOTH)
    is_first = place == 0
    is_last = place == grid.count - 1
    before, _ = spots(grid, 2 * jnp.maximum(place - 1, 0), place)
    after, _ = spots(grid, 2 * jnp.minimum(place + 1, grid.count - 1), place)
    near = jnp.stack([*before, *after])
    plan, tiles = make_plan(grid, place, near, tile_pose, tile_point, tile_valid, jac_tiles)
    theta = (highest + lowest) / 2.0
    delta = (highest - lowest) / 2.0
    sigma = theta / delta
    ratio = 1.0 / sigma
    right_side = jnp.swapaxes(right_side, 1, 2)
    step = right_side / theta
    solution = jnp.zeros(right_side.shape, jnp.float32)
    residual = right_side
    for turn in range(ITERS):
        if turn > 0:
            new_ratio = 1.0 / (2.0 * sigma - ratio)
            step = new_ratio * ratio * step + 2.0 * new_ratio / delta * residual
            ratio = new_ratio
        solution = solution + step
        low = step.astype(jnp.bfloat16)
        if turn == 0:
            extra = jnp.broadcast_to(prior_weight[:, None, :], (2, 16, prior_weight.shape[1]))
            low = jnp.concatenate([low, extra.astype(jnp.bfloat16)], axis=1)
        result = jnp.swapaxes(solution, 1, 2)
        rhs = step.shape[1]
        sums, pieces, swapped, plan, tiles = gather_field(grid, low, plan, tiles, rhs)
        rest, point_sums, sides = rest_product(grid, plan, tiles, rhs, sums, pieces, swapped)
        gram = scatter_sum(grid, plan, tiles, rest, point_sums)
        sides = sides.astype(jnp.float32)
        if turn == 0:
            w_left, w_right = edge_weights(prior_weight, *sides[:, :, step.shape[1]], is_first, is_last)
        left, right = sides[:, :, : step.shape[1]]
        right = jnp.where(is_last, step[::-1], right)
        prior = w_left * (step - left) + w_right * (step - right)
        residual = residual - (gram + prior + damping * step)
    return result, jnp.swapaxes(residual, 1, 2)


def solution(mesh):
    return jax.shard_map(
        on_device,
        mesh=mesh,
        in_specs=(
            P(BOTH, None, None),
            P(BOTH),
            P(BOTH),
            P(BOTH),
            P(BOTH, None),
            P(BOTH, None, None),
        ),
        out_specs=(P(BOTH, None, None), P(BOTH, None, None)),
        check_vma=False,
    )
```

```python
import functools
import math

import jax
import jax.numpy as jnp
from jax import lax
from jax.experimental import pallas as pl
from jax.experimental.pallas import tpu as pltpu
from jax.sharding import PartitionSpec as P

PT_DEV = 16
ITERS = 3
CORES = 2
UNROLL = 8
AREAS = 2
NEAR = 2 * AREAS

damping = 0.5
lowest = 0.5
highest = 8.0
BOTH = ("row", "col")
ONE, TWO, BOTH_AXES = ("x", "y"), ("y", "x"), "x y"


class Grid:
    def __init__(self):
        rows = lax.axis_size("row")
        cols = lax.axis_size("col")
        self.sizes = {"y": rows // CORES, "core": CORES, "z": cols // 2, "x": 2}
        self.count = rows * cols
        self.plane = self.sizes["z"] * CORES * 2

    def coords(self, device):
        cols = self.sizes["z"] * 2
        if isinstance(device, int):
            row, col = device // cols, device % cols
            return {"y": row // 2, "core": row % 2, "z": col // 2, "x": col % 2}
        row, col = lax.div(device, cols), lax.rem(device, cols)
        return {"y": lax.div(row, 2), "core": lax.rem(row, 2), "z": lax.div(col, 2), "x": lax.rem(col, 2)}

    def device(self, at):
        row = at["y"] * 2 + at["core"]
        col = at["z"] * 2 + at["x"]
        return row * self.sizes["z"] * 2 + col

    def spot(self, pose, home):
        at, base = self.coords(lax.div(pose, 2)), self.coords(home)
        away = {a: lax.rem(at[a] - base[a] + n, n) for a, n in self.sizes.items()}
        x, y, z = away["x"], away["y"], at["z"] ^ base["z"]
        if self.sizes["y"] == 2:
            swap = base["core"] == 1
            x, y = jnp.where(swap, y, x), jnp.where(swap, x, y)
        chip = (y * 2 + x) * self.sizes["z"] + z
        spot = (chip * CORES + at["core"]) * 2 + lax.rem(pose, 2)
        area = jnp.where(spot < self.plane, 0, 1)
        return area, spot - area * self.plane

    def send(self, block, axes, distance):
        route = []
        for source in range(self.count):
            at = self.coords(source)
            names = axes if isinstance(axes, str) else axes[at["core"]]
            for name in names.split():
                moved = (at[name] + distance) % self.sizes[name]
                at[name] = at[name] ^ distance if name == "z" else moved
            route.append((source, self.device(at)))
        return lax.ppermute(block, BOTH, route)

    def fetch(self, block, axes, distance):
        return self.send(block, axes, -distance)

    def swap(self, block):
        return self.send(block, "core", 1)


def along_z(grid, block):
    depth = grid.sizes["z"]
    moved = [grid.send(block, "z", r) for r in range(depth - 1, 0, -1)]
    return jnp.concatenate([block] + moved[::-1])


def gather_field(grid, low, plan, load, *early):
    wide = grid.sizes["y"]
    base = along_z(grid, low)
    if wide == 2:
        corner = grid.send(low, BOTH_AXES, 1)
        base, corner, plan, *early = lax.optimization_barrier((base, corner, plan, *early))
        tiles = load()
        sums = base_product(plan, tiles, base)
        over = [grid.send(base, axes, 1) for axes in (ONE, TWO)]
        far = along_z(grid, corner)
        far, *sums = lax.optimization_barrier((far, *sums))
        pieces = [*over, far]
    else:
        base, plan, *early = lax.optimization_barrier((base, plan, *early))
        tiles = load()
        sums = base_product(plan, tiles, base)
        lines = [base] + [grid.fetch(base, "y", r) for r in range(1, wide)]
        pieces = []
        for line in lines:
            pieces += [line, grid.fetch(line, "x", 1)]
        pieces = pieces[1:]
    return sums, pieces, plan, tiles, early


def scatter_sum(grid, plan, tiles, rest, low):
    depth, wide = grid.sizes["z"], grid.sizes["y"]
    order = range(depth - 1, 0, -1)
    shape = (depth, 2 * CORES, low.shape[1], tiles.shape[2])

    def narrow(v):
        return v.astype(jnp.bfloat16)

    def widen(v):
        return v.astype(jnp.float32)

    diagonal = 0.0
    if wide == 2:
        one, two, here, *parts = rest
        one, two, *parts = lax.optimization_barrier((one, two, *parts))
        one, two = grid.send(one, ONE, 1), grid.send(two, TWO, 1)
        parts = [grid.send(parts[r - 1], "z", r) for r in order]
        parts[0], low = lax.optimization_barrier((parts[0], low))
        base = base_return(grid, plan, tiles, low)
        *parts, one, two, base = lax.optimization_barrier((*parts, one, two, base))
        base = (base + widen(one) + widen(two)).reshape(shape)
        corner = narrow(here + sum(widen(part) for part in parts))
    else:
        total = jnp.concatenate([base_return(grid, plan, tiles, low), rest[0]])
        total = total.reshape((wide, 2) + shape)
        total = total[:, 0] + widen(grid.send(narrow(total[:, 1]), "x", 1))
        base = total[0]
        for r in range(1, wide):
            base = base + widen(grid.send(narrow(total[r]), "y", r))
        corner = None
    parts = [narrow(base[r]) for r in order]
    if corner is not None:
        *parts, corner = lax.optimization_barrier((*parts, corner))
        diagonal = widen(grid.send(corner, BOTH_AXES, 1))
    gram = base[0] + diagonal
    for r, part in zip(order, parts):
        gram = gram + widen(grid.send(part, "z", r))
    return gram


def plan_kernel(near, area, pose, point, valid, out):
    tiles, slots = area.shape[1], out.shape[1]
    row_id = lax.broadcasted_iota(jnp.int32, (tiles, tiles), 0)
    col_id = lax.broadcasted_iota(jnp.int32, (tiles, tiles), 1)
    lane = lax.broadcasted_iota(jnp.int32, (tiles, slots), 1)

    def column(row):
        return jnp.sum(jnp.where(row_id == col_id, row, 0.0), axis=1, keepdims=True)

    def half_up(v, unit):
        whole = v.astype(jnp.int32) + (unit - 1)
        return (whole & ~(unit - 1)).astype(jnp.float32)

    def arrange(key, phase):
        key_col, phase_col = column(key), column(phase)
        same = jnp.where((key_col == key) & (real_col > 0.0) & (real > 0.0), 1.0, 0.0)
        count = jnp.sum(same, axis=0, keepdims=True)
        rank = jnp.sum(jnp.where(row_id < col_id, same, 0.0), axis=0, keepdims=True)
        rank_col = jnp.sum(jnp.where(col_id < row_id, same, 0.0), axis=1, keepdims=True)
        room = jnp.where((rank == 0.0) & (real > 0.0), half_up(count, 2), 0.0)
        place = jnp.sum(jnp.where(key < key_col, room, 0.0), axis=1, keepdims=True) + rank_col
        end, gap, bounds = 0.0, 0.0, []
        for k in range(AREAS):
            used = jnp.sum(jnp.where(phase == k, room, 0.0), axis=1, keepdims=True)
            place = place + jnp.where(phase_col == k, gap, 0.0)
            padded = half_up(used, 2 * UNROLL)
            end, gap = end + padded, gap + padded - used
            bounds.append(end)
        place = jnp.where(real_col > 0.0, place, -1.0)
        return jnp.where(place.astype(jnp.int32) == lane, 1.0, 0.0), bounds

    def pick(hit, values):
        return jnp.sum(hit * values, axis=0, keepdims=True)

    real = valid[...].astype(jnp.float32)
    real_col = column(real)
    area_row = area[...].astype(jnp.float32)
    pose_row = pose[...].astype(jnp.float32)
    point_row = point[...].astype(jnp.float32)
    pose_col, point_col = column(pose_row), column(point_row)
    tile_col = column(col_id[:1].astype(jnp.float32))
    points = CORES * PT_DEV
    hit, ends = arrange(area_row * points + point_row, area_row)
    rows = [
        pick(hit, tile_col),
        pick(hit, pose_col),
        pick(hit, jnp.ones_like(tile_col)),
        pick(hit, point_col),
    ]
    turned = AREAS - 1.0 - area_row
    hit, bounds = arrange(turned * 65536.0 + pose_row, turned)
    rows += [
        pick(hit, tile_col),
        pick(hit, point_col - points) + points,
        pick(hit, pose_col),
    ]
    ends += bounds
    spot = lane[:1]
    tail = jnp.zeros_like(rows[0])
    for k, end in enumerate(ends):
        tail = jnp.where(spot == k, end * (0.5 / UNROLL), tail)
    for k in range(near.shape[0]):
        tail = jnp.where(spot == NEAR + k, near[k].astype(jnp.float32), tail)
    for k, row in enumerate(rows + [tail]):
        out[k : k + 1] = row.astype(jnp.int32)


def make_plan(grid, place, near, indices):
    pose, point, valid = indices
    tiles = pose.shape[0]
    area, pose = grid.spot(pose, place)
    slots = tiles + max(AREAS * CORES * PT_DEV, min(tiles, 2 * grid.count)) + 2 * AREAS * UNROLL
    slots = -(-slots // 128) * 128
    rows = [v.reshape(1, tiles) for v in (area, pose, point, valid)]
    vmem = pl.BlockSpec(memory_space=pltpu.VMEM)
    return pl.pallas_call(
        plan_kernel,
        out_shape=jax.ShapeDtypeStruct((8, slots), jnp.int32),
        in_specs=[pl.BlockSpec(memory_space=pltpu.SMEM)] + [vmem] * 4,
        out_specs=vmem,
    )(near, *rows)


def join_kernel(first, second, out, sems):
    half = first.shape[0]
    copies = [
        pltpu.make_async_copy(first, out.at[pl.ds(0, half)], sems.at[0]),
        pltpu.make_async_copy(second, out.at[pl.ds(half, half)], sems.at[1]),
    ]
    for copy in copies:
        copy.start()
    for copy in copies:
        copy.wait()


def join_tiles(first, second):
    shape = (2 * first.shape[0], *first.shape[1:])
    return pl.pallas_call(
        join_kernel,
        out_shape=jax.ShapeDtypeStruct(shape, first.dtype),
        in_specs=[pl.BlockSpec(memory_space=pl.ANY)] * 2,
        out_specs=pl.BlockSpec(memory_space=pltpu.VMEM),
        scratch_shapes=[pltpu.SemaphoreType.DMA((2,))],
        compiler_params=pltpu.CompilerParams(vmem_limit_bytes=2 * math.prod(shape) + 4 * 1024 * 1024),
    )(first, second)


NT = (((1,), (1,)), ((), ()))
NN = (((1,), (0,)), ((), ()))
F_TILE, F_POSE, F_REAL, F_POINT, B_TILE, B_POINT, B_POSE, ENDS = range(8)


def forward(plan, tiles, field, acc, begin, end):
    def body(i, _):
        for u in range(UNROLL):
            j = 2 * (i * UNROLL + u)
            block = [
                field[plan[F_POSE, j + h], : acc.shape[1]]
                * plan[F_REAL, j + h].astype(jnp.float32).astype(jnp.bfloat16)
                for h in range(2)
            ]
            tile = [tiles[plan[F_TILE, j + h]] for h in range(2)]
            acc[plan[F_POINT, j]] += lax.dot_general(
                jnp.concatenate(block, axis=1),
                jnp.concatenate(tile, axis=1),
                NT,
                preferred_element_type=jnp.float32,
            )
        return 0

    lax.fori_loop(begin, end, body, 0)


def backward(plan, tiles, low, total, begin, end):
    def body(i, _):
        for u in range(UNROLL):
            j = 2 * (i * UNROLL + u)
            block = [low[plan[B_POINT, j + h]] for h in range(2)]
            tile = [tiles[plan[B_TILE, j + h]] for h in range(2)]
            total[plan[B_POSE, j]] += lax.dot_general(
                jnp.concatenate(block, axis=1),
                jnp.concatenate(tile, axis=0),
                NN,
                preferred_element_type=jnp.float32,
            )
        return 0

    lax.fori_loop(begin, end, body, 0)


def assemble(pieces, field):
    start = 0
    for piece in pieces:
        field[start : start + piece.shape[0]] = piece[...]
        start += piece.shape[0]


def near_side(plan, field, sides, area):
    for side in range(sides.shape[0]):
        spot = NEAR + 2 * side

        @pl.when(plan[ENDS, spot] == area)
        def _():
            sides[side] = field[pl.ds(plan[ENDS, spot + 1], 2)]


def base_forward(plan_in, tiles, field, acc, sides, plan, sem):
    copy = pltpu.make_async_copy(plan_in, plan, sem)
    copy.start()
    acc[...] = jnp.zeros_like(acc)
    sides[...] = jnp.zeros_like(sides)
    copy.wait()
    near_side(plan, field, sides, 0)
    forward(plan, tiles, field, acc, 0, plan[ENDS, 0])


def rest_both(cuts, plan_in, tiles, part, sides_in, *refs):
    pieces, refs = refs[: -len(cuts) - 7], refs[-len(cuts) - 7 :]
    (acc, sides, low), outs, (field, total, plan, sem) = refs[:3], refs[3:-4], refs[-4:]
    copy = pltpu.make_async_copy(plan_in, plan, sem)
    copy.start()
    assemble(pieces, field)
    total[...] = jnp.zeros_like(total)
    points = acc.shape[0]
    low[points] = jnp.zeros(low.shape[1:], jnp.bfloat16)
    copy.wait()
    near_side(plan, field, sides, 1)
    forward(plan, tiles, field, acc, plan[ENDS, 0], plan[ENDS, 1])
    low[:points] = acc[...].astype(jnp.bfloat16)
    backward(plan, tiles, low, total, 0, plan[ENDS, AREAS])
    start = 0
    for size, out in zip(cuts, outs):
        out[...] = total[start : start + size].astype(out.dtype)
        start += size


def base_backward(plan_in, tiles, low, base, plan, sem):
    copy = pltpu.make_async_copy(plan_in, plan, sem)
    copy.start()
    base[...] = jnp.zeros_like(base)
    copy.wait()
    backward(plan, tiles, low, base, plan[ENDS, AREAS], plan[ENDS, AREAS + 1])


def call(kernel, outs, scratch, args, kinds, tiles, share, aliases={}):
    place = {
        "a": pl.BlockSpec(memory_space=pl.ANY),
        "v": pl.BlockSpec(memory_space=pltpu.VMEM),
    }
    size = sum(math.prod(v.shape) * v.dtype.itemsize for v in [*outs, *args])
    size += sum(math.prod(v.shape) * jnp.dtype(v.dtype).itemsize for v in scratch)
    scratch = scratch + [pltpu.SMEM(args[0].shape, jnp.int32), pltpu.SemaphoreType.DMA]
    return pl.pallas_call(
        kernel,
        out_shape=outs,
        in_specs=[place[kind] for kind in kinds],
        out_specs=[place["v"]] * len(outs),
        scratch_shapes=scratch,
        input_output_aliases=aliases,
        compiler_params=pltpu.CompilerParams(vmem_limit_bytes=size + 2 * 1024 * 1024),
        cost_estimate=pl.CostEstimate(
            flops=int(share * 4 * tiles.size * 128),
            bytes_accessed=tiles.size * 2,
            transcendentals=0,
        ),
    )(*args)


def array(lead, like, kind):
    return jax.ShapeDtypeStruct((lead, *like[1:]), kind)


def base_product(plan, tiles, base):
    rows = tiles.shape[1] // CORES
    acc = (0, rows, tiles.shape[1])
    return call(
        base_forward,
        [
            array(CORES * PT_DEV, acc, jnp.float32),
            jax.ShapeDtypeStruct((2 * CORES, 2, *base.shape[1:]), jnp.bfloat16),
        ],
        [],
        [plan, tiles, base],
        "avv",
        tiles,
        0.125,
    )


def rest_product(grid, plan, tiles, sums, pieces):
    plane = grid.plane
    rest = 2 * grid.count - plane
    if grid.sizes["y"] == 2:
        group = 2 * CORES
        cuts = [plane, plane, group] + [group] * (grid.sizes["z"] - 1)
        kinds = [jnp.bfloat16, jnp.bfloat16, jnp.float32] + [jnp.bfloat16] * (grid.sizes["z"] - 1)
    else:
        cuts, kinds = [rest], [jnp.float32]
    rows, points = sums[0].shape[1:]
    like = (0, rows, tiles.shape[2])
    _, sides, low, *outs = call(
        functools.partial(rest_both, cuts),
        [
            *[jax.ShapeDtypeStruct(v.shape, v.dtype) for v in sums],
            array(CORES * PT_DEV + 1, (0, rows, points), jnp.bfloat16),
            *[array(cut, like, kind) for cut, kind in zip(cuts, kinds)],
        ],
        [pltpu.VMEM((rest, *pieces[0].shape[1:]), jnp.bfloat16), pltpu.VMEM((rest, *like[1:]), jnp.float32)],
        [plan, tiles, *sums, *pieces],
        "avvv" + "v" * len(pieces),
        tiles,
        0.75,
        {2: 0, 3: 1},
    )
    return outs, low, sides


def base_return(grid, plan, tiles, low):
    (base,) = call(
        base_backward,
        [array(grid.plane, (0, low.shape[1], tiles.shape[2]), jnp.float32)],
        [],
        [plan, tiles, low],
        "avv",
        tiles,
        0.125,
    )
    return base


def in_order(core, mine, theirs, axis):
    low, high = jnp.where(core == 0, mine, theirs), jnp.where(core == 0, theirs, mine)
    return jnp.concatenate([low, high], axis=axis)


def on_device(jac_tiles, tile_pose, tile_point, tile_valid, prior_weight, right_side):
    grid = Grid()
    place = lax.axis_index(BOTH)
    at = grid.coords(place)
    core = at["core"]
    homes = [grid.device(at | {"core": c}) for c in range(CORES)]
    params, rhs = right_side.shape[1:]
    rows = rhs // CORES

    def half(v, which):
        return lax.dynamic_slice_in_dim(v, which * rows, rows, 1)

    def whole(v):
        v = v.reshape((CORES, 2) + v.shape[1:])
        mine = lax.dynamic_index_in_dim(v, core, 0, keepdims=False)
        theirs = grid.swap(lax.dynamic_index_in_dim(v, 1 - core, 0, keepdims=False))
        return jnp.swapaxes(in_order(core, mine, theirs, 1), 1, 2)

    turned = jnp.swapaxes(right_side, 1, 2)
    extra = jnp.broadcast_to(prior_weight[:, None, :], (2, 8, params))
    mine = jnp.concatenate([half(turned, core), extra], axis=1)
    theirs = grid.swap(jnp.concatenate([half(turned, 1 - core), extra], axis=1))
    both = in_order(core, mine, theirs, 0)
    right_side, weights = both[:, :rows], both[:, rows]

    indices = jnp.stack([tile_pose, tile_point, tile_valid])
    other_tiles = grid.swap(jac_tiles)
    shift = jnp.array([[0], [PT_DEV], [0]], jnp.int32)
    indices = jnp.concatenate([indices, grid.swap(indices) + shift], axis=1)
    near = []
    for home in homes:
        near += grid.spot(2 * jnp.maximum(home - 1, 0), place)
        near += grid.spot(2 * jnp.minimum(home + 1, grid.count - 1), place)
    plan = make_plan(grid, place, jnp.stack(near), indices)
    tiles = None

    def load():
        return join_tiles(jac_tiles, other_tiles) if tiles is None else tiles

    zero = jnp.zeros((params,), jnp.float32)
    theta = (highest + lowest) / 2.0
    delta = (highest - lowest) / 2.0
    sigma = theta / delta
    ratio = 1.0 / sigma
    step = right_side / theta
    solution = jnp.zeros(right_side.shape, jnp.float32)
    residual = right_side
    for turn in range(ITERS):
        if turn > 0:
            new_ratio = 1.0 / (2.0 * sigma - ratio)
            step = new_ratio * ratio * step + 2.0 * new_ratio / delta * residual
            ratio = new_ratio
        solution = solution + step
        low = step.astype(jnp.bfloat16)
        early = []
        if turn == 0:
            extra = jnp.broadcast_to(weights[:, None, :], (2 * CORES, 16, params))
            low = jnp.concatenate([low, extra.astype(jnp.bfloat16)], axis=1)
        if turn == ITERS - 1:
            early = [whole(solution)]
        sums, pieces, plan, tiles, early = gather_field(grid, low, plan, load, *early)
        rest, point_sums, sides = rest_product(grid, plan, tiles, sums, pieces)
        gram = scatter_sum(grid, plan, tiles, rest, point_sums)
        sides = sides.astype(jnp.float32)
        if turn == 0:
            w_left, w_right = [], []
            for c, home in enumerate(homes):
                first, last = home == 0, home == grid.count - 1
                left, right = sides[2 * c, :, rows], sides[2 * c + 1, :, rows]
                one, two = weights[2 * c], weights[2 * c + 1]
                w_left += [jnp.where(first, zero, left[0]), jnp.where(first, zero, two)]
                w_right += [one, jnp.where(last, one, right[1])]
            w_left = jnp.stack(w_left)[:, None, :]
            w_right = jnp.stack(w_right)[:, None, :]
        left = jnp.concatenate([sides[2 * c, :, :rows] for c in range(CORES)])
        right = []
        for c, home in enumerate(homes):
            turned = step[2 * c : 2 * c + 2][::-1]
            right.append(jnp.where(home == grid.count - 1, turned, sides[2 * c + 1, :, :rows]))
        prior = w_left * (step - left) + w_right * (step - jnp.concatenate(right))
        residual = residual - (gram + prior + damping * step)
    return early[0], whole(residual)


def solution(mesh):
    return jax.shard_map(
        on_device,
        mesh=mesh,
        in_specs=(
            P(BOTH, None, None),
            P(BOTH),
            P(BOTH),
            P(BOTH),
            P(BOTH, None),
            P(BOTH, None, None),
        ),
        out_specs=(P(BOTH, None, None), P(BOTH, None, None)),
        check_vma=False,
    )
```

```python
import functools
import math

import jax
import jax.numpy as jnp
from jax import lax
from jax.experimental import pallas as pl
from jax.experimental.pallas import tpu as pltpu
from jax.sharding import PartitionSpec as P

PT_DEV = 16
ITERS = 3
CORES = 2
UNROLL = 8
AREAS = 2
NEAR = 2 * AREAS

damping = 0.5
lowest = 0.5
highest = 8.0
BOTH = ("row", "col")
ONE, TWO, BOTH_AXES = ("x", "y"), ("y", "x"), "x y"


class Grid:
    def __init__(self):
        rows = lax.axis_size("row")
        cols = lax.axis_size("col")
        self.sizes = {"y": rows // CORES, "core": CORES, "z": cols // 2, "x": 2}
        self.count = rows * cols
        self.plane = self.sizes["z"] * CORES * 2

    def coords(self, device):
        cols = self.sizes["z"] * 2
        if isinstance(device, int):
            row, col = device // cols, device % cols
            return {"y": row // 2, "core": row % 2, "z": col // 2, "x": col % 2}
        row, col = lax.div(device, cols), lax.rem(device, cols)
        return {"y": lax.div(row, 2), "core": lax.rem(row, 2), "z": lax.div(col, 2), "x": lax.rem(col, 2)}

    def device(self, at):
        row = at["y"] * 2 + at["core"]
        col = at["z"] * 2 + at["x"]
        return row * self.sizes["z"] * 2 + col

    def spot(self, pose, home):
        at, base = self.coords(lax.div(pose, 2)), self.coords(home)
        away = {a: lax.rem(at[a] - base[a] + n, n) for a, n in self.sizes.items()}
        x, y, z = away["x"], away["y"], at["z"] ^ base["z"]
        if self.sizes["y"] == 2:
            swap = base["core"] == 1
            x, y = jnp.where(swap, y, x), jnp.where(swap, x, y)
        z = jnp.where(z == 0, 0, self.sizes["z"] - z)
        chip = (y * 2 + x) * self.sizes["z"] + z
        spot = (chip * CORES + at["core"]) * 2 + lax.rem(pose, 2)
        area = jnp.where(spot < self.plane, 0, 1)
        return area, spot - area * self.plane

    def send(self, block, axes, distance):
        route = []
        for source in range(self.count):
            at = self.coords(source)
            names = axes if isinstance(axes, str) else axes[at["core"]]
            for name in names.split():
                moved = (at[name] + distance) % self.sizes[name]
                at[name] = at[name] ^ distance if name == "z" else moved
            route.append((source, self.device(at)))
        return lax.ppermute(block, BOTH, route)

    def fetch(self, block, axes, distance):
        return self.send(block, axes, -distance)

    def swap(self, block):
        return self.send(block, "core", 1)


def along_z(grid, block):
    depth = grid.sizes["z"]
    moved = [grid.send(block, "z", r) for r in range(1, depth)]
    return jnp.concatenate([block] + moved[::-1])


def gather_field(grid, low, plan, load):
    wide = grid.sizes["y"]
    base = along_z(grid, low)
    if wide == 2:
        corner = grid.send(low, BOTH_AXES, 1)
        base, corner, plan = lax.optimization_barrier((base, corner, plan))
        tiles = load()
        sums = base_product(plan, tiles, base)
        over = [grid.send(base, axes, 1) for axes in (ONE, TWO)]
        far = along_z(grid, corner)
        far, *sums = lax.optimization_barrier((far, *sums))
        pieces = [*over, far]
    else:
        base, plan = lax.optimization_barrier((base, plan))
        tiles = load()
        sums = base_product(plan, tiles, base)
        lines = [base] + [grid.fetch(base, "y", r) for r in range(1, wide)]
        pieces = []
        for line in lines:
            pieces += [line, grid.fetch(line, "x", 1)]
        pieces = pieces[1:]
    return sums, pieces, plan, tiles


def scatter_sum(grid, plan, tiles, rest, low):
    depth, wide = grid.sizes["z"], grid.sizes["y"]
    order = range(depth - 1, 0, -1)
    shape = (depth, 2 * CORES, low.shape[1], tiles.shape[2])

    def narrow(v):
        return v.astype(jnp.bfloat16)

    def widen(v):
        return v.astype(jnp.float32)

    diagonal = 0.0
    if wide == 2:
        one, two, here, *parts = rest
        one, two, *parts = lax.optimization_barrier((one, two, *parts))
        one, two = grid.send(one, ONE, 1), grid.send(two, TWO, 1)
        parts = [grid.send(parts[depth - r - 1], "z", r) for r in order]
        parts[0], low = lax.optimization_barrier((parts[0], low))
        base = base_return(grid, plan, tiles, low)
        *parts, one, two, base = lax.optimization_barrier((*parts, one, two, base))
        base = (base + widen(one) + widen(two)).reshape(shape)
        corner = narrow(here + sum(widen(part) for part in parts))
    else:
        total = jnp.concatenate([base_return(grid, plan, tiles, low), rest[0]])
        total = total.reshape((wide, 2) + shape)
        total = total[:, 0] + widen(grid.send(narrow(total[:, 1]), "x", 1))
        base = total[0]
        for r in range(1, wide):
            base = base + widen(grid.send(narrow(total[r]), "y", r))
        corner = None
    parts = [narrow(base[depth - r]) for r in order]
    if corner is not None:
        *parts, corner = lax.optimization_barrier((*parts, corner))
        diagonal = widen(grid.send(corner, BOTH_AXES, 1))
    gram = base[0] + diagonal
    for r, part in zip(order, parts):
        gram = gram + widen(grid.send(part, "z", r))
    return gram


def plan_kernel(near, area, pose, point, valid, out):
    tiles, slots = area.shape[1], out.shape[1]
    row_id = lax.broadcasted_iota(jnp.int32, (tiles, tiles), 0)
    col_id = lax.broadcasted_iota(jnp.int32, (tiles, tiles), 1)
    lane = lax.broadcasted_iota(jnp.int32, (tiles, slots), 1)

    def column(row):
        return jnp.sum(jnp.where(row_id == col_id, row, 0.0), axis=1, keepdims=True)

    def half_up(v, unit):
        whole = v.astype(jnp.int32) + (unit - 1)
        return (whole & ~(unit - 1)).astype(jnp.float32)

    def arrange(key, phase):
        key_col, phase_col = column(key), column(phase)
        same = jnp.where((key_col == key) & (real_col > 0.0) & (real > 0.0), 1.0, 0.0)
        count = jnp.sum(same, axis=0, keepdims=True)
        rank = jnp.sum(jnp.where(row_id < col_id, same, 0.0), axis=0, keepdims=True)
        rank_col = jnp.sum(jnp.where(col_id < row_id, same, 0.0), axis=1, keepdims=True)
        room = jnp.where((rank == 0.0) & (real > 0.0), half_up(count, 2), 0.0)
        place = jnp.sum(jnp.where(key < key_col, room, 0.0), axis=1, keepdims=True) + rank_col
        end, gap, bounds = 0.0, 0.0, []
        for k in range(AREAS):
            used = jnp.sum(jnp.where(phase == k, room, 0.0), axis=1, keepdims=True)
            place = place + jnp.where(phase_col == k, gap, 0.0)
            padded = half_up(used, 2 * UNROLL)
            end, gap = end + padded, gap + padded - used
            bounds.append(end)
        place = jnp.where(real_col > 0.0, place, -1.0)
        return jnp.where(place.astype(jnp.int32) == lane, 1.0, 0.0), bounds

    def pick(hit, values):
        return jnp.sum(hit * values, axis=0, keepdims=True)

    real = valid[...].astype(jnp.float32)
    real_col = column(real)
    area_row = area[...].astype(jnp.float32)
    pose_row = pose[...].astype(jnp.float32)
    point_row = point[...].astype(jnp.float32)
    pose_col, point_col = column(pose_row), column(point_row)
    tile_col = column(col_id[:1].astype(jnp.float32))
    points = CORES * PT_DEV
    hit, ends = arrange(area_row * points + point_row, area_row)
    rows = [
        pick(hit, tile_col),
        pick(hit, pose_col),
        pick(hit, jnp.ones_like(tile_col)),
        pick(hit, point_col),
    ]
    turned = AREAS - 1.0 - area_row
    hit, bounds = arrange(turned * 65536.0 + pose_row, turned)
    rows += [
        pick(hit, tile_col),
        pick(hit, point_col - points) + points,
        pick(hit, pose_col),
    ]
    ends += bounds
    spot = lane[:1]
    tail = jnp.zeros_like(rows[0])
    for k, end in enumerate(ends):
        tail = jnp.where(spot == k, end * (0.5 / UNROLL), tail)
    for k in range(near.shape[0]):
        tail = jnp.where(spot == NEAR + k, near[k].astype(jnp.float32), tail)
    for k, row in enumerate(rows + [tail]):
        out[k : k + 1] = row.astype(jnp.int32)


def make_plan(grid, place, near, indices):
    pose, point, valid = indices
    tiles = pose.shape[0]
    area, pose = grid.spot(pose, place)
    slots = tiles + max(AREAS * CORES * PT_DEV, min(tiles, 2 * grid.count)) + 2 * AREAS * UNROLL
    slots = -(-slots // 128) * 128
    rows = [v.reshape(1, tiles) for v in (area, pose, point, valid)]
    vmem = pl.BlockSpec(memory_space=pltpu.VMEM)
    return pl.pallas_call(
        plan_kernel,
        out_shape=jax.ShapeDtypeStruct((8, slots), jnp.int32),
        in_specs=[pl.BlockSpec(memory_space=pltpu.SMEM)] + [vmem] * 4,
        out_specs=vmem,
        compiler_params=pltpu.CompilerParams(vmem_limit_bytes=32 * tiles * slots + 2 * 1024 * 1024),
    )(near, *rows)


def join_kernel(first, second, out, sems):
    half = first.shape[0]
    copies = [
        pltpu.make_async_copy(first, out.at[pl.ds(0, half)], sems.at[0]),
        pltpu.make_async_copy(second, out.at[pl.ds(half, half)], sems.at[1]),
    ]
    for copy in copies:
        copy.start()
    for copy in copies:
        copy.wait()


def join_tiles(first, second):
    shape = (2 * first.shape[0], *first.shape[1:])
    return pl.pallas_call(
        join_kernel,
        out_shape=jax.ShapeDtypeStruct(shape, first.dtype),
        in_specs=[pl.BlockSpec(memory_space=pl.ANY)] * 2,
        out_specs=pl.BlockSpec(memory_space=pltpu.VMEM),
        scratch_shapes=[pltpu.SemaphoreType.DMA((2,))],
        compiler_params=pltpu.CompilerParams(vmem_limit_bytes=2 * 1024 * 1024),
    )(first, second)


NT = (((1,), (1,)), ((), ()))
NN = (((1,), (0,)), ((), ()))
F_TILE, F_POSE, F_REAL, F_POINT, B_TILE, B_POINT, B_POSE, ENDS = range(8)


def forward(plan, tiles, field, acc, begin, end):
    def body(i, _):
        for u in range(UNROLL):
            j = 2 * (i * UNROLL + u)
            block = [
                field[plan[F_POSE, j + h], : acc.shape[1]]
                * plan[F_REAL, j + h].astype(jnp.float32).astype(jnp.bfloat16)
                for h in range(2)
            ]
            tile = [tiles[plan[F_TILE, j + h]] for h in range(2)]
            acc[plan[F_POINT, j]] += lax.dot_general(
                jnp.concatenate(block, axis=1),
                jnp.concatenate(tile, axis=1),
                NT,
                preferred_element_type=jnp.float32,
            )
        return 0

    lax.fori_loop(begin, end, body, 0)


def backward(plan, tiles, low, total, begin, end):
    def body(i, _):
        for u in range(UNROLL):
            j = 2 * (i * UNROLL + u)
            block = [low[plan[B_POINT, j + h]] for h in range(2)]
            tile = [tiles[plan[B_TILE, j + h]] for h in range(2)]
            total[plan[B_POSE, j]] += lax.dot_general(
                jnp.concatenate(block, axis=1),
                jnp.concatenate(tile, axis=0),
                NN,
                preferred_element_type=jnp.float32,
            )
        return 0

    lax.fori_loop(begin, end, body, 0)


def assemble(pieces, field):
    start = 0
    for piece in pieces:
        field[start : start + piece.shape[0]] = piece[...]
        start += piece.shape[0]


def near_side(plan, field, sides, area):
    for side in range(sides.shape[0]):
        spot = NEAR + 2 * side

        @pl.when(plan[ENDS, spot] == area)
        def _():
            sides[side] = field[pl.ds(plan[ENDS, spot + 1], 2)]


def base_forward(plan_in, tiles, field, acc, sides, plan, sem):
    copy = pltpu.make_async_copy(plan_in, plan, sem)
    copy.start()
    acc[...] = jnp.zeros_like(acc)
    sides[...] = jnp.zeros_like(sides)
    copy.wait()
    near_side(plan, field, sides, 0)
    forward(plan, tiles, field, acc, 0, plan[ENDS, 0])


def rest_both(cuts, plan_in, tiles, part, sides_in, *refs):
    pieces, refs = refs[: -len(cuts) - 7], refs[-len(cuts) - 7 :]
    (acc, sides, low), outs, (field, total, plan, sem) = refs[:3], refs[3:-4], refs[-4:]
    copy = pltpu.make_async_copy(plan_in, plan, sem)
    copy.start()
    assemble(pieces, field)
    total[...] = jnp.zeros_like(total)
    points = acc.shape[0]
    low[points] = jnp.zeros(low.shape[1:], jnp.bfloat16)
    copy.wait()
    near_side(plan, field, sides, 1)
    forward(plan, tiles, field, acc, plan[ENDS, 0], plan[ENDS, 1])
    low[:points] = acc[...].astype(jnp.bfloat16)
    backward(plan, tiles, low, total, 0, plan[ENDS, AREAS])
    start = 0
    for size, out in zip(cuts, outs):
        out[...] = total[start : start + size].astype(out.dtype)
        start += size


def base_backward(plan_in, tiles, low, base, plan, sem):
    copy = pltpu.make_async_copy(plan_in, plan, sem)
    copy.start()
    base[...] = jnp.zeros_like(base)
    copy.wait()
    backward(plan, tiles, low, base, plan[ENDS, AREAS], plan[ENDS, AREAS + 1])


def call(kernel, outs, scratch, args, kinds, tiles, share, aliases={}):
    place = {
        "a": pl.BlockSpec(memory_space=pl.ANY),
        "v": pl.BlockSpec(memory_space=pltpu.VMEM),
    }
    size = sum(math.prod(v.shape) * jnp.dtype(v.dtype).itemsize for v in scratch)
    scratch = scratch + [pltpu.SMEM(args[0].shape, jnp.int32), pltpu.SemaphoreType.DMA]
    return pl.pallas_call(
        kernel,
        out_shape=outs,
        in_specs=[place[kind] for kind in kinds],
        out_specs=[place["v"]] * len(outs),
        scratch_shapes=scratch,
        input_output_aliases=aliases,
        compiler_params=pltpu.CompilerParams(vmem_limit_bytes=size + 3 * 1024 * 1024),
        cost_estimate=pl.CostEstimate(
            flops=int(share * 4 * tiles.size * 128),
            bytes_accessed=tiles.size * 2,
            transcendentals=0,
        ),
    )(*args)


def array(lead, like, kind):
    return jax.ShapeDtypeStruct((lead, *like[1:]), kind)


def base_product(plan, tiles, base):
    rows = tiles.shape[1] // CORES
    acc = (0, rows, tiles.shape[1])
    return call(
        base_forward,
        [
            array(CORES * PT_DEV, acc, jnp.float32),
            jax.ShapeDtypeStruct((2 * CORES, 2, *base.shape[1:]), jnp.bfloat16),
        ],
        [],
        [plan, tiles, base],
        "avv",
        tiles,
        0.125,
    )


def rest_product(grid, plan, tiles, sums, pieces):
    plane = grid.plane
    rest = 2 * grid.count - plane
    if grid.sizes["y"] == 2:
        group = 2 * CORES
        cuts = [plane, plane, group] + [group] * (grid.sizes["z"] - 1)
        kinds = [jnp.bfloat16, jnp.bfloat16, jnp.float32] + [jnp.bfloat16] * (grid.sizes["z"] - 1)
    else:
        cuts, kinds = [rest], [jnp.float32]
    rows, points = sums[0].shape[1:]
    like = (0, rows, tiles.shape[2])
    _, sides, low, *outs = call(
        functools.partial(rest_both, cuts),
        [
            *[jax.ShapeDtypeStruct(v.shape, v.dtype) for v in sums],
            array(CORES * PT_DEV + 1, (0, rows, points), jnp.bfloat16),
            *[array(cut, like, kind) for cut, kind in zip(cuts, kinds)],
        ],
        [pltpu.VMEM((rest, *pieces[0].shape[1:]), jnp.bfloat16), pltpu.VMEM((rest, *like[1:]), jnp.float32)],
        [plan, tiles, *sums, *pieces],
        "avvv" + "v" * len(pieces),
        tiles,
        0.75,
        {2: 0, 3: 1},
    )
    return outs, low, sides


def base_return(grid, plan, tiles, low):
    (base,) = call(
        base_backward,
        [array(grid.plane, (0, low.shape[1], tiles.shape[2]), jnp.float32)],
        [],
        [plan, tiles, low],
        "avv",
        tiles,
        0.125,
    )
    return base


def in_order(core, mine, theirs, axis):
    low, high = jnp.where(core == 0, mine, theirs), jnp.where(core == 0, theirs, mine)
    return jnp.concatenate([low, high], axis=axis)


def on_device(jac_tiles, tile_pose, tile_point, tile_valid, prior_weight, right_side):
    grid = Grid()
    place = lax.axis_index(BOTH)
    at = grid.coords(place)
    core = at["core"]
    homes = [grid.device(at | {"core": c}) for c in range(CORES)]
    params, rhs = right_side.shape[1:]
    rows = rhs // CORES

    def half(v, which):
        return lax.dynamic_slice_in_dim(v, which * rows, rows, 1)

    def whole(*values):
        v = jnp.stack(values).reshape((-1, CORES, 2) + values[0].shape[1:])
        mine = lax.dynamic_index_in_dim(v, core, 1, keepdims=False)
        theirs = grid.swap(lax.dynamic_index_in_dim(v, 1 - core, 1, keepdims=False))
        return tuple(jnp.swapaxes(in_order(core, mine, theirs, 2), 2, 3))

    turned = jnp.swapaxes(right_side, 1, 2)
    names = jnp.stack([tile_pose, tile_point, tile_valid]).astype(jnp.float32)
    width = -(-names.shape[1] // params)
    names = jnp.pad(names, ((0, 0), (0, width * params - names.shape[1])))
    extra = jnp.concatenate([prior_weight, names.reshape(3 * width, params)])
    extra = jnp.pad(extra, ((0, -extra.shape[0] % 16), (0, 0))).reshape(2, -1, params)
    pack = jnp.concatenate([half(turned, 1 - core), extra], axis=1)
    other_tiles = grid.swap(jac_tiles)
    theirs = grid.swap(pack)
    right_side = in_order(core, half(turned, core), theirs[:, :rows], 0)
    theirs = theirs[:, rows:].reshape(-1, params)
    weights = in_order(core, prior_weight, theirs[:2], 0)
    names = theirs[2 : 2 + 3 * width].reshape(3, -1)[:, : tile_pose.shape[0]].astype(jnp.int32)
    indices = jnp.stack([tile_pose, tile_point, tile_valid])
    shift = jnp.array([[0], [PT_DEV], [0]], jnp.int32)
    indices = jnp.concatenate([indices, names + shift], axis=1)
    near = []
    for home in homes:
        near += grid.spot(2 * jnp.maximum(home - 1, 0), place)
        near += grid.spot(2 * jnp.minimum(home + 1, grid.count - 1), place)
    plan = make_plan(grid, place, jnp.stack(near), indices)
    tiles = None

    def load():
        return join_tiles(jac_tiles, other_tiles) if tiles is None else tiles

    zero = jnp.zeros((params,), jnp.float32)
    theta = (highest + lowest) / 2.0
    delta = (highest - lowest) / 2.0
    sigma = theta / delta
    ratio = 1.0 / sigma
    step = right_side / theta
    solution = jnp.zeros(right_side.shape, jnp.float32)
    residual = right_side
    for turn in range(ITERS):
        if turn > 0:
            new_ratio = 1.0 / (2.0 * sigma - ratio)
            step = new_ratio * ratio * step + 2.0 * new_ratio / delta * residual
            ratio = new_ratio
        solution = solution + step
        low = step.astype(jnp.bfloat16)
        if turn == 0:
            extra = jnp.broadcast_to(weights[:, None, :], (2 * CORES, 16, params))
            low = jnp.concatenate([low, extra.astype(jnp.bfloat16)], axis=1)
        sums, pieces, plan, tiles = gather_field(grid, low, plan, load)
        rest, point_sums, sides = rest_product(grid, plan, tiles, sums, pieces)
        gram = scatter_sum(grid, plan, tiles, rest, point_sums)
        sides = sides.astype(jnp.float32)
        if turn == 0:
            w_left, w_right = [], []
            for c, home in enumerate(homes):
                first, last = home == 0, home == grid.count - 1
                left, right = sides[2 * c, :, rows], sides[2 * c + 1, :, rows]
                one, two = weights[2 * c], weights[2 * c + 1]
                w_left += [jnp.where(first, zero, left[0]), jnp.where(first, zero, two)]
                w_right += [one, jnp.where(last, one, right[1])]
            w_left = jnp.stack(w_left)[:, None, :]
            w_right = jnp.stack(w_right)[:, None, :]
        left = jnp.concatenate([sides[2 * c, :, :rows] for c in range(CORES)])
        right = []
        for c, home in enumerate(homes):
            turned = step[2 * c : 2 * c + 2][::-1]
            right.append(jnp.where(home == grid.count - 1, turned, sides[2 * c + 1, :, :rows]))
        prior = w_left * (step - left) + w_right * (step - jnp.concatenate(right))
        residual = residual - (gram + prior + damping * step)
    return whole(solution, residual)


def solution(mesh):
    return jax.shard_map(
        on_device,
        mesh=mesh,
        in_specs=(
            P(BOTH, None, None),
            P(BOTH),
            P(BOTH),
            P(BOTH),
            P(BOTH, None),
            P(BOTH, None, None),
        ),
        out_specs=(P(BOTH, None, None), P(BOTH, None, None)),
        check_vma=False,
    )
```

```python
import functools
import math

import jax
import jax.numpy as jnp
from jax import lax
from jax.experimental import pallas as pl
from jax.experimental.pallas import tpu as pltpu
from jax.sharding import PartitionSpec as P

PT_DEV = 16
ITERS = 3
CORES = 2
UNROLL = 8
AREAS = 2
PHASES = AREAS * CORES
NEAR = 2 * PHASES

damping = 0.5
lowest = 0.5
highest = 8.0
BOTH = ("row", "col")
ONE, TWO, BOTH_AXES = ("x", "y"), ("y", "x"), "x y"


class Grid:
    def __init__(self):
        rows = lax.axis_size("row")
        cols = lax.axis_size("col")
        self.sizes = {"y": rows // CORES, "core": CORES, "z": cols // 2, "x": 2}
        self.count = rows * cols
        self.plane = self.sizes["z"] * CORES * 2

    def coords(self, device):
        cols = self.sizes["z"] * 2
        if isinstance(device, int):
            row, col = device // cols, device % cols
            return {"y": row // 2, "core": row % 2, "z": col // 2, "x": col % 2}
        row, col = lax.div(device, cols), lax.rem(device, cols)
        return {"y": lax.div(row, 2), "core": lax.rem(row, 2), "z": lax.div(col, 2), "x": lax.rem(col, 2)}

    def device(self, at):
        row = at["y"] * 2 + at["core"]
        col = at["z"] * 2 + at["x"]
        return row * self.sizes["z"] * 2 + col

    def spot(self, pose, home):
        at, base = self.coords(lax.div(pose, 2)), self.coords(home)
        away = {a: lax.rem(at[a] - base[a] + n, n) for a, n in self.sizes.items()}
        x, y, z = away["x"], away["y"], at["z"] ^ base["z"]
        if self.sizes["y"] == 2:
            swap = base["core"] == 1
            x, y = jnp.where(swap, y, x), jnp.where(swap, x, y)
        z = jnp.where(z == 0, 0, self.sizes["z"] - z)
        chip = (y * 2 + x) * self.sizes["z"] + z
        spot = (chip * CORES + at["core"]) * 2 + lax.rem(pose, 2)
        area = jnp.where(spot < self.plane, 0, 1)
        return area, spot - area * self.plane

    def send(self, block, axes, distance):
        route = []
        for source in range(self.count):
            at = self.coords(source)
            names = axes if isinstance(axes, str) else axes[at["core"]]
            for name in names.split():
                moved = (at[name] + distance) % self.sizes[name]
                at[name] = at[name] ^ distance if name == "z" else moved
            route.append((source, self.device(at)))
        return lax.ppermute(block, BOTH, route)

    def fetch(self, block, axes, distance):
        return self.send(block, axes, -distance)

    def swap(self, block):
        return self.send(block, "core", 1)


def along_z(grid, block):
    depth = grid.sizes["z"]
    moved = [grid.send(block, "z", r) for r in range(1, depth)]
    return jnp.concatenate([block] + moved[::-1])


def gather_field(grid, low, plan, tiles):
    wide = grid.sizes["y"]
    base = along_z(grid, low)
    if wide == 2:
        corner = grid.send(low, BOTH_AXES, 1)
        base, corner, plan = lax.optimization_barrier((base, corner, plan))
        sums = base_product(plan, tiles, base)
        over = [grid.send(base, axes, 1) for axes in (ONE, TWO)]
        far = along_z(grid, corner)
        far, *sums = lax.optimization_barrier((far, *sums))
        pieces = [*over, far]
    else:
        base, plan = lax.optimization_barrier((base, plan))
        sums = base_product(plan, tiles, base)
        lines = [base] + [grid.fetch(base, "y", r) for r in range(1, wide)]
        pieces = []
        for line in lines:
            pieces += [line, grid.fetch(line, "x", 1)]
        pieces = pieces[1:]
    return sums, pieces, plan


def scatter_sum(grid, plan, tiles, rest, low):
    depth, wide = grid.sizes["z"], grid.sizes["y"]
    order = range(depth - 1, 0, -1)
    shape = (depth, 2 * CORES, low.shape[1], tiles[0].shape[2])

    def narrow(v):
        return v.astype(jnp.bfloat16)

    def widen(v):
        return v.astype(jnp.float32)

    diagonal = 0.0
    if wide == 2:
        one, two, here, *parts = rest
        one, two, *parts = lax.optimization_barrier((one, two, *parts))
        one, two = grid.send(one, ONE, 1), grid.send(two, TWO, 1)
        parts = [grid.send(parts[depth - r - 1], "z", r) for r in order]
        parts[0], low = lax.optimization_barrier((parts[0], low))
        base = base_return(grid, plan, tiles, low)
        *parts, one, two, base = lax.optimization_barrier((*parts, one, two, base))
        base = (base + widen(one) + widen(two)).reshape(shape)
        corner = narrow(here + sum(widen(part) for part in parts))
    else:
        total = jnp.concatenate([base_return(grid, plan, tiles, low), rest[0]])
        total = total.reshape((wide, 2) + shape)
        total = total[:, 0] + widen(grid.send(narrow(total[:, 1]), "x", 1))
        base = total[0]
        for r in range(1, wide):
            base = base + widen(grid.send(narrow(total[r]), "y", r))
        corner = None
    parts = [narrow(base[depth - r]) for r in order]
    if corner is not None:
        *parts, corner = lax.optimization_barrier((*parts, corner))
        diagonal = widen(grid.send(corner, BOTH_AXES, 1))
    gram = base[0] + diagonal
    for r, part in zip(order, parts):
        gram = gram + widen(grid.send(part, "z", r))
    return gram


def plan_kernel(near, area, pose, point, valid, out):
    tiles, slots = area.shape[1], out.shape[1]
    row_id = lax.broadcasted_iota(jnp.int32, (tiles, tiles), 0)
    col_id = lax.broadcasted_iota(jnp.int32, (tiles, tiles), 1)
    lane = lax.broadcasted_iota(jnp.int32, (tiles, slots), 1)

    def column(row):
        return jnp.sum(jnp.where(row_id == col_id, row, 0.0), axis=1, keepdims=True)

    def half_up(v, unit):
        whole = v.astype(jnp.int32) + (unit - 1)
        return (whole & ~(unit - 1)).astype(jnp.float32)

    def arrange(key, phase):
        key_col, phase_col = column(key), column(phase)
        same = jnp.where((key_col == key) & (real_col > 0.0) & (real > 0.0), 1.0, 0.0)
        count = jnp.sum(same, axis=0, keepdims=True)
        rank = jnp.sum(jnp.where(row_id < col_id, same, 0.0), axis=0, keepdims=True)
        rank_col = jnp.sum(jnp.where(col_id < row_id, same, 0.0), axis=1, keepdims=True)
        room = jnp.where((rank == 0.0) & (real > 0.0), half_up(count, 2), 0.0)
        place = jnp.sum(jnp.where(key < key_col, room, 0.0), axis=1, keepdims=True) + rank_col
        end, gap, bounds = 0.0, 0.0, []
        for k in range(PHASES):
            used = jnp.sum(jnp.where(phase == k, room, 0.0), axis=1, keepdims=True)
            place = place + jnp.where(phase_col == k, gap, 0.0)
            padded = half_up(used, 2 * UNROLL)
            end, gap = end + padded, gap + padded - used
            bounds.append(end)
        place = jnp.where(real_col > 0.0, place, -1.0)
        return jnp.where(place.astype(jnp.int32) == lane, 1.0, 0.0), bounds

    def pick(hit, values):
        return jnp.sum(hit * values, axis=0, keepdims=True)

    real = valid[...].astype(jnp.float32)
    real_col = column(real)
    area_row = area[...].astype(jnp.float32)
    source = jnp.where(col_id[:1] < tiles // CORES, 0.0, 1.0)
    pose_row = pose[...].astype(jnp.float32)
    point_row = point[...].astype(jnp.float32)
    pose_col, point_col = column(pose_row), column(point_row)
    tile_col = column(col_id[:1].astype(jnp.float32) - source * (tiles // CORES))
    points = CORES * PT_DEV
    phase = area_row * CORES + source
    hit, ends = arrange(phase * points + point_row, phase)
    rows = [
        pick(hit, tile_col),
        pick(hit, pose_col),
        pick(hit, jnp.ones_like(tile_col)),
        pick(hit, point_col),
    ]
    phase = (AREAS - 1.0 - area_row) * CORES + source
    hit, bounds = arrange(phase * 65536.0 + pose_row, phase)
    rows += [
        pick(hit, tile_col),
        pick(hit, point_col - points) + points,
        pick(hit, pose_col),
    ]
    ends += bounds
    spot = lane[:1]
    tail = jnp.zeros_like(rows[0])
    for k, end in enumerate(ends):
        tail = jnp.where(spot == k, end * (0.5 / UNROLL), tail)
    for k in range(near.shape[0]):
        tail = jnp.where(spot == NEAR + k, near[k].astype(jnp.float32), tail)
    for k, row in enumerate(rows + [tail]):
        out[k : k + 1] = row.astype(jnp.int32)


def make_plan(grid, place, near, indices):
    pose, point, valid = indices
    tiles = pose.shape[0]
    area, pose = grid.spot(pose, place)
    slots = tiles + max(AREAS * CORES * PT_DEV, min(tiles, 2 * CORES * grid.count)) + 2 * PHASES * UNROLL
    slots = -(-slots // 128) * 128
    rows = [v.reshape(1, tiles) for v in (area, pose, point, valid)]
    vmem = pl.BlockSpec(memory_space=pltpu.VMEM)
    return pl.pallas_call(
        plan_kernel,
        out_shape=jax.ShapeDtypeStruct((8, slots), jnp.int32),
        in_specs=[pl.BlockSpec(memory_space=pltpu.SMEM)] + [vmem] * 4,
        out_specs=vmem,
        compiler_params=pltpu.CompilerParams(vmem_limit_bytes=32 * tiles * slots + 2 * 1024 * 1024),
    )(near, *rows)


NT = (((1,), (1,)), ((), ()))
NN = (((1,), (0,)), ((), ()))
F_TILE, F_POSE, F_REAL, F_POINT, B_TILE, B_POINT, B_POSE, ENDS = range(8)


def forward(plan, sources, field, acc, first):
    for k, tiles in enumerate(sources):
        begin = plan[ENDS, first + k - 1] if first + k else 0
        forward_one(plan, tiles, field, acc, begin, plan[ENDS, first + k])


def forward_one(plan, tiles, field, acc, begin, end):
    def body(i, _):
        for u in range(UNROLL):
            j = 2 * (i * UNROLL + u)
            block = [
                field[plan[F_POSE, j + h], : acc.shape[1]]
                * plan[F_REAL, j + h].astype(jnp.float32).astype(jnp.bfloat16)
                for h in range(2)
            ]
            tile = [tiles[plan[F_TILE, j + h]] for h in range(2)]
            acc[plan[F_POINT, j]] += lax.dot_general(
                jnp.concatenate(block, axis=1),
                jnp.concatenate(tile, axis=1),
                NT,
                preferred_element_type=jnp.float32,
            )
        return 0

    lax.fori_loop(begin, end, body, 0)


def backward(plan, sources, low, total, first):
    for k, tiles in enumerate(sources):
        begin = plan[ENDS, PHASES + first + k - 1] if first + k else 0
        backward_one(plan, tiles, low, total, begin, plan[ENDS, PHASES + first + k])


def backward_one(plan, tiles, low, total, begin, end):
    def body(i, _):
        for u in range(UNROLL):
            j = 2 * (i * UNROLL + u)
            block = [low[plan[B_POINT, j + h]] for h in range(2)]
            tile = [tiles[plan[B_TILE, j + h]] for h in range(2)]
            total[plan[B_POSE, j]] += lax.dot_general(
                jnp.concatenate(block, axis=1),
                jnp.concatenate(tile, axis=0),
                NN,
                preferred_element_type=jnp.float32,
            )
        return 0

    lax.fori_loop(begin, end, body, 0)


def assemble(pieces, field):
    start = 0
    for piece in pieces:
        field[start : start + piece.shape[0]] = piece[...]
        start += piece.shape[0]


def near_side(plan, field, sides, area):
    for side in range(sides.shape[0]):
        spot = NEAR + 2 * side

        @pl.when(plan[ENDS, spot] == area)
        def _():
            sides[side] = field[pl.ds(plan[ENDS, spot + 1], 2)]


def base_forward(plan_in, tiles, others, field, acc, sides, plan, sem):
    copy = pltpu.make_async_copy(plan_in, plan, sem)
    copy.start()
    acc[...] = jnp.zeros_like(acc)
    sides[...] = jnp.zeros_like(sides)
    copy.wait()
    near_side(plan, field, sides, 0)
    forward(plan, (tiles, others), field, acc, 0)


def rest_both(cuts, plan_in, tiles, others, part, sides_in, *refs):
    pieces, refs = refs[: -len(cuts) - 7], refs[-len(cuts) - 7 :]
    (acc, sides, low), outs, (field, total, plan, sem) = refs[:3], refs[3:-4], refs[-4:]
    copy = pltpu.make_async_copy(plan_in, plan, sem)
    copy.start()
    assemble(pieces, field)
    total[...] = jnp.zeros_like(total)
    points = acc.shape[0]
    low[points] = jnp.zeros(low.shape[1:], jnp.bfloat16)
    copy.wait()
    near_side(plan, field, sides, 1)
    forward(plan, (tiles, others), field, acc, CORES)
    low[:points] = acc[...].astype(jnp.bfloat16)
    backward(plan, (tiles, others), low, total, 0)
    start = 0
    for size, out in zip(cuts, outs):
        out[...] = total[start : start + size].astype(out.dtype)
        start += size


def base_backward(plan_in, tiles, others, low, base, plan, sem):
    copy = pltpu.make_async_copy(plan_in, plan, sem)
    copy.start()
    base[...] = jnp.zeros_like(base)
    copy.wait()
    backward(plan, (tiles, others), low, base, CORES)


def call(kernel, outs, scratch, args, kinds, tiles, share, aliases={}):
    place = {
        "a": pl.BlockSpec(memory_space=pl.ANY),
        "v": pl.BlockSpec(memory_space=pltpu.VMEM),
    }
    size = sum(math.prod(v.shape) * jnp.dtype(v.dtype).itemsize for v in scratch)
    scratch = scratch + [pltpu.SMEM(args[0].shape, jnp.int32), pltpu.SemaphoreType.DMA]
    return pl.pallas_call(
        kernel,
        out_shape=outs,
        in_specs=[place[kind] for kind in kinds],
        out_specs=[place["v"]] * len(outs),
        scratch_shapes=scratch,
        input_output_aliases=aliases,
        compiler_params=pltpu.CompilerParams(vmem_limit_bytes=size + 12 * 1024 * 1024),
        cost_estimate=pl.CostEstimate(
            flops=int(share * 4 * tiles[0].size * 128),
            bytes_accessed=tiles[0].size * 4,
            transcendentals=0,
        ),
    )(*args)


def array(lead, like, kind):
    return jax.ShapeDtypeStruct((lead, *like[1:]), kind)


def base_product(plan, tiles, base):
    points = tiles[0].shape[1]
    acc = (0, points // CORES, points)
    return call(
        base_forward,
        [
            array(CORES * PT_DEV, acc, jnp.float32),
            jax.ShapeDtypeStruct((2 * CORES, 2, *base.shape[1:]), jnp.bfloat16),
        ],
        [],
        [plan, *tiles, base],
        "avvv",
        tiles,
        0.125,
    )


def rest_product(grid, plan, tiles, sums, pieces):
    plane = grid.plane
    rest = 2 * grid.count - plane
    if grid.sizes["y"] == 2:
        group = 2 * CORES
        cuts = [plane, plane, group] + [group] * (grid.sizes["z"] - 1)
        kinds = [jnp.bfloat16, jnp.bfloat16, jnp.float32] + [jnp.bfloat16] * (grid.sizes["z"] - 1)
    else:
        cuts, kinds = [rest], [jnp.float32]
    rows, points = sums[0].shape[1:]
    like = (0, rows, tiles[0].shape[2])
    _, sides, low, *outs = call(
        functools.partial(rest_both, cuts),
        [
            *[jax.ShapeDtypeStruct(v.shape, v.dtype) for v in sums],
            array(CORES * PT_DEV + 1, (0, rows, points), jnp.bfloat16),
            *[array(cut, like, kind) for cut, kind in zip(cuts, kinds)],
        ],
        [pltpu.VMEM((rest, *pieces[0].shape[1:]), jnp.bfloat16), pltpu.VMEM((rest, *like[1:]), jnp.float32)],
        [plan, *tiles, *sums, *pieces],
        "avvvv" + "v" * len(pieces),
        tiles,
        0.75,
        {3: 0, 4: 1},
    )
    return outs, low, sides


def base_return(grid, plan, tiles, low):
    (base,) = call(
        base_backward,
        [array(grid.plane, (0, low.shape[1], tiles[0].shape[2]), jnp.float32)],
        [],
        [plan, *tiles, low],
        "avvv",
        tiles,
        0.125,
    )
    return base


def in_order(core, mine, theirs, axis):
    low, high = jnp.where(core == 0, mine, theirs), jnp.where(core == 0, theirs, mine)
    return jnp.concatenate([low, high], axis=axis)


def on_device(jac_tiles, tile_pose, tile_point, tile_valid, prior_weight, right_side):
    grid = Grid()
    place = lax.axis_index(BOTH)
    at = grid.coords(place)
    core = at["core"]
    homes = [grid.device(at | {"core": c}) for c in range(CORES)]
    params, rhs = right_side.shape[1:]
    rows = rhs // CORES

    def half(v, which):
        return lax.dynamic_slice_in_dim(v, which * rows, rows, 1)

    def whole(*values):
        v = jnp.stack(values).reshape((-1, CORES, 2) + values[0].shape[1:])
        mine = lax.dynamic_index_in_dim(v, core, 1, keepdims=False)
        theirs = grid.swap(lax.dynamic_index_in_dim(v, 1 - core, 1, keepdims=False))
        return tuple(jnp.swapaxes(in_order(core, mine, theirs, 2), 2, 3))

    turned = jnp.swapaxes(right_side, 1, 2)
    names = jnp.stack([tile_pose, tile_point, tile_valid]).astype(jnp.float32)
    width = -(-names.shape[1] // params)
    names = jnp.pad(names, ((0, 0), (0, width * params - names.shape[1])))
    extra = jnp.concatenate([prior_weight, names.reshape(3 * width, params)])
    extra = jnp.pad(extra, ((0, -extra.shape[0] % 16), (0, 0))).reshape(2, -1, params)
    pack = lax.optimization_barrier(jnp.concatenate([half(turned, 1 - core), extra], axis=1))
    other_tiles = grid.swap(jac_tiles)
    theirs = grid.swap(pack)
    right_side = in_order(core, half(turned, core), theirs[:, :rows], 0)
    notes = [v[:, rows:].reshape(-1, params) for v in (pack, theirs)]
    weights = in_order(core, notes[0][:2], notes[1][:2], 0)
    names = [v[2 : 2 + 3 * width].reshape(3, -1)[:, : tile_pose.shape[0]] for v in notes]
    shift = jnp.array([[0.0], [PT_DEV], [0.0]], jnp.float32)
    indices = jnp.concatenate([names[0], names[1] + shift], axis=1).astype(jnp.int32)
    near = []
    for home in homes:
        near += grid.spot(2 * jnp.maximum(home - 1, 0), place)
        near += grid.spot(2 * jnp.minimum(home + 1, grid.count - 1), place)
    plan = make_plan(grid, place, jnp.stack(near), indices)
    tiles = jac_tiles, other_tiles
    zero = jnp.zeros((params,), jnp.float32)
    theta = (highest + lowest) / 2.0
    delta = (highest - lowest) / 2.0
    sigma = theta / delta
    ratio = 1.0 / sigma
    step = right_side / theta
    solution = jnp.zeros(right_side.shape, jnp.float32)
    residual = right_side
    for turn in range(ITERS):
        if turn > 0:
            new_ratio = 1.0 / (2.0 * sigma - ratio)
            step = new_ratio * ratio * step + 2.0 * new_ratio / delta * residual
            ratio = new_ratio
        solution = solution + step
        low = step.astype(jnp.bfloat16)
        if turn == 0:
            extra = jnp.broadcast_to(weights[:, None, :], (2 * CORES, 16, params))
            low = jnp.concatenate([low, extra.astype(jnp.bfloat16)], axis=1)
        sums, pieces, plan = gather_field(grid, low, plan, tiles)
        rest, point_sums, sides = rest_product(grid, plan, tiles, sums, pieces)
        gram = scatter_sum(grid, plan, tiles, rest, point_sums)
        sides = sides.astype(jnp.float32)
        if turn == 0:
            w_left, w_right = [], []
            for c, home in enumerate(homes):
                first, last = home == 0, home == grid.count - 1
                left, right = sides[2 * c, :, rows], sides[2 * c + 1, :, rows]
                one, two = weights[2 * c], weights[2 * c + 1]
                w_left += [jnp.where(first, zero, left[0]), jnp.where(first, zero, two)]
                w_right += [one, jnp.where(last, one, right[1])]
            w_left = jnp.stack(w_left)[:, None, :]
            w_right = jnp.stack(w_right)[:, None, :]
        left = jnp.concatenate([sides[2 * c, :, :rows] for c in range(CORES)])
        right = []
        for c, home in enumerate(homes):
            turned = step[2 * c : 2 * c + 2][::-1]
            right.append(jnp.where(home == grid.count - 1, turned, sides[2 * c + 1, :, :rows]))
        prior = w_left * (step - left) + w_right * (step - jnp.concatenate(right))
        residual = residual - (gram + prior + damping * step)
    return whole(solution, residual)


def solution(mesh):
    return jax.shard_map(
        on_device,
        mesh=mesh,
        in_specs=(
            P(BOTH, None, None),
            P(BOTH),
            P(BOTH),
            P(BOTH),
            P(BOTH, None),
            P(BOTH, None, None),
        ),
        out_specs=(P(BOTH, None, None), P(BOTH, None, None)),
        check_vma=False,
    )
```

```python
import functools
import math

import jax
import jax.numpy as jnp
from jax import lax
from jax.experimental import pallas as pl
from jax.experimental.pallas import tpu as pltpu
from jax.sharding import PartitionSpec as P

PT_DEV = 16
ITERS = 3
CORES = 2
UNROLL = 16
AREAS = 2
NEAR = 2 * AREAS

damping = 0.5
lowest = 0.5
highest = 8.0
BOTH = ("row", "col")
ONE, TWO, BOTH_AXES = ("x", "y"), ("y", "x"), "x y"


class Grid:
    def __init__(self):
        rows = lax.axis_size("row")
        cols = lax.axis_size("col")
        self.sizes = {"y": rows // CORES, "core": CORES, "z": cols // 2, "x": 2}
        self.count = rows * cols
        self.plane = self.sizes["z"] * CORES * 2

    def coords(self, device):
        cols = self.sizes["z"] * 2
        if isinstance(device, int):
            row, col = device // cols, device % cols
            return {"y": row // 2, "core": row % 2, "z": col // 2, "x": col % 2}
        row, col = lax.div(device, cols), lax.rem(device, cols)
        return {"y": lax.div(row, 2), "core": lax.rem(row, 2), "z": lax.div(col, 2), "x": lax.rem(col, 2)}

    def device(self, at):
        row = at["y"] * 2 + at["core"]
        col = at["z"] * 2 + at["x"]
        return row * self.sizes["z"] * 2 + col

    def spot(self, pose, home):
        at, base = self.coords(lax.div(pose, 2)), self.coords(home)
        away = {a: lax.rem(at[a] - base[a] + n, n) for a, n in self.sizes.items()}
        x, y, z = away["x"], away["y"], at["z"] ^ base["z"]
        if self.sizes["y"] == 2:
            swap = base["core"] == 1
            x, y = jnp.where(swap, y, x), jnp.where(swap, x, y)
        z = jnp.where(z == 0, 0, self.sizes["z"] - z)
        chip = (y * 2 + x) * self.sizes["z"] + z
        spot = (chip * CORES + at["core"]) * 2 + lax.rem(pose, 2)
        area = jnp.where(spot < self.plane, 0, 1)
        return area, spot - area * self.plane

    def send(self, block, axes, distance):
        route = []
        for source in range(self.count):
            at = self.coords(source)
            names = axes if isinstance(axes, str) else axes[at["core"]]
            for name in names.split():
                moved = (at[name] + distance) % self.sizes[name]
                at[name] = at[name] ^ distance if name == "z" else moved
            route.append((source, self.device(at)))
        return lax.ppermute(block, BOTH, route)

    def fetch(self, block, axes, distance):
        return self.send(block, axes, -distance)

    def swap(self, block):
        return self.send(block, "core", 1)


def along_z(grid, block):
    depth = grid.sizes["z"]
    moved = [grid.send(block, "z", r) for r in range(1, depth)]
    return jnp.concatenate([block] + moved[::-1])


def gather_field(grid, low, plan, load):
    wide = grid.sizes["y"]
    base = along_z(grid, low)
    if wide == 2:
        corner = grid.send(low, BOTH_AXES, 1)
        base, corner, plan = lax.optimization_barrier((base, corner, plan))
        tiles = load()
        sums = base_product(plan, tiles, base)
        over = [grid.send(base, axes, 1) for axes in (ONE, TWO)]
        far = along_z(grid, corner)
        far, *sums = lax.optimization_barrier((far, *sums))
        pieces = [*over, far]
    else:
        base, plan = lax.optimization_barrier((base, plan))
        tiles = load()
        sums = base_product(plan, tiles, base)
        lines = [base] + [grid.fetch(base, "y", r) for r in range(1, wide)]
        pieces = []
        for line in lines:
            pieces += [line, grid.fetch(line, "x", 1)]
        pieces = pieces[1:]
    return sums, pieces, plan, tiles


def scatter_sum(grid, plan, tiles, rest, low):
    depth, wide = grid.sizes["z"], grid.sizes["y"]
    order = range(depth - 1, 0, -1)
    shape = (depth, 2 * CORES, low.shape[1], tiles.shape[2])

    def narrow(v):
        return v.astype(jnp.bfloat16)

    def widen(v):
        return v.astype(jnp.float32)

    diagonal = 0.0
    if wide == 2:
        one, two, here, *parts = rest
        one, two, *parts = lax.optimization_barrier((one, two, *parts))
        one, two = grid.send(one, ONE, 1), grid.send(two, TWO, 1)
        parts = [grid.send(parts[depth - r - 1], "z", r) for r in order]
        parts[0], low = lax.optimization_barrier((parts[0], low))
        base = base_return(grid, plan, tiles, low)
        *parts, one, two, base = lax.optimization_barrier((*parts, one, two, base))
        base = (base + widen(one) + widen(two)).reshape(shape)
        corner = narrow(here + sum(widen(part) for part in parts))
    else:
        total = jnp.concatenate([base_return(grid, plan, tiles, low), rest[0]])
        total = total.reshape((wide, 2) + shape)
        total = total[:, 0] + widen(grid.send(narrow(total[:, 1]), "x", 1))
        base = total[0]
        for r in range(1, wide):
            base = base + widen(grid.send(narrow(total[r]), "y", r))
        corner = None
    parts = [narrow(base[depth - r]) for r in order]
    if corner is not None:
        *parts, corner = lax.optimization_barrier((*parts, corner))
        diagonal = widen(grid.send(corner, BOTH_AXES, 1))
    gram = base[0] + diagonal
    for r, part in zip(order, parts):
        gram = gram + widen(grid.send(part, "z", r))
    return gram


def plan_kernel(near, area, pose, point, valid, out):
    tiles, slots = area.shape[1], out.shape[1]
    row_id = lax.broadcasted_iota(jnp.int32, (tiles, tiles), 0)
    col_id = lax.broadcasted_iota(jnp.int32, (tiles, tiles), 1)
    lane = lax.broadcasted_iota(jnp.int32, (tiles, slots), 1)

    def column(row):
        return jnp.sum(jnp.where(row_id == col_id, row, 0.0), axis=1, keepdims=True)

    def half_up(v, unit):
        whole = v.astype(jnp.int32) + (unit - 1)
        return (whole & ~(unit - 1)).astype(jnp.float32)

    def arrange(key, phase):
        key_col, phase_col = column(key), column(phase)
        same = jnp.where((key_col == key) & (real_col > 0.0) & (real > 0.0), 1.0, 0.0)
        count = jnp.sum(same, axis=0, keepdims=True)
        rank = jnp.sum(jnp.where(row_id < col_id, same, 0.0), axis=0, keepdims=True)
        rank_col = jnp.sum(jnp.where(col_id < row_id, same, 0.0), axis=1, keepdims=True)
        room = jnp.where((rank == 0.0) & (real > 0.0), half_up(count, 2), 0.0)
        place = jnp.sum(jnp.where(key < key_col, room, 0.0), axis=1, keepdims=True) + rank_col
        end, gap, bounds = 0.0, 0.0, []
        for k in range(AREAS):
            used = jnp.sum(jnp.where(phase == k, room, 0.0), axis=1, keepdims=True)
            place = place + jnp.where(phase_col == k, gap, 0.0)
            padded = half_up(used, 2 * UNROLL)
            end, gap = end + padded, gap + padded - used
            bounds.append(end)
        place = jnp.where(real_col > 0.0, place, -1.0)
        return jnp.where(place.astype(jnp.int32) == lane, 1.0, 0.0), bounds

    def pick(hit, values):
        return jnp.sum(hit * values, axis=0, keepdims=True)

    real = valid[...].astype(jnp.float32)
    real_col = column(real)
    area_row = area[...].astype(jnp.float32)
    pose_row = pose[...].astype(jnp.float32)
    point_row = point[...].astype(jnp.float32)
    pose_col, point_col = column(pose_row), column(point_row)
    tile_col = column(col_id[:1].astype(jnp.float32))
    points = CORES * PT_DEV
    hit, ends = arrange(area_row * points + point_row, area_row)
    rows = [
        pick(hit, tile_col),
        pick(hit, pose_col),
        pick(hit, jnp.ones_like(tile_col)),
        pick(hit, point_col),
    ]
    turned = AREAS - 1.0 - area_row
    hit, bounds = arrange(turned * 65536.0 + pose_row, turned)
    rows += [
        pick(hit, tile_col),
        pick(hit, point_col - points) + points,
        pick(hit, pose_col),
    ]
    ends += bounds
    spot = lane[:1]
    tail = jnp.zeros_like(rows[0])
    for k, end in enumerate(ends):
        tail = jnp.where(spot == k, end * (0.5 / UNROLL), tail)
    for k in range(near.shape[0]):
        tail = jnp.where(spot == NEAR + k, near[k].astype(jnp.float32), tail)
    for k, row in enumerate(rows + [tail]):
        out[k : k + 1] = row.astype(jnp.int32)


def make_plan(grid, place, near, indices):
    pose, point, valid = indices
    tiles = pose.shape[0]
    area, pose = grid.spot(pose, place)
    slots = tiles + max(AREAS * CORES * PT_DEV, min(tiles, 2 * grid.count)) + 2 * AREAS * UNROLL
    slots = -(-slots // 128) * 128
    rows = [v.reshape(1, tiles) for v in (area, pose, point, valid)]
    vmem = pl.BlockSpec(memory_space=pltpu.VMEM)
    return pl.pallas_call(
        plan_kernel,
        out_shape=jax.ShapeDtypeStruct((8, slots), jnp.int32),
        in_specs=[pl.BlockSpec(memory_space=pltpu.SMEM)] + [vmem] * 4,
        out_specs=vmem,
        compiler_params=pltpu.CompilerParams(vmem_limit_bytes=32 * tiles * slots + 2 * 1024 * 1024),
    )(near, *rows)


def join_kernel(first, second, out, sems):
    half = first.shape[0]
    copies = [
        pltpu.make_async_copy(first, out.at[pl.ds(0, half)], sems.at[0]),
        pltpu.make_async_copy(second, out.at[pl.ds(half, half)], sems.at[1]),
    ]
    for copy in copies:
        copy.start()
    for copy in copies:
        copy.wait()


def join_tiles(first, second):
    shape = (2 * first.shape[0], *first.shape[1:])
    return pl.pallas_call(
        join_kernel,
        out_shape=jax.ShapeDtypeStruct(shape, first.dtype),
        in_specs=[pl.BlockSpec(memory_space=pl.ANY)] * 2,
        out_specs=pl.BlockSpec(memory_space=pltpu.VMEM),
        scratch_shapes=[pltpu.SemaphoreType.DMA((2,))],
        compiler_params=pltpu.CompilerParams(vmem_limit_bytes=2 * 1024 * 1024),
    )(first, second)


NT = (((1,), (1,)), ((), ()))
NN = (((1,), (0,)), ((), ()))
F_TILE, F_POSE, F_REAL, F_POINT, B_TILE, B_POINT, B_POSE, ENDS = range(8)


def forward(plan, tiles, field, acc, begin, end):
    def body(i, _):
        for u in range(UNROLL):
            j = 2 * (i * UNROLL + u)
            block = [
                field[plan[F_POSE, j + h], : acc.shape[1]]
                * plan[F_REAL, j + h].astype(jnp.float32).astype(jnp.bfloat16)
                for h in range(2)
            ]
            tile = [tiles[plan[F_TILE, j + h]] for h in range(2)]
            acc[plan[F_POINT, j]] += lax.dot_general(
                jnp.concatenate(block, axis=1),
                jnp.concatenate(tile, axis=1),
                NT,
                preferred_element_type=jnp.float32,
            )
        return 0

    lax.fori_loop(begin, end, body, 0)


def backward(plan, tiles, low, total, begin, end):
    def body(i, _):
        for u in range(UNROLL):
            j = 2 * (i * UNROLL + u)
            block = [low[plan[B_POINT, j + h]] for h in range(2)]
            tile = [tiles[plan[B_TILE, j + h]] for h in range(2)]
            total[plan[B_POSE, j]] += lax.dot_general(
                jnp.concatenate(block, axis=1),
                jnp.concatenate(tile, axis=0),
                NN,
                preferred_element_type=jnp.float32,
            )
        return 0

    lax.fori_loop(begin, end, body, 0)


def assemble(pieces, field):
    start = 0
    for piece in pieces:
        field[start : start + piece.shape[0]] = piece[...]
        start += piece.shape[0]


def near_side(plan, field, sides, area):
    for side in range(sides.shape[0]):
        spot = NEAR + 2 * side

        @pl.when(plan[ENDS, spot] == area)
        def _():
            sides[side] = field[pl.ds(plan[ENDS, spot + 1], 2)]


def base_forward(plan_in, tiles, field, acc, sides, plan, sem):
    copy = pltpu.make_async_copy(plan_in, plan, sem)
    copy.start()
    acc[...] = jnp.zeros_like(acc)
    sides[...] = jnp.zeros_like(sides)
    copy.wait()
    near_side(plan, field, sides, 0)
    forward(plan, tiles, field, acc, 0, plan[ENDS, 0])


def rest_both(cuts, plan_in, tiles, part, sides_in, *refs):
    pieces, refs = refs[: -len(cuts) - 7], refs[-len(cuts) - 7 :]
    (acc, sides, low), outs, (field, total, plan, sem) = refs[:3], refs[3:-4], refs[-4:]
    copy = pltpu.make_async_copy(plan_in, plan, sem)
    copy.start()
    assemble(pieces, field)
    total[...] = jnp.zeros_like(total)
    acc[...] = part[...]
    sides[...] = sides_in[...]
    points = acc.shape[0]
    low[points] = jnp.zeros(low.shape[1:], jnp.bfloat16)
    copy.wait()
    near_side(plan, field, sides, 1)
    forward(plan, tiles, field, acc, plan[ENDS, 0], plan[ENDS, 1])
    low[:points] = acc[...].astype(jnp.bfloat16)
    backward(plan, tiles, low, total, 0, plan[ENDS, AREAS])
    start = 0
    for size, out in zip(cuts, outs):
        out[...] = total[start : start + size].astype(out.dtype)
        start += size


def base_backward(plan_in, tiles, low, base, plan, sem):
    copy = pltpu.make_async_copy(plan_in, plan, sem)
    copy.start()
    base[...] = jnp.zeros_like(base)
    copy.wait()
    backward(plan, tiles, low, base, plan[ENDS, AREAS], plan[ENDS, AREAS + 1])


def call(kernel, outs, scratch, args, kinds, tiles, share, aliases={}):
    place = {
        "a": pl.BlockSpec(memory_space=pl.ANY),
        "v": pl.BlockSpec(memory_space=pltpu.VMEM),
    }
    size = sum(math.prod(v.shape) * jnp.dtype(v.dtype).itemsize for v in scratch)
    scratch = scratch + [pltpu.SMEM(args[0].shape, jnp.int32), pltpu.SemaphoreType.DMA]
    return pl.pallas_call(
        kernel,
        out_shape=outs,
        in_specs=[place[kind] for kind in kinds],
        out_specs=[place["v"]] * len(outs),
        scratch_shapes=scratch,
        input_output_aliases=aliases,
        compiler_params=pltpu.CompilerParams(vmem_limit_bytes=size + 3 * 1024 * 1024),
        cost_estimate=pl.CostEstimate(
            flops=int(share * 4 * tiles.size * 128),
            bytes_accessed=tiles.size * 2,
            transcendentals=0,
        ),
    )(*args)


def array(lead, like, kind):
    return jax.ShapeDtypeStruct((lead, *like[1:]), kind)


def base_product(plan, tiles, base):
    rows = tiles.shape[1] // CORES
    acc = (0, rows, tiles.shape[1])
    return call(
        base_forward,
        [
            array(CORES * PT_DEV, acc, jnp.float32),
            jax.ShapeDtypeStruct((2 * CORES, 2, *base.shape[1:]), jnp.bfloat16),
        ],
        [],
        [plan, tiles, base],
        "avv",
        tiles,
        0.125,
    )


def rest_product(grid, plan, tiles, sums, pieces):
    plane = grid.plane
    rest = 2 * grid.count - plane
    if grid.sizes["y"] == 2:
        group = 2 * CORES
        cuts = [plane, plane, group] + [group] * (grid.sizes["z"] - 1)
        kinds = [jnp.bfloat16, jnp.bfloat16, jnp.float32] + [jnp.bfloat16] * (grid.sizes["z"] - 1)
    else:
        cuts, kinds = [rest], [jnp.float32]
    rows, points = sums[0].shape[1:]
    like = (0, rows, tiles.shape[2])
    _, sides, low, *outs = call(
        functools.partial(rest_both, cuts),
        [
            *[jax.ShapeDtypeStruct(v.shape, v.dtype) for v in sums],
            array(CORES * PT_DEV + 1, (0, rows, points), jnp.bfloat16),
            *[array(cut, like, kind) for cut, kind in zip(cuts, kinds)],
        ],
        [pltpu.VMEM((rest, *pieces[0].shape[1:]), jnp.bfloat16), pltpu.VMEM((rest, *like[1:]), jnp.float32)],
        [plan, tiles, *sums, *pieces],
        "avvv" + "v" * len(pieces),
        tiles,
        0.75,
        {2: 0, 3: 1},
    )
    return outs, low, sides


def base_return(grid, plan, tiles, low):
    (base,) = call(
        base_backward,
        [array(grid.plane, (0, low.shape[1], tiles.shape[2]), jnp.float32)],
        [],
        [plan, tiles, low],
        "avv",
        tiles,
        0.125,
    )
    return base


def in_order(core, mine, theirs, axis):
    low, high = jnp.where(core == 0, mine, theirs), jnp.where(core == 0, theirs, mine)
    return jnp.concatenate([low, high], axis=axis)


def on_device(jac_tiles, tile_pose, tile_point, tile_valid, prior_weight, right_side):
    grid = Grid()
    place = lax.axis_index(BOTH)
    at = grid.coords(place)
    core = at["core"]
    homes = [grid.device(at | {"core": c}) for c in range(CORES)]
    params, rhs = right_side.shape[1:]
    rows = rhs // CORES

    def half(v, which):
        return lax.dynamic_slice_in_dim(v, which * rows, rows, 1)

    def whole(*values):
        v = jnp.stack(values).reshape((-1, CORES, 2) + values[0].shape[1:])
        mine = lax.dynamic_index_in_dim(v, core, 1, keepdims=False)
        theirs = grid.swap(lax.dynamic_index_in_dim(v, 1 - core, 1, keepdims=False))
        return tuple(jnp.swapaxes(in_order(core, mine, theirs, 2), 2, 3))

    turned = jnp.swapaxes(right_side, 1, 2)
    names = jnp.stack([tile_pose, tile_point, tile_valid]).astype(jnp.float32)
    width = -(-names.shape[1] // params)
    names = jnp.pad(names, ((0, 0), (0, width * params - names.shape[1])))
    extra = jnp.concatenate([prior_weight, names.reshape(3 * width, params)])
    extra = jnp.pad(extra, ((0, -extra.shape[0] % 16), (0, 0))).reshape(2, -1, params)
    pack = lax.optimization_barrier(jnp.concatenate([half(turned, 1 - core), extra], axis=1))
    other_tiles = grid.swap(jac_tiles)
    theirs = grid.swap(pack)
    right_side = in_order(core, half(turned, core), theirs[:, :rows], 0)
    notes = [v[:, rows:].reshape(-1, params) for v in (pack, theirs)]
    weights = in_order(core, notes[0][:2], notes[1][:2], 0)
    names = [v[2 : 2 + 3 * width].reshape(3, -1)[:, : tile_pose.shape[0]] for v in notes]
    shift = jnp.array([[0.0], [PT_DEV], [0.0]], jnp.float32)
    indices = jnp.concatenate([names[0], names[1] + shift], axis=1).astype(jnp.int32)
    near = []
    for home in homes:
        near += grid.spot(2 * jnp.maximum(home - 1, 0), place)
        near += grid.spot(2 * jnp.minimum(home + 1, grid.count - 1), place)
    plan = make_plan(grid, place, jnp.stack(near), indices)
    tiles = None

    def load():
        return join_tiles(jac_tiles, other_tiles) if tiles is None else tiles

    zero = jnp.zeros((params,), jnp.float32)
    theta = (highest + lowest) / 2.0
    delta = (highest - lowest) / 2.0
    sigma = theta / delta
    ratio = 1.0 / sigma
    step = right_side / theta
    solution = jnp.zeros(right_side.shape, jnp.float32)
    residual = right_side
    for turn in range(ITERS):
        if turn > 0:
            new_ratio = 1.0 / (2.0 * sigma - ratio)
            step = new_ratio * ratio * step + 2.0 * new_ratio / delta * residual
            ratio = new_ratio
        solution = solution + step
        low = step.astype(jnp.bfloat16)
        if turn == 0:
            extra = jnp.broadcast_to(weights[:, None, :], (2 * CORES, 16, params))
            low = jnp.concatenate([low, extra.astype(jnp.bfloat16)], axis=1)
        sums, pieces, plan, tiles = gather_field(grid, low, plan, load)
        rest, point_sums, sides = rest_product(grid, plan, tiles, sums, pieces)
        gram = scatter_sum(grid, plan, tiles, rest, point_sums)
        sides = sides.astype(jnp.float32)
        if turn == 0:
            w_left, w_right = [], []
            for c, home in enumerate(homes):
                first, last = home == 0, home == grid.count - 1
                left, right = sides[2 * c, :, rows], sides[2 * c + 1, :, rows]
                one, two = weights[2 * c], weights[2 * c + 1]
                w_left += [jnp.where(first, zero, left[0]), jnp.where(first, zero, two)]
                w_right += [one, jnp.where(last, one, right[1])]
            w_left = jnp.stack(w_left)[:, None, :]
            w_right = jnp.stack(w_right)[:, None, :]
        left = jnp.concatenate([sides[2 * c, :, :rows] for c in range(CORES)])
        right = []
        for c, home in enumerate(homes):
            turned = step[2 * c : 2 * c + 2][::-1]
            right.append(jnp.where(home == grid.count - 1, turned, sides[2 * c + 1, :, :rows]))
        prior = w_left * (step - left) + w_right * (step - jnp.concatenate(right))
        residual = residual - (gram + prior + damping * step)
    return whole(solution, residual)


def solution(mesh):
    return jax.shard_map(
        on_device,
        mesh=mesh,
        in_specs=(
            P(BOTH, None, None),
            P(BOTH),
            P(BOTH),
            P(BOTH),
            P(BOTH, None),
            P(BOTH, None, None),
        ),
        out_specs=(P(BOTH, None, None), P(BOTH, None, None)),
        check_vma=False,
    )
```

```python
import functools
import math

import jax
import jax.numpy as jnp
from jax import lax
from jax.experimental import pallas as pl
from jax.experimental.pallas import tpu as pltpu
from jax.sharding import PartitionSpec as P

PT_DEV = 16
ITERS = 3
CORES = 2
UNROLL = 16
AREAS = 2
NEAR = 2 * AREAS

damping = 0.5
lowest = 0.5
highest = 8.0
BOTH = ("row", "col")
ONE, TWO, BOTH_AXES = ("x", "y"), ("y", "x"), "x y"


class Grid:
    def __init__(self):
        rows = lax.axis_size("row")
        cols = lax.axis_size("col")
        self.sizes = {"y": rows // CORES, "core": CORES, "z": cols // 2, "x": 2}
        self.count = rows * cols
        self.plane = self.sizes["z"] * CORES * 2

    def coords(self, device):
        cols = self.sizes["z"] * 2
        if isinstance(device, int):
            row, col = device // cols, device % cols
            return {"y": row // 2, "core": row % 2, "z": col // 2, "x": col % 2}
        row, col = lax.div(device, cols), lax.rem(device, cols)
        return {"y": lax.div(row, 2), "core": lax.rem(row, 2), "z": lax.div(col, 2), "x": lax.rem(col, 2)}

    def device(self, at):
        row = at["y"] * 2 + at["core"]
        col = at["z"] * 2 + at["x"]
        return row * self.sizes["z"] * 2 + col

    def spot(self, pose, home):
        at, base = self.coords(lax.div(pose, 2)), self.coords(home)
        away = {a: lax.rem(at[a] - base[a] + n, n) for a, n in self.sizes.items()}
        x, y, z = away["x"], away["y"], at["z"] ^ base["z"]
        if self.sizes["y"] == 2:
            swap = base["core"] == 1
            x, y = jnp.where(swap, y, x), jnp.where(swap, x, y)
        z = jnp.where(z == 0, 0, self.sizes["z"] - z)
        chip = (y * 2 + x) * self.sizes["z"] + z
        spot = (chip * CORES + at["core"]) * 2 + lax.rem(pose, 2)
        area = jnp.where(spot < self.plane, 0, 1)
        return area, spot - area * self.plane

    def send(self, block, axes, distance):
        route = []
        for source in range(self.count):
            at = self.coords(source)
            names = axes if isinstance(axes, str) else axes[at["core"]]
            for name in names.split():
                moved = (at[name] + distance) % self.sizes[name]
                at[name] = at[name] ^ distance if name == "z" else moved
            route.append((source, self.device(at)))
        return lax.ppermute(block, BOTH, route)

    def fetch(self, block, axes, distance):
        return self.send(block, axes, -distance)

    def swap(self, block):
        return self.send(block, "core", 1)


def along_z(grid, block, beside=None):
    depth = grid.sizes["z"]
    moved = [grid.send(block, "z", r) for r in range(1, depth)]
    if beside is not None:
        moved[-1], beside = lax.optimization_barrier((moved[-1], beside))
    return jnp.concatenate([block] + moved[::-1]), beside


def gather_field(grid, low, plan, load):
    wide = grid.sizes["y"]
    if wide == 2:
        base, corner = along_z(grid, low, grid.send(low, BOTH_AXES, 1))
        base, corner, plan = lax.optimization_barrier((base, corner, plan))
        tiles = load()
        sums = base_product(plan, tiles, base)
        over = [grid.send(base, axes, 1) for axes in (ONE, TWO)]
        far, _ = along_z(grid, corner)
        far, *sums = lax.optimization_barrier((far, *sums))
        pieces = [*over, far]
    else:
        base, _ = along_z(grid, low)
        base, plan = lax.optimization_barrier((base, plan))
        tiles = load()
        sums = base_product(plan, tiles, base)
        lines = [base] + [grid.fetch(base, "y", r) for r in range(1, wide)]
        pieces = []
        for line in lines:
            pieces += [line, grid.fetch(line, "x", 1)]
        pieces = pieces[1:]
    return sums, pieces, plan, tiles


def scatter_sum(grid, plan, tiles, rest, low):
    depth, wide = grid.sizes["z"], grid.sizes["y"]
    order = range(depth - 1, 0, -1)
    shape = (depth, 2 * CORES, low.shape[1], tiles.shape[2])

    def narrow(v):
        return v.astype(jnp.bfloat16)

    def widen(v):
        return v.astype(jnp.float32)

    diagonal = jnp.zeros((), jnp.float32)
    if wide == 2:
        one, two, here, *parts = rest
        one, two, *parts = lax.optimization_barrier((one, two, *parts))
        one, two = grid.send(one, ONE, 1), grid.send(two, TWO, 1)
        parts = [grid.send(parts[depth - r - 1], "z", r) for r in order]
        parts[0], low = lax.optimization_barrier((parts[0], low))
        base = base_return(grid, plan, tiles, low)
        *parts, one, two, base = lax.optimization_barrier((*parts, one, two, base))
        base = (base + widen(one) + widen(two)).reshape(shape)
        corner = narrow(here + sum(widen(part) for part in parts))
    else:
        total = jnp.concatenate([base_return(grid, plan, tiles, low), rest[0]])
        total = total.reshape((wide, 2) + shape)
        total = total[:, 0] + widen(grid.send(narrow(total[:, 1]), "x", 1))
        base = total[0]
        for r in range(1, wide):
            base = base + widen(grid.send(narrow(total[r]), "y", r))
        corner = None
    parts = [narrow(base[depth - r]) for r in order]
    if corner is not None:
        *parts, corner = lax.optimization_barrier((*parts, corner))
        diagonal = grid.send(corner, BOTH_AXES, 1)
    parts = [grid.send(part, "z", r) for r, part in zip(order, parts)]
    if corner is not None:
        parts[0], diagonal = lax.optimization_barrier((parts[0], diagonal))
    gram = base[0] + widen(diagonal)
    for part in parts:
        gram = gram + widen(part)
    return gram


def plan_kernel(near, area, pose, point, valid, out):
    tiles, slots = area.shape[1], out.shape[1]
    row_id = lax.broadcasted_iota(jnp.int32, (tiles, tiles), 0)
    col_id = lax.broadcasted_iota(jnp.int32, (tiles, tiles), 1)
    lane = lax.broadcasted_iota(jnp.int32, (tiles, slots), 1)

    def column(row):
        return jnp.sum(jnp.where(row_id == col_id, row, 0.0), axis=1, keepdims=True)

    def half_up(v, unit):
        whole = v.astype(jnp.int32) + (unit - 1)
        return (whole & ~(unit - 1)).astype(jnp.float32)

    def arrange(key, phase):
        key_col, phase_col = column(key), column(phase)
        same = jnp.where((key_col == key) & (real_col > 0.0) & (real > 0.0), 1.0, 0.0)
        count = jnp.sum(same, axis=0, keepdims=True)
        rank = jnp.sum(jnp.where(row_id < col_id, same, 0.0), axis=0, keepdims=True)
        rank_col = jnp.sum(jnp.where(col_id < row_id, same, 0.0), axis=1, keepdims=True)
        room = jnp.where((rank == 0.0) & (real > 0.0), half_up(count, 2), 0.0)
        place = jnp.sum(jnp.where(key < key_col, room, 0.0), axis=1, keepdims=True) + rank_col
        end, gap, bounds = 0.0, 0.0, []
        for k in range(AREAS):
            used = jnp.sum(jnp.where(phase == k, room, 0.0), axis=1, keepdims=True)
            place = place + jnp.where(phase_col == k, gap, 0.0)
            padded = half_up(used, 2 * UNROLL)
            end, gap = end + padded, gap + padded - used
            bounds.append(end)
        place = jnp.where(real_col > 0.0, place, -1.0)
        return jnp.where(place.astype(jnp.int32) == lane, 1.0, 0.0), bounds

    def pick(hit, values):
        return jnp.sum(hit * values, axis=0, keepdims=True)

    real = valid[...].astype(jnp.float32)
    real_col = column(real)
    area_row = area[...].astype(jnp.float32)
    pose_row = pose[...].astype(jnp.float32)
    point_row = point[...].astype(jnp.float32)
    pose_col, point_col = column(pose_row), column(point_row)
    tile_col = column(col_id[:1].astype(jnp.float32))
    points = CORES * PT_DEV
    hit, ends = arrange(area_row * points + point_row, area_row)
    rows = [
        pick(hit, tile_col),
        pick(hit, pose_col),
        pick(hit, jnp.ones_like(tile_col)),
        pick(hit, point_col),
    ]
    turned = AREAS - 1.0 - area_row
    hit, bounds = arrange(turned * 65536.0 + pose_row, turned)
    rows += [
        pick(hit, tile_col),
        pick(hit, point_col - points) + points,
        pick(hit, pose_col),
    ]
    ends += bounds
    spot = lane[:1]
    tail = jnp.zeros_like(rows[0])
    for k, end in enumerate(ends):
        tail = jnp.where(spot == k, end * (0.5 / UNROLL), tail)
    for k in range(near.shape[0]):
        tail = jnp.where(spot == NEAR + k, near[k].astype(jnp.float32), tail)
    for k, row in enumerate(rows + [tail]):
        out[k : k + 1] = row.astype(jnp.int32)


def make_plan(grid, place, near, indices):
    pose, point, valid = indices
    tiles = pose.shape[0]
    area, pose = grid.spot(pose, place)
    slots = tiles + max(AREAS * CORES * PT_DEV, min(tiles, 2 * grid.count)) + 2 * AREAS * UNROLL
    slots = -(-slots // 128) * 128
    rows = [v.reshape(1, tiles) for v in (area, pose, point, valid)]
    vmem = pl.BlockSpec(memory_space=pltpu.VMEM)
    return pl.pallas_call(
        plan_kernel,
        out_shape=jax.ShapeDtypeStruct((8, slots), jnp.int32),
        in_specs=[pl.BlockSpec(memory_space=pltpu.SMEM)] + [vmem] * 4,
        out_specs=vmem,
        compiler_params=pltpu.CompilerParams(vmem_limit_bytes=32 * tiles * slots + 2 * 1024 * 1024),
    )(near, *rows)


def join_kernel(first, second, out, sems):
    half = first.shape[0]
    copies = [
        pltpu.make_async_copy(first, out.at[pl.ds(0, half)], sems.at[0]),
        pltpu.make_async_copy(second, out.at[pl.ds(half, half)], sems.at[1]),
    ]
    for copy in copies:
        copy.start()
    for copy in copies:
        copy.wait()


def join_tiles(first, second):
    shape = (2 * first.shape[0], *first.shape[1:])
    return pl.pallas_call(
        join_kernel,
        out_shape=jax.ShapeDtypeStruct(shape, first.dtype),
        in_specs=[pl.BlockSpec(memory_space=pl.ANY)] * 2,
        out_specs=pl.BlockSpec(memory_space=pltpu.VMEM),
        scratch_shapes=[pltpu.SemaphoreType.DMA((2,))],
        compiler_params=pltpu.CompilerParams(vmem_limit_bytes=2 * 1024 * 1024),
    )(first, second)


NT = (((1,), (1,)), ((), ()))
NN = (((1,), (0,)), ((), ()))
F_TILE, F_POSE, F_REAL, F_POINT, B_TILE, B_POINT, B_POSE, ENDS = range(8)


def forward(plan, tiles, field, acc, begin, end):
    def body(i, _):
        for u in range(UNROLL):
            j = 2 * (i * UNROLL + u)
            block = [
                field[plan[F_POSE, j + h], : acc.shape[1]]
                * plan[F_REAL, j + h].astype(jnp.float32).astype(jnp.bfloat16)
                for h in range(2)
            ]
            tile = [tiles[plan[F_TILE, j + h]] for h in range(2)]
            acc[plan[F_POINT, j]] += lax.dot_general(
                jnp.concatenate(block, axis=1),
                jnp.concatenate(tile, axis=1),
                NT,
                preferred_element_type=jnp.float32,
            )
        return 0

    lax.fori_loop(begin, end, body, 0)


def backward(plan, tiles, low, total, begin, end):
    def body(i, _):
        for u in range(UNROLL):
            j = 2 * (i * UNROLL + u)
            block = [low[plan[B_POINT, j + h]] for h in range(2)]
            tile = [tiles[plan[B_TILE, j + h]] for h in range(2)]
            total[plan[B_POSE, j]] += lax.dot_general(
                jnp.concatenate(block, axis=1),
                jnp.concatenate(tile, axis=0),
                NN,
                preferred_element_type=jnp.float32,
            )
        return 0

    lax.fori_loop(begin, end, body, 0)


def assemble(pieces, field):
    start = 0
    for piece in pieces:
        field[start : start + piece.shape[0]] = piece[...]
        start += piece.shape[0]


def near_side(plan, field, sides, area):
    for side in range(sides.shape[0]):
        spot = NEAR + 2 * side

        @pl.when(plan[ENDS, spot] == area)
        def _():
            sides[side] = field[pl.ds(plan[ENDS, spot + 1], 2)]


def base_forward(plan_in, tiles, field, acc, sides, plan, sem):
    copy = pltpu.make_async_copy(plan_in, plan, sem)
    copy.start()
    acc[...] = jnp.zeros_like(acc)
    sides[...] = jnp.zeros_like(sides)
    copy.wait()
    near_side(plan, field, sides, 0)
    forward(plan, tiles, field, acc, 0, plan[ENDS, 0])


def rest_both(cuts, plan_in, tiles, part, sides_in, *refs):
    pieces, refs = refs[: -len(cuts) - 7], refs[-len(cuts) - 7 :]
    (acc, sides, low), outs, (field, total, plan, sem) = refs[:3], refs[3:-4], refs[-4:]
    copy = pltpu.make_async_copy(plan_in, plan, sem)
    copy.start()
    assemble(pieces, field)
    total[...] = jnp.zeros_like(total)
    acc[...] = part[...]
    sides[...] = sides_in[...]
    points = acc.shape[0]
    low[points] = jnp.zeros(low.shape[1:], jnp.bfloat16)
    copy.wait()
    near_side(plan, field, sides, 1)
    forward(plan, tiles, field, acc, plan[ENDS, 0], plan[ENDS, 1])
    low[:points] = acc[...].astype(jnp.bfloat16)
    backward(plan, tiles, low, total, 0, plan[ENDS, AREAS])
    start = 0
    for size, out in zip(cuts, outs):
        out[...] = total[start : start + size].astype(out.dtype)
        start += size


def base_backward(plan_in, tiles, low, base, plan, sem):
    copy = pltpu.make_async_copy(plan_in, plan, sem)
    copy.start()
    base[...] = jnp.zeros_like(base)
    copy.wait()
    backward(plan, tiles, low, base, plan[ENDS, AREAS], plan[ENDS, AREAS + 1])


def call(kernel, outs, scratch, args, kinds, tiles, share, aliases={}):
    place = {
        "a": pl.BlockSpec(memory_space=pl.ANY),
        "v": pl.BlockSpec(memory_space=pltpu.VMEM),
    }
    size = sum(math.prod(v.shape) * jnp.dtype(v.dtype).itemsize for v in scratch)
    scratch = scratch + [pltpu.SMEM(args[0].shape, jnp.int32), pltpu.SemaphoreType.DMA]
    return pl.pallas_call(
        kernel,
        out_shape=outs,
        in_specs=[place[kind] for kind in kinds],
        out_specs=[place["v"]] * len(outs),
        scratch_shapes=scratch,
        input_output_aliases=aliases,
        compiler_params=pltpu.CompilerParams(vmem_limit_bytes=size + 3 * 1024 * 1024),
        cost_estimate=pl.CostEstimate(
            flops=int(share * 4 * tiles.size * 128),
            bytes_accessed=tiles.size * 2,
            transcendentals=0,
        ),
    )(*args)


def array(lead, like, kind):
    return jax.ShapeDtypeStruct((lead, *like[1:]), kind)


def base_product(plan, tiles, base):
    rows = tiles.shape[1] // CORES
    acc = (0, rows, tiles.shape[1])
    return call(
        base_forward,
        [
            array(CORES * PT_DEV, acc, jnp.float32),
            jax.ShapeDtypeStruct((2 * CORES, 2, *base.shape[1:]), jnp.bfloat16),
        ],
        [],
        [plan, tiles, base],
        "avv",
        tiles,
        0.125,
    )


def rest_product(grid, plan, tiles, sums, pieces):
    plane = grid.plane
    rest = 2 * grid.count - plane
    if grid.sizes["y"] == 2:
        group = 2 * CORES
        cuts = [plane, plane, group] + [group] * (grid.sizes["z"] - 1)
        kinds = [jnp.bfloat16, jnp.bfloat16, jnp.float32] + [jnp.bfloat16] * (grid.sizes["z"] - 1)
    else:
        cuts, kinds = [rest], [jnp.float32]
    rows, points = sums[0].shape[1:]
    like = (0, rows, tiles.shape[2])
    _, sides, low, *outs = call(
        functools.partial(rest_both, cuts),
        [
            *[jax.ShapeDtypeStruct(v.shape, v.dtype) for v in sums],
            array(CORES * PT_DEV + 1, (0, rows, points), jnp.bfloat16),
            *[array(cut, like, kind) for cut, kind in zip(cuts, kinds)],
        ],
        [pltpu.VMEM((rest, *pieces[0].shape[1:]), jnp.bfloat16), pltpu.VMEM((rest, *like[1:]), jnp.float32)],
        [plan, tiles, *sums, *pieces],
        "avvv" + "v" * len(pieces),
        tiles,
        0.75,
        {2: 0, 3: 1},
    )
    return outs, low, sides


def base_return(grid, plan, tiles, low):
    (base,) = call(
        base_backward,
        [array(grid.plane, (0, low.shape[1], tiles.shape[2]), jnp.float32)],
        [],
        [plan, tiles, low],
        "avv",
        tiles,
        0.125,
    )
    return base


def in_order(core, mine, theirs, axis):
    low, high = jnp.where(core == 0, mine, theirs), jnp.where(core == 0, theirs, mine)
    return jnp.concatenate([low, high], axis=axis)


def on_device(jac_tiles, tile_pose, tile_point, tile_valid, prior_weight, right_side):
    grid = Grid()
    place = lax.axis_index(BOTH)
    at = grid.coords(place)
    core = at["core"]
    homes = [grid.device(at | {"core": c}) for c in range(CORES)]
    params, rhs = right_side.shape[1:]
    rows = rhs // CORES

    def half(v, which):
        return lax.dynamic_slice_in_dim(v, which * rows, rows, 1)

    def whole(*values):
        v = jnp.stack(values).reshape((-1, CORES, 2) + values[0].shape[1:])
        mine = lax.dynamic_index_in_dim(v, core, 1, keepdims=False)
        theirs = grid.swap(lax.dynamic_index_in_dim(v, 1 - core, 1, keepdims=False))
        return tuple(jnp.swapaxes(in_order(core, mine, theirs, 2), 2, 3))

    turned = jnp.swapaxes(right_side, 1, 2)
    names = jnp.stack([tile_pose, tile_point, tile_valid]).astype(jnp.float32)
    width = -(-names.shape[1] // params)
    names = jnp.pad(names, ((0, 0), (0, width * params - names.shape[1])))
    extra = jnp.concatenate([prior_weight, names.reshape(3 * width, params)])
    extra = jnp.pad(extra, ((0, -extra.shape[0] % 16), (0, 0))).reshape(2, -1, params)
    pack = lax.optimization_barrier(jnp.concatenate([half(turned, 1 - core), extra], axis=1))
    other_tiles = grid.swap(jac_tiles)
    theirs = grid.swap(pack)
    right_side = in_order(core, half(turned, core), theirs[:, :rows], 0)
    notes = [v[:, rows:].reshape(-1, params) for v in (pack, theirs)]
    weights = in_order(core, notes[0][:2], notes[1][:2], 0)
    names = [v[2 : 2 + 3 * width].reshape(3, -1)[:, : tile_pose.shape[0]] for v in notes]
    shift = jnp.array([[0.0], [PT_DEV], [0.0]], jnp.float32)
    indices = jnp.concatenate([names[0], names[1] + shift], axis=1).astype(jnp.int32)
    near = []
    for home in homes:
        near += grid.spot(2 * jnp.maximum(home - 1, 0), place)
        near += grid.spot(2 * jnp.minimum(home + 1, grid.count - 1), place)
    plan = make_plan(grid, place, jnp.stack(near), indices)
    tiles = None

    def load():
        return join_tiles(jac_tiles, other_tiles) if tiles is None else tiles

    zero = jnp.zeros((params,), jnp.float32)
    theta = (highest + lowest) / 2.0
    delta = (highest - lowest) / 2.0
    sigma = theta / delta
    ratio = 1.0 / sigma
    step = right_side / theta
    solution = jnp.zeros(right_side.shape, jnp.float32)
    residual = right_side
    for turn in range(ITERS):
        if turn > 0:
            new_ratio = 1.0 / (2.0 * sigma - ratio)
            step = new_ratio * ratio * step + 2.0 * new_ratio / delta * residual
            ratio = new_ratio
        solution = solution + step
        low = step.astype(jnp.bfloat16)
        if turn == 0:
            extra = jnp.broadcast_to(weights[:, None, :], (2 * CORES, 16, params))
            low = jnp.concatenate([low, extra.astype(jnp.bfloat16)], axis=1)
        sums, pieces, plan, tiles = gather_field(grid, low, plan, load)
        rest, point_sums, sides = rest_product(grid, plan, tiles, sums, pieces)
        gram = scatter_sum(grid, plan, tiles, rest, point_sums)
        sides = sides.astype(jnp.float32)
        if turn == 0:
            w_left, w_right = [], []
            for c, home in enumerate(homes):
                first, last = home == 0, home == grid.count - 1
                left, right = sides[2 * c, :, rows], sides[2 * c + 1, :, rows]
                one, two = weights[2 * c], weights[2 * c + 1]
                w_left += [jnp.where(first, zero, left[0]), jnp.where(first, zero, two)]
                w_right += [one, jnp.where(last, one, right[1])]
            w_left = jnp.stack(w_left)[:, None, :]
            w_right = jnp.stack(w_right)[:, None, :]
        left = jnp.concatenate([sides[2 * c, :, :rows] for c in range(CORES)])
        right = []
        for c, home in enumerate(homes):
            turned = step[2 * c : 2 * c + 2][::-1]
            right.append(jnp.where(home == grid.count - 1, turned, sides[2 * c + 1, :, :rows]))
        prior = w_left * (step - left) + w_right * (step - jnp.concatenate(right))
        residual = residual - (gram + prior + damping * step)
    return whole(solution, residual)


def solution(mesh):
    return jax.shard_map(
        on_device,
        mesh=mesh,
        in_specs=(
            P(BOTH, None, None),
            P(BOTH),
            P(BOTH),
            P(BOTH),
            P(BOTH, None),
            P(BOTH, None, None),
        ),
        out_specs=(P(BOTH, None, None), P(BOTH, None, None)),
        check_vma=False,
    )
```

```python
import functools
import math

import jax
import jax.numpy as jnp
from jax import lax
from jax.experimental import pallas as pl
from jax.experimental.pallas import tpu as pltpu
from jax.sharding import PartitionSpec as P

PT_DEV = 16
ITERS = 3
CORES = 2
UNROLL = 16
AREAS = 2
NEAR = 2 * AREAS

damping = 0.5
lowest = 0.5
highest = 8.0
BOTH = ("row", "col")
ONE, TWO, BOTH_AXES = ("x", "y"), ("y", "x"), "x y"


class Grid:
    def __init__(self):
        rows = lax.axis_size("row")
        cols = lax.axis_size("col")
        self.sizes = {"y": rows // CORES, "core": CORES, "z": cols // 2, "x": 2}
        self.count = rows * cols
        self.plane = self.sizes["z"] * CORES * 2

    def coords(self, device):
        cols = self.sizes["z"] * 2
        if isinstance(device, int):
            row, col = device // cols, device % cols
            return {"y": row // 2, "core": row % 2, "z": col // 2, "x": col % 2}
        row, col = lax.div(device, cols), lax.rem(device, cols)
        return {"y": lax.div(row, 2), "core": lax.rem(row, 2), "z": lax.div(col, 2), "x": lax.rem(col, 2)}

    def device(self, at):
        row = at["y"] * 2 + at["core"]
        col = at["z"] * 2 + at["x"]
        return row * self.sizes["z"] * 2 + col

    def spot(self, pose, home):
        at, base = self.coords(lax.div(pose, 2)), self.coords(home)
        away = {a: lax.rem(at[a] - base[a] + n, n) for a, n in self.sizes.items()}
        x, y, z = away["x"], away["y"], at["z"] ^ base["z"]
        if self.sizes["y"] == 2:
            swap = base["core"] == 1
            x, y = jnp.where(swap, y, x), jnp.where(swap, x, y)
        z = jnp.where(z == 0, 0, self.sizes["z"] - z)
        chip = (y * 2 + x) * self.sizes["z"] + z
        spot = (chip * CORES + at["core"]) * 2 + lax.rem(pose, 2)
        area = jnp.where(spot < self.plane, 0, 1)
        return area, spot - area * self.plane

    def send(self, block, axes, distance):
        route = []
        for source in range(self.count):
            at = self.coords(source)
            names = axes if isinstance(axes, str) else axes[at["core"]]
            for name in names.split():
                moved = (at[name] + distance) % self.sizes[name]
                at[name] = at[name] ^ distance if name == "z" else moved
            route.append((source, self.device(at)))
        return lax.ppermute(block, BOTH, route)

    def fetch(self, block, axes, distance):
        return self.send(block, axes, -distance)

    def swap(self, block):
        return self.send(block, "core", 1)


def along_z(grid, block, beside=None):
    depth = grid.sizes["z"]
    moved = [grid.send(block, "z", r) for r in range(1, depth)]
    if beside is not None:
        moved[-1], beside = lax.optimization_barrier((moved[-1], beside))
    return jnp.concatenate([block] + moved[::-1]), beside


def gather_field(grid, low, plan, load, *held):
    wide = grid.sizes["y"]
    if wide == 2:
        base, corner = along_z(grid, low, grid.send(low, BOTH_AXES, 1))
        base, corner, plan, *held = lax.optimization_barrier((base, corner, plan, *held))
        tiles = load(*held)
        sums = base_product(plan, tiles, base)
        over = [grid.send(base, axes, 1) for axes in (ONE, TWO)]
        far, _ = along_z(grid, corner)
        far, *sums = lax.optimization_barrier((far, *sums))
        pieces = [*over, far]
    else:
        base, _ = along_z(grid, low)
        base, plan, *held = lax.optimization_barrier((base, plan, *held))
        tiles = load(*held)
        sums = base_product(plan, tiles, base)
        lines = [base] + [grid.fetch(base, "y", r) for r in range(1, wide)]
        pieces = []
        for line in lines:
            pieces += [line, grid.fetch(line, "x", 1)]
        pieces = pieces[1:]
    return sums, pieces, plan, tiles


def scatter_sum(grid, plan, tiles, rest, low):
    depth, wide = grid.sizes["z"], grid.sizes["y"]
    order = range(depth - 1, 0, -1)
    shape = (depth, 2 * CORES, low.shape[1], tiles.shape[2])

    def narrow(v):
        return v.astype(jnp.bfloat16)

    def widen(v):
        return v.astype(jnp.float32)

    diagonal = jnp.zeros((), jnp.float32)
    if wide == 2:
        one, two, here, *parts = rest
        one, two, *parts = lax.optimization_barrier((one, two, *parts))
        one, two = grid.send(one, ONE, 1), grid.send(two, TWO, 1)
        parts = [grid.send(parts[depth - r - 1], "z", r) for r in order]
        parts[0], low = lax.optimization_barrier((parts[0], low))
        base = base_return(grid, plan, tiles, low)
        *parts, one, two, base = lax.optimization_barrier((*parts, one, two, base))
        base = (base + widen(one) + widen(two)).reshape(shape)
        corner = narrow(here + sum(widen(part) for part in parts))
    else:
        total = jnp.concatenate([base_return(grid, plan, tiles, low), rest[0]])
        total = total.reshape((wide, 2) + shape)
        total = total[:, 0] + widen(grid.send(narrow(total[:, 1]), "x", 1))
        base = total[0]
        for r in range(1, wide):
            base = base + widen(grid.send(narrow(total[r]), "y", r))
        corner = None
    parts = [narrow(base[depth - r]) for r in order]
    if corner is not None:
        *parts, corner = lax.optimization_barrier((*parts, corner))
        diagonal = grid.send(corner, BOTH_AXES, 1)
    parts = [grid.send(part, "z", r) for r, part in zip(order, parts)]
    if corner is not None:
        parts[0], diagonal = lax.optimization_barrier((parts[0], diagonal))
    gram = base[0] + widen(diagonal)
    for part in parts:
        gram = gram + widen(part)
    return gram


def plan_kernel(near, area, pose, point, valid, out):
    tiles, slots = area.shape[1], out.shape[1]
    row_id = lax.broadcasted_iota(jnp.int32, (tiles, tiles), 0)
    col_id = lax.broadcasted_iota(jnp.int32, (tiles, tiles), 1)
    lane = lax.broadcasted_iota(jnp.int32, (tiles, slots), 1)

    def column(row):
        return jnp.sum(jnp.where(row_id == col_id, row, 0.0), axis=1, keepdims=True)

    def half_up(v, unit):
        whole = v.astype(jnp.int32) + (unit - 1)
        return (whole & ~(unit - 1)).astype(jnp.float32)

    def arrange(key, phase):
        key_col, phase_col = column(key), column(phase)
        same = jnp.where((key_col == key) & (real_col > 0.0) & (real > 0.0), 1.0, 0.0)
        count = jnp.sum(same, axis=0, keepdims=True)
        rank = jnp.sum(jnp.where(row_id < col_id, same, 0.0), axis=0, keepdims=True)
        rank_col = jnp.sum(jnp.where(col_id < row_id, same, 0.0), axis=1, keepdims=True)
        room = jnp.where((rank == 0.0) & (real > 0.0), half_up(count, 2), 0.0)
        place = jnp.sum(jnp.where(key < key_col, room, 0.0), axis=1, keepdims=True) + rank_col
        end, gap, bounds = 0.0, 0.0, []
        for k in range(AREAS):
            used = jnp.sum(jnp.where(phase == k, room, 0.0), axis=1, keepdims=True)
            place = place + jnp.where(phase_col == k, gap, 0.0)
            padded = half_up(used, 2 * UNROLL)
            end, gap = end + padded, gap + padded - used
            bounds.append(end)
        place = jnp.where(real_col > 0.0, place, -1.0)
        return jnp.where(place.astype(jnp.int32) == lane, 1.0, 0.0), bounds

    def pick(hit, values):
        return jnp.sum(hit * values, axis=0, keepdims=True)

    real = valid[...].astype(jnp.float32)
    real_col = column(real)
    area_row = area[...].astype(jnp.float32)
    pose_row = pose[...].astype(jnp.float32)
    point_row = point[...].astype(jnp.float32)
    pose_col, point_col = column(pose_row), column(point_row)
    tile_col = column(col_id[:1].astype(jnp.float32))
    points = CORES * PT_DEV
    hit, ends = arrange(area_row * points + point_row, area_row)
    rows = [
        pick(hit, tile_col),
        pick(hit, pose_col),
        pick(hit, jnp.ones_like(tile_col)),
        pick(hit, point_col),
    ]
    turned = AREAS - 1.0 - area_row
    hit, bounds = arrange(turned * 65536.0 + pose_row, turned)
    rows += [
        pick(hit, tile_col),
        pick(hit, point_col - points) + points,
        pick(hit, pose_col),
    ]
    ends += bounds
    spot = lane[:1]
    tail = jnp.zeros_like(rows[0])
    for k, end in enumerate(ends):
        tail = jnp.where(spot == k, end * (0.5 / UNROLL), tail)
    for k in range(near.shape[0]):
        tail = jnp.where(spot == NEAR + k, near[k].astype(jnp.float32), tail)
    for k, row in enumerate(rows + [tail]):
        out[k : k + 1] = row.astype(jnp.int32)


def make_plan(grid, place, near, indices):
    pose, point, valid = indices
    tiles = pose.shape[0]
    area, pose = grid.spot(pose, place)
    slots = tiles + max(AREAS * CORES * PT_DEV, min(tiles, 2 * grid.count)) + 2 * AREAS * UNROLL
    slots = -(-slots // 128) * 128
    rows = [v.reshape(1, tiles) for v in (area, pose, point, valid)]
    vmem = pl.BlockSpec(memory_space=pltpu.VMEM)
    return pl.pallas_call(
        plan_kernel,
        out_shape=jax.ShapeDtypeStruct((8, slots), jnp.int32),
        in_specs=[pl.BlockSpec(memory_space=pltpu.SMEM)] + [vmem] * 4,
        out_specs=vmem,
        compiler_params=pltpu.CompilerParams(vmem_limit_bytes=32 * tiles * slots + 2 * 1024 * 1024),
    )(near, *rows)


def join_kernel(first, second, out, sems):
    half = first.shape[0]
    copies = [
        pltpu.make_async_copy(first, out.at[pl.ds(0, half)], sems.at[0]),
        pltpu.make_async_copy(second, out.at[pl.ds(half, half)], sems.at[1]),
    ]
    for copy in copies:
        copy.start()
    for copy in copies:
        copy.wait()


def join_tiles(first, second):
    shape = (2 * first.shape[0], *first.shape[1:])
    return pl.pallas_call(
        join_kernel,
        out_shape=jax.ShapeDtypeStruct(shape, first.dtype),
        in_specs=[pl.BlockSpec(memory_space=pl.ANY)] * 2,
        out_specs=pl.BlockSpec(memory_space=pltpu.VMEM),
        scratch_shapes=[pltpu.SemaphoreType.DMA((2,))],
        compiler_params=pltpu.CompilerParams(vmem_limit_bytes=2 * 1024 * 1024),
    )(first, second)


NT = (((1,), (1,)), ((), ()))
NN = (((1,), (0,)), ((), ()))
F_TILE, F_POSE, F_REAL, F_POINT, B_TILE, B_POINT, B_POSE, ENDS = range(8)


def forward(plan, tiles, field, acc, begin, end):
    def body(i, _):
        for u in range(UNROLL):
            j = 2 * (i * UNROLL + u)
            block = [
                field[plan[F_POSE, j + h], : acc.shape[1]]
                * plan[F_REAL, j + h].astype(jnp.float32).astype(jnp.bfloat16)
                for h in range(2)
            ]
            tile = [tiles[plan[F_TILE, j + h]] for h in range(2)]
            acc[plan[F_POINT, j]] += lax.dot_general(
                jnp.concatenate(block, axis=1),
                jnp.concatenate(tile, axis=1),
                NT,
                preferred_element_type=jnp.float32,
            )
        return 0

    lax.fori_loop(begin, end, body, 0)


def backward(plan, tiles, low, total, begin, end):
    def body(i, _):
        for u in range(UNROLL):
            j = 2 * (i * UNROLL + u)
            block = [low[plan[B_POINT, j + h]] for h in range(2)]
            tile = [tiles[plan[B_TILE, j + h]] for h in range(2)]
            total[plan[B_POSE, j]] += lax.dot_general(
                jnp.concatenate(block, axis=1),
                jnp.concatenate(tile, axis=0),
                NN,
                preferred_element_type=jnp.float32,
            )
        return 0

    lax.fori_loop(begin, end, body, 0)


def assemble(pieces, field):
    start = 0
    for piece in pieces:
        field[start : start + piece.shape[0]] = piece[...]
        start += piece.shape[0]


def near_side(plan, field, sides, area):
    for side in range(sides.shape[0]):
        spot = NEAR + 2 * side

        @pl.when(plan[ENDS, spot] == area)
        def _():
            sides[side] = field[pl.ds(plan[ENDS, spot + 1], 2)]


def base_forward(plan_in, tiles, field, acc, sides, plan, sem):
    copy = pltpu.make_async_copy(plan_in, plan, sem)
    copy.start()
    acc[...] = jnp.zeros_like(acc)
    sides[...] = jnp.zeros_like(sides)
    copy.wait()
    near_side(plan, field, sides, 0)
    forward(plan, tiles, field, acc, 0, plan[ENDS, 0])


def rest_both(cuts, plan_in, tiles, part, sides_in, *refs):
    pieces, refs = refs[: -len(cuts) - 7], refs[-len(cuts) - 7 :]
    (acc, sides, low), outs, (field, total, plan, sem) = refs[:3], refs[3:-4], refs[-4:]
    copy = pltpu.make_async_copy(plan_in, plan, sem)
    copy.start()
    assemble(pieces, field)
    total[...] = jnp.zeros_like(total)
    acc[...] = part[...]
    sides[...] = sides_in[...]
    points = acc.shape[0]
    low[points] = jnp.zeros(low.shape[1:], jnp.bfloat16)
    copy.wait()
    near_side(plan, field, sides, 1)
    forward(plan, tiles, field, acc, plan[ENDS, 0], plan[ENDS, 1])
    low[:points] = acc[...].astype(jnp.bfloat16)
    backward(plan, tiles, low, total, 0, plan[ENDS, AREAS])
    start = 0
    for size, out in zip(cuts, outs):
        out[...] = total[start : start + size].astype(out.dtype)
        start += size


def base_backward(plan_in, tiles, low, base, plan, sem):
    copy = pltpu.make_async_copy(plan_in, plan, sem)
    copy.start()
    base[...] = jnp.zeros_like(base)
    copy.wait()
    backward(plan, tiles, low, base, plan[ENDS, AREAS], plan[ENDS, AREAS + 1])


def call(kernel, outs, scratch, args, kinds, tiles, share, aliases={}):
    place = {
        "a": pl.BlockSpec(memory_space=pl.ANY),
        "v": pl.BlockSpec(memory_space=pltpu.VMEM),
    }
    size = sum(math.prod(v.shape) * jnp.dtype(v.dtype).itemsize for v in scratch)
    scratch = scratch + [pltpu.SMEM(args[0].shape, jnp.int32), pltpu.SemaphoreType.DMA]
    return pl.pallas_call(
        kernel,
        out_shape=outs,
        in_specs=[place[kind] for kind in kinds],
        out_specs=[place["v"]] * len(outs),
        scratch_shapes=scratch,
        input_output_aliases=aliases,
        compiler_params=pltpu.CompilerParams(vmem_limit_bytes=size + 3 * 1024 * 1024),
        cost_estimate=pl.CostEstimate(
            flops=int(share * 4 * tiles.size * 128),
            bytes_accessed=tiles.size * 2,
            transcendentals=0,
        ),
    )(*args)


def array(lead, like, kind):
    return jax.ShapeDtypeStruct((lead, *like[1:]), kind)


def base_product(plan, tiles, base):
    rows = tiles.shape[1] // CORES
    acc = (0, rows, tiles.shape[1])
    return call(
        base_forward,
        [
            array(CORES * PT_DEV, acc, jnp.float32),
            jax.ShapeDtypeStruct((2 * CORES, 2, *base.shape[1:]), jnp.bfloat16),
        ],
        [],
        [plan, tiles, base],
        "avv",
        tiles,
        0.125,
    )


def rest_product(grid, plan, tiles, sums, pieces):
    plane = grid.plane
    rest = 2 * grid.count - plane
    if grid.sizes["y"] == 2:
        group = 2 * CORES
        cuts = [plane, plane, group] + [group] * (grid.sizes["z"] - 1)
        kinds = [jnp.bfloat16, jnp.bfloat16, jnp.float32] + [jnp.bfloat16] * (grid.sizes["z"] - 1)
    else:
        cuts, kinds = [rest], [jnp.float32]
    rows, points = sums[0].shape[1:]
    like = (0, rows, tiles.shape[2])
    _, sides, low, *outs = call(
        functools.partial(rest_both, cuts),
        [
            *[jax.ShapeDtypeStruct(v.shape, v.dtype) for v in sums],
            array(CORES * PT_DEV + 1, (0, rows, points), jnp.bfloat16),
            *[array(cut, like, kind) for cut, kind in zip(cuts, kinds)],
        ],
        [pltpu.VMEM((rest, *pieces[0].shape[1:]), jnp.bfloat16), pltpu.VMEM((rest, *like[1:]), jnp.float32)],
        [plan, tiles, *sums, *pieces],
        "avvv" + "v" * len(pieces),
        tiles,
        0.75,
        {2: 0, 3: 1},
    )
    return outs, low, sides


def base_return(grid, plan, tiles, low):
    (base,) = call(
        base_backward,
        [array(grid.plane, (0, low.shape[1], tiles.shape[2]), jnp.float32)],
        [],
        [plan, tiles, low],
        "avv",
        tiles,
        0.125,
    )
    return base


def in_order(core, mine, theirs, axis):
    low, high = jnp.where(core == 0, mine, theirs), jnp.where(core == 0, theirs, mine)
    return jnp.concatenate([low, high], axis=axis)


def on_device(jac_tiles, tile_pose, tile_point, tile_valid, prior_weight, right_side):
    grid = Grid()
    place = lax.axis_index(BOTH)
    at = grid.coords(place)
    core = at["core"]
    homes = [grid.device(at | {"core": c}) for c in range(CORES)]
    params, rhs = right_side.shape[1:]
    rows = rhs // CORES

    def half(v, which):
        return lax.dynamic_slice_in_dim(v, which * rows, rows, 1)

    def whole(*values):
        v = jnp.stack(values).reshape((-1, CORES, 2) + values[0].shape[1:])
        mine = lax.dynamic_index_in_dim(v, core, 1, keepdims=False)
        theirs = grid.swap(lax.dynamic_index_in_dim(v, 1 - core, 1, keepdims=False))
        return tuple(jnp.swapaxes(in_order(core, mine, theirs, 2), 2, 3))

    turned = jnp.swapaxes(right_side, 1, 2)
    names = jnp.stack([tile_pose, tile_point, tile_valid]).astype(jnp.float32)
    width = -(-names.shape[1] // params)
    names = jnp.pad(names, ((0, 0), (0, width * params - names.shape[1])))
    extra = jnp.concatenate([prior_weight, names.reshape(3 * width, params)])
    extra = jnp.pad(extra, ((0, -extra.shape[0] % 16), (0, 0))).reshape(2, -1, params)
    pack = lax.optimization_barrier(jnp.concatenate([half(turned, 1 - core), extra], axis=1))
    theirs = grid.swap(pack)
    theirs, sent_tiles = lax.optimization_barrier((theirs, jac_tiles))
    other_tiles = grid.swap(sent_tiles)
    right_side = in_order(core, half(turned, core), theirs[:, :rows], 0)
    notes = [v[:, rows:].reshape(-1, params) for v in (pack, theirs)]
    weights = in_order(core, notes[0][:2], notes[1][:2], 0)
    names = [v[2 : 2 + 3 * width].reshape(3, -1)[:, : tile_pose.shape[0]] for v in notes]
    shift = jnp.array([[0.0], [PT_DEV], [0.0]], jnp.float32)
    indices = jnp.concatenate([names[0], names[1] + shift], axis=1).astype(jnp.int32)
    near = []
    for home in homes:
        near += grid.spot(2 * jnp.maximum(home - 1, 0), place)
        near += grid.spot(2 * jnp.minimum(home + 1, grid.count - 1), place)
    plan = make_plan(grid, place, jnp.stack(near), indices)
    tiles = None

    def load(*arrived):
        return join_tiles(jac_tiles, *arrived) if arrived else tiles

    zero = jnp.zeros((params,), jnp.float32)
    theta = (highest + lowest) / 2.0
    delta = (highest - lowest) / 2.0
    sigma = theta / delta
    ratio = 1.0 / sigma
    step = right_side / theta
    solution = jnp.zeros(right_side.shape, jnp.float32)
    residual = right_side
    for turn in range(ITERS):
        if turn > 0:
            new_ratio = 1.0 / (2.0 * sigma - ratio)
            step = new_ratio * ratio * step + 2.0 * new_ratio / delta * residual
            ratio = new_ratio
        solution = solution + step
        low = step.astype(jnp.bfloat16)
        if turn == 0:
            extra = jnp.broadcast_to(weights[:, None, :], (2 * CORES, 16, params))
            low = jnp.concatenate([low, extra.astype(jnp.bfloat16)], axis=1)
        sums, pieces, plan, tiles = gather_field(grid, low, plan, load, *([other_tiles] if turn == 0 else []))
        rest, point_sums, sides = rest_product(grid, plan, tiles, sums, pieces)
        gram = scatter_sum(grid, plan, tiles, rest, point_sums)
        sides = sides.astype(jnp.float32)
        if turn == 0:
            w_left, w_right = [], []
            for c, home in enumerate(homes):
                first, last = home == 0, home == grid.count - 1
                left, right = sides[2 * c, :, rows], sides[2 * c + 1, :, rows]
                one, two = weights[2 * c], weights[2 * c + 1]
                w_left += [jnp.where(first, zero, left[0]), jnp.where(first, zero, two)]
                w_right += [one, jnp.where(last, one, right[1])]
            w_left = jnp.stack(w_left)[:, None, :]
            w_right = jnp.stack(w_right)[:, None, :]
        left = jnp.concatenate([sides[2 * c, :, :rows] for c in range(CORES)])
        right = []
        for c, home in enumerate(homes):
            turned = step[2 * c : 2 * c + 2][::-1]
            right.append(jnp.where(home == grid.count - 1, turned, sides[2 * c + 1, :, :rows]))
        prior = w_left * (step - left) + w_right * (step - jnp.concatenate(right))
        residual = residual - (gram + prior + damping * step)
    return whole(solution, residual)


def solution(mesh):
    return jax.shard_map(
        on_device,
        mesh=mesh,
        in_specs=(
            P(BOTH, None, None),
            P(BOTH),
            P(BOTH),
            P(BOTH),
            P(BOTH, None),
            P(BOTH, None, None),
        ),
        out_specs=(P(BOTH, None, None), P(BOTH, None, None)),
        check_vma=False,
    )
```

```python
import functools
import math

import jax
import jax.numpy as jnp
from jax import lax
from jax.experimental import pallas as pl
from jax.experimental.pallas import tpu as pltpu
from jax.sharding import PartitionSpec as P

PT_DEV = 16
ITERS = 3
CORES = 2
UNROLL = 16
AREAS = 2
NEAR = 2 * AREAS

damping = 0.5
lowest = 0.5
highest = 8.0
BOTH = ("row", "col")
ONE, TWO, BOTH_AXES = ("y", "x"), ("x", "y"), "x y"


class Grid:
    def __init__(self):
        rows = lax.axis_size("row")
        cols = lax.axis_size("col")
        self.sizes = {"y": rows // CORES, "core": CORES, "z": cols // 2, "x": 2}
        self.count = rows * cols
        self.plane = self.sizes["z"] * CORES * 2

    def coords(self, device):
        cols = self.sizes["z"] * 2
        if isinstance(device, int):
            row, col = device // cols, device % cols
            return {"y": row // 2, "core": row % 2, "z": col // 2, "x": col % 2}
        row, col = lax.div(device, cols), lax.rem(device, cols)
        return {"y": lax.div(row, 2), "core": lax.rem(row, 2), "z": lax.div(col, 2), "x": lax.rem(col, 2)}

    def device(self, at):
        row = at["y"] * 2 + at["core"]
        col = at["z"] * 2 + at["x"]
        return row * self.sizes["z"] * 2 + col

    def spot(self, pose, home):
        at, base = self.coords(lax.div(pose, 2)), self.coords(home)
        away = {a: lax.rem(at[a] - base[a] + n, n) for a, n in self.sizes.items()}
        x, y, z = away["x"], away["y"], at["z"] ^ base["z"]
        if self.sizes["y"] == 2:
            swap = base["core"] == 0
            x, y = jnp.where(swap, y, x), jnp.where(swap, x, y)
        z = jnp.where(z == 0, 0, self.sizes["z"] - z)
        chip = (y * 2 + x) * self.sizes["z"] + z
        spot = (chip * CORES + at["core"]) * 2 + lax.rem(pose, 2)
        area = jnp.where(spot < self.plane, 0, 1)
        return area, spot - area * self.plane

    def send(self, block, axes, distance):
        route = []
        for source in range(self.count):
            at = self.coords(source)
            names = axes if isinstance(axes, str) else axes[at["core"]]
            for name in names.split():
                moved = (at[name] + distance) % self.sizes[name]
                at[name] = at[name] ^ distance if name == "z" else moved
            route.append((source, self.device(at)))
        return lax.ppermute(block, BOTH, route)

    def fetch(self, block, axes, distance):
        return self.send(block, axes, -distance)

    def swap(self, block):
        return self.send(block, "core", 1)


def along_z(grid, block, beside=None):
    depth = grid.sizes["z"]
    moved = [grid.send(block, "z", r) for r in range(1, depth)]
    if beside is not None:
        moved[-1], beside = lax.optimization_barrier((moved[-1], beside))
    return jnp.concatenate([block] + moved[::-1]), beside


def gather_field(grid, low, plan, load, *held):
    wide = grid.sizes["y"]
    if wide == 2:
        base, corner = along_z(grid, low, grid.send(low, BOTH_AXES, 1))
        base, corner, plan, *held = lax.optimization_barrier((base, corner, plan, *held))
        tiles = load(*held)
        sums = base_product(plan, tiles, base)
        over = [grid.send(base, axes, 1) for axes in (ONE, TWO)]
        far, _ = along_z(grid, corner)
        far, *sums = lax.optimization_barrier((far, *sums))
        pieces = [*over, far]
    else:
        base, _ = along_z(grid, low)
        base, plan, *held = lax.optimization_barrier((base, plan, *held))
        tiles = load(*held)
        sums = base_product(plan, tiles, base)
        lines = [base] + [grid.fetch(base, "y", r) for r in range(1, wide)]
        pieces = []
        for line in lines:
            pieces += [line, grid.fetch(line, "x", 1)]
        pieces = pieces[1:]
    return sums, pieces, plan, tiles


def scatter_sum(grid, plan, tiles, rest, low):
    depth, wide = grid.sizes["z"], grid.sizes["y"]
    order = range(depth - 1, 0, -1)
    shape = (depth, 2 * CORES, low.shape[1], tiles.shape[2])

    def narrow(v):
        return v.astype(jnp.bfloat16)

    def widen(v):
        return v.astype(jnp.float32)

    diagonal = jnp.zeros((), jnp.float32)
    if wide == 2:
        one, two, here, *parts = rest
        one, two, *parts = lax.optimization_barrier((one, two, *parts))
        one, two = grid.send(one, ONE, 1), grid.send(two, TWO, 1)
        parts = [grid.send(parts[depth - r - 1], "z", r) for r in order]
        parts[0], low = lax.optimization_barrier((parts[0], low))
        base = base_return(grid, plan, tiles, low)
        *parts, one, two, base = lax.optimization_barrier((*parts, one, two, base))
        base = (base + widen(one) + widen(two)).reshape(shape)
        corner = narrow(here + sum(widen(part) for part in parts))
    else:
        total = jnp.concatenate([base_return(grid, plan, tiles, low), rest[0]])
        total = total.reshape((wide, 2) + shape)
        total = total[:, 0] + widen(grid.send(narrow(total[:, 1]), "x", 1))
        base = total[0]
        for r in range(1, wide):
            base = base + widen(grid.send(narrow(total[r]), "y", r))
        corner = None
    parts = [narrow(base[depth - r]) for r in order]
    if corner is not None:
        *parts, corner = lax.optimization_barrier((*parts, corner))
        diagonal = grid.send(corner, BOTH_AXES, 1)
    parts = [grid.send(part, "z", r) for r, part in zip(order, parts)]
    if corner is not None:
        parts[0], diagonal = lax.optimization_barrier((parts[0], diagonal))
    gram = base[0] + widen(diagonal)
    for part in parts:
        gram = gram + widen(part)
    return gram


def plan_kernel(near, area, pose, point, valid, out):
    tiles, slots = area.shape[1], out.shape[1]
    row_id = lax.broadcasted_iota(jnp.int32, (tiles, tiles), 0)
    col_id = lax.broadcasted_iota(jnp.int32, (tiles, tiles), 1)
    lane = lax.broadcasted_iota(jnp.int32, (tiles, slots), 1)

    def column(row):
        return jnp.sum(jnp.where(row_id == col_id, row, 0.0), axis=1, keepdims=True)

    def half_up(v, unit):
        whole = v.astype(jnp.int32) + (unit - 1)
        return (whole & ~(unit - 1)).astype(jnp.float32)

    def arrange(key, phase):
        key_col, phase_col = column(key), column(phase)
        same = jnp.where((key_col == key) & (real_col > 0.0) & (real > 0.0), 1.0, 0.0)
        count = jnp.sum(same, axis=0, keepdims=True)
        rank = jnp.sum(jnp.where(row_id < col_id, same, 0.0), axis=0, keepdims=True)
        rank_col = jnp.sum(jnp.where(col_id < row_id, same, 0.0), axis=1, keepdims=True)
        room = jnp.where((rank == 0.0) & (real > 0.0), half_up(count, 2), 0.0)
        place = jnp.sum(jnp.where(key < key_col, room, 0.0), axis=1, keepdims=True) + rank_col
        end, gap, bounds = 0.0, 0.0, []
        for k in range(AREAS):
            used = jnp.sum(jnp.where(phase == k, room, 0.0), axis=1, keepdims=True)
            place = place + jnp.where(phase_col == k, gap, 0.0)
            padded = half_up(used, 2 * UNROLL)
            end, gap = end + padded, gap + padded - used
            bounds.append(end)
        place = jnp.where(real_col > 0.0, place, -1.0)
        return jnp.where(place.astype(jnp.int32) == lane, 1.0, 0.0), bounds

    def pick(hit, values):
        return jnp.sum(hit * values, axis=0, keepdims=True)

    real = valid[...].astype(jnp.float32)
    real_col = column(real)
    area_row = area[...].astype(jnp.float32)
    pose_row = pose[...].astype(jnp.float32)
    point_row = point[...].astype(jnp.float32)
    pose_col, point_col = column(pose_row), column(point_row)
    tile_col = column(col_id[:1].astype(jnp.float32))
    points = CORES * PT_DEV
    hit, ends = arrange(area_row * points + point_row, area_row)
    rows = [
        pick(hit, tile_col),
        pick(hit, pose_col),
        pick(hit, jnp.ones_like(tile_col)),
        pick(hit, point_col),
    ]
    turned = AREAS - 1.0 - area_row
    hit, bounds = arrange(turned * 65536.0 + pose_row, turned)
    rows += [
        pick(hit, tile_col),
        pick(hit, point_col - points) + points,
        pick(hit, pose_col),
    ]
    ends += bounds
    spot = lane[:1]
    tail = jnp.zeros_like(rows[0])
    for k, end in enumerate(ends):
        tail = jnp.where(spot == k, end * (0.5 / UNROLL), tail)
    for k in range(near.shape[0]):
        tail = jnp.where(spot == NEAR + k, near[k].astype(jnp.float32), tail)
    for k, row in enumerate(rows + [tail]):
        out[k : k + 1] = row.astype(jnp.int32)


def make_plan(grid, place, near, indices):
    pose, point, valid = indices
    tiles = pose.shape[0]
    area, pose = grid.spot(pose, place)
    slots = tiles + max(AREAS * CORES * PT_DEV, min(tiles, 2 * grid.count)) + 2 * AREAS * UNROLL
    slots = -(-slots // 128) * 128
    rows = [v.reshape(1, tiles) for v in (area, pose, point, valid)]
    vmem = pl.BlockSpec(memory_space=pltpu.VMEM)
    return pl.pallas_call(
        plan_kernel,
        out_shape=jax.ShapeDtypeStruct((8, slots), jnp.int32),
        in_specs=[pl.BlockSpec(memory_space=pltpu.SMEM)] + [vmem] * 4,
        out_specs=vmem,
        compiler_params=pltpu.CompilerParams(vmem_limit_bytes=32 * tiles * slots + 2 * 1024 * 1024),
    )(near, *rows)


def join_kernel(first, second, out, sems):
    half = first.shape[0]
    copies = [
        pltpu.make_async_copy(first, out.at[pl.ds(0, half)], sems.at[0]),
        pltpu.make_async_copy(second, out.at[pl.ds(half, half)], sems.at[1]),
    ]
    for copy in copies:
        copy.start()
    for copy in copies:
        copy.wait()


def join_tiles(first, second):
    shape = (2 * first.shape[0], *first.shape[1:])
    return pl.pallas_call(
        join_kernel,
        out_shape=jax.ShapeDtypeStruct(shape, first.dtype),
        in_specs=[pl.BlockSpec(memory_space=pl.ANY)] * 2,
        out_specs=pl.BlockSpec(memory_space=pltpu.VMEM),
        scratch_shapes=[pltpu.SemaphoreType.DMA((2,))],
        compiler_params=pltpu.CompilerParams(vmem_limit_bytes=2 * 1024 * 1024),
    )(first, second)


NT = (((1,), (1,)), ((), ()))
NN = (((1,), (0,)), ((), ()))
F_TILE, F_POSE, F_REAL, F_POINT, B_TILE, B_POINT, B_POSE, ENDS = range(8)


def forward(plan, tiles, field, acc, begin, end):
    def body(i, _):
        for u in range(UNROLL):
            j = 2 * (i * UNROLL + u)
            block = [
                field[plan[F_POSE, j + h], : acc.shape[1]]
                * plan[F_REAL, j + h].astype(jnp.float32).astype(jnp.bfloat16)
                for h in range(2)
            ]
            tile = [tiles[plan[F_TILE, j + h]] for h in range(2)]
            acc[plan[F_POINT, j]] += lax.dot_general(
                jnp.concatenate(block, axis=1),
                jnp.concatenate(tile, axis=1),
                NT,
                preferred_element_type=jnp.float32,
            )
        return 0

    lax.fori_loop(begin, end, body, 0)


def backward(plan, tiles, low, total, begin, end):
    def body(i, _):
        for u in range(UNROLL):
            j = 2 * (i * UNROLL + u)
            block = [low[plan[B_POINT, j + h]] for h in range(2)]
            tile = [tiles[plan[B_TILE, j + h]] for h in range(2)]
            total[plan[B_POSE, j]] += lax.dot_general(
                jnp.concatenate(block, axis=1),
                jnp.concatenate(tile, axis=0),
                NN,
                preferred_element_type=jnp.float32,
            )
        return 0

    lax.fori_loop(begin, end, body, 0)


def assemble(pieces, field):
    start = 0
    for piece in pieces:
        field[start : start + piece.shape[0]] = piece[...]
        start += piece.shape[0]


def near_side(plan, field, sides, area):
    for side in range(sides.shape[0]):
        spot = NEAR + 2 * side

        @pl.when(plan[ENDS, spot] == area)
        def _():
            sides[side] = field[pl.ds(plan[ENDS, spot + 1], 2)]


def base_forward(plan_in, tiles, field, acc, sides, plan, sem):
    copy = pltpu.make_async_copy(plan_in, plan, sem)
    copy.start()
    acc[...] = jnp.zeros_like(acc)
    sides[...] = jnp.zeros_like(sides)
    copy.wait()
    near_side(plan, field, sides, 0)
    forward(plan, tiles, field, acc, 0, plan[ENDS, 0])


def rest_both(cuts, plan_in, tiles, part, sides_in, *refs):
    pieces, refs = refs[: -len(cuts) - 7], refs[-len(cuts) - 7 :]
    (acc, sides, low), outs, (field, total, plan, sem) = refs[:3], refs[3:-4], refs[-4:]
    copy = pltpu.make_async_copy(plan_in, plan, sem)
    copy.start()
    assemble(pieces, field)
    total[...] = jnp.zeros_like(total)
    acc[...] = part[...]
    sides[...] = sides_in[...]
    points = acc.shape[0]
    low[points] = jnp.zeros(low.shape[1:], jnp.bfloat16)
    copy.wait()
    near_side(plan, field, sides, 1)
    forward(plan, tiles, field, acc, plan[ENDS, 0], plan[ENDS, 1])
    low[:points] = acc[...].astype(jnp.bfloat16)
    backward(plan, tiles, low, total, 0, plan[ENDS, AREAS])
    start = 0
    for size, out in zip(cuts, outs):
        out[...] = total[start : start + size].astype(out.dtype)
        start += size


def base_backward(plan_in, tiles, low, base, plan, sem):
    copy = pltpu.make_async_copy(plan_in, plan, sem)
    copy.start()
    base[...] = jnp.zeros_like(base)
    copy.wait()
    backward(plan, tiles, low, base, plan[ENDS, AREAS], plan[ENDS, AREAS + 1])


def call(kernel, outs, scratch, args, kinds, tiles, share, aliases={}):
    place = {
        "a": pl.BlockSpec(memory_space=pl.ANY),
        "v": pl.BlockSpec(memory_space=pltpu.VMEM),
    }
    size = sum(math.prod(v.shape) * jnp.dtype(v.dtype).itemsize for v in scratch)
    scratch = scratch + [pltpu.SMEM(args[0].shape, jnp.int32), pltpu.SemaphoreType.DMA]
    return pl.pallas_call(
        kernel,
        out_shape=outs,
        in_specs=[place[kind] for kind in kinds],
        out_specs=[place["v"]] * len(outs),
        scratch_shapes=scratch,
        input_output_aliases=aliases,
        compiler_params=pltpu.CompilerParams(vmem_limit_bytes=size + 3 * 1024 * 1024),
        cost_estimate=pl.CostEstimate(
            flops=int(share * 4 * tiles.size * 128),
            bytes_accessed=tiles.size * 2,
            transcendentals=0,
        ),
    )(*args)


def array(lead, like, kind):
    return jax.ShapeDtypeStruct((lead, *like[1:]), kind)


def base_product(plan, tiles, base):
    rows = tiles.shape[1] // CORES
    acc = (0, rows, tiles.shape[1])
    return call(
        base_forward,
        [
            array(CORES * PT_DEV, acc, jnp.float32),
            jax.ShapeDtypeStruct((2 * CORES, 2, *base.shape[1:]), jnp.bfloat16),
        ],
        [],
        [plan, tiles, base],
        "avv",
        tiles,
        0.125,
    )


def rest_product(grid, plan, tiles, sums, pieces):
    plane = grid.plane
    rest = 2 * grid.count - plane
    if grid.sizes["y"] == 2:
        group = 2 * CORES
        cuts = [plane, plane, group] + [group] * (grid.sizes["z"] - 1)
        kinds = [jnp.bfloat16, jnp.bfloat16, jnp.float32] + [jnp.bfloat16] * (grid.sizes["z"] - 1)
    else:
        cuts, kinds = [rest], [jnp.float32]
    rows, points = sums[0].shape[1:]
    like = (0, rows, tiles.shape[2])
    _, sides, low, *outs = call(
        functools.partial(rest_both, cuts),
        [
            *[jax.ShapeDtypeStruct(v.shape, v.dtype) for v in sums],
            array(CORES * PT_DEV + 1, (0, rows, points), jnp.bfloat16),
            *[array(cut, like, kind) for cut, kind in zip(cuts, kinds)],
        ],
        [pltpu.VMEM((rest, *pieces[0].shape[1:]), jnp.bfloat16), pltpu.VMEM((rest, *like[1:]), jnp.float32)],
        [plan, tiles, *sums, *pieces],
        "avvv" + "v" * len(pieces),
        tiles,
        0.75,
        {2: 0, 3: 1},
    )
    return outs, low, sides


def base_return(grid, plan, tiles, low):
    (base,) = call(
        base_backward,
        [array(grid.plane, (0, low.shape[1], tiles.shape[2]), jnp.float32)],
        [],
        [plan, tiles, low],
        "avv",
        tiles,
        0.125,
    )
    return base


def in_order(core, mine, theirs, axis):
    low, high = jnp.where(core == 0, mine, theirs), jnp.where(core == 0, theirs, mine)
    return jnp.concatenate([low, high], axis=axis)


def on_device(jac_tiles, tile_pose, tile_point, tile_valid, prior_weight, right_side):
    grid = Grid()
    place = lax.axis_index(BOTH)
    at = grid.coords(place)
    core = at["core"]
    homes = [grid.device(at | {"core": c}) for c in range(CORES)]
    params, rhs = right_side.shape[1:]
    rows = rhs // CORES

    def half(v, which):
        return lax.dynamic_slice_in_dim(v, which * rows, rows, 1)

    def whole(*values):
        v = jnp.stack(values).reshape((-1, CORES, 2) + values[0].shape[1:])
        mine = lax.dynamic_index_in_dim(v, core, 1, keepdims=False)
        theirs = grid.swap(lax.dynamic_index_in_dim(v, 1 - core, 1, keepdims=False))
        return tuple(jnp.swapaxes(in_order(core, mine, theirs, 2), 2, 3))

    turned = jnp.swapaxes(right_side, 1, 2)
    names = jnp.stack([tile_pose, tile_point, tile_valid]).astype(jnp.float32)
    width = -(-names.shape[1] // params)
    names = jnp.pad(names, ((0, 0), (0, width * params - names.shape[1])))
    extra = jnp.concatenate([prior_weight, names.reshape(3 * width, params)])
    extra = jnp.pad(extra, ((0, -extra.shape[0] % 16), (0, 0))).reshape(2, -1, params)
    pack = lax.optimization_barrier(jnp.concatenate([half(turned, 1 - core), extra], axis=1))
    theirs = grid.swap(pack)
    theirs, sent_tiles = lax.optimization_barrier((theirs, jac_tiles))
    other_tiles = grid.swap(sent_tiles)
    right_side = in_order(core, half(turned, core), theirs[:, :rows], 0)
    notes = [v[:, rows:].reshape(-1, params) for v in (pack, theirs)]
    weights = in_order(core, notes[0][:2], notes[1][:2], 0)
    names = [v[2 : 2 + 3 * width].reshape(3, -1)[:, : tile_pose.shape[0]] for v in notes]
    shift = jnp.array([[0.0], [PT_DEV], [0.0]], jnp.float32)
    indices = jnp.concatenate([names[0], names[1] + shift], axis=1).astype(jnp.int32)
    near = []
    for home in homes:
        near += grid.spot(2 * jnp.maximum(home - 1, 0), place)
        near += grid.spot(2 * jnp.minimum(home + 1, grid.count - 1), place)
    plan = make_plan(grid, place, jnp.stack(near), indices)
    tiles = None

    def load(*arrived):
        return join_tiles(jac_tiles, *arrived) if arrived else tiles

    zero = jnp.zeros((params,), jnp.float32)
    theta = (highest + lowest) / 2.0
    delta = (highest - lowest) / 2.0
    sigma = theta / delta
    ratio = 1.0 / sigma
    step = right_side / theta
    solution = jnp.zeros(right_side.shape, jnp.float32)
    residual = right_side
    for turn in range(ITERS):
        if turn > 0:
            new_ratio = 1.0 / (2.0 * sigma - ratio)
            step = new_ratio * ratio * step + 2.0 * new_ratio / delta * residual
            ratio = new_ratio
        solution = solution + step
        low = step.astype(jnp.bfloat16)
        if turn == 0:
            extra = jnp.broadcast_to(weights[:, None, :], (2 * CORES, 16, params))
            low = jnp.concatenate([low, extra.astype(jnp.bfloat16)], axis=1)
        sums, pieces, plan, tiles = gather_field(grid, low, plan, load, *([other_tiles] if turn == 0 else []))
        rest, point_sums, sides = rest_product(grid, plan, tiles, sums, pieces)
        gram = scatter_sum(grid, plan, tiles, rest, point_sums)
        sides = sides.astype(jnp.float32)
        if turn == 0:
            w_left, w_right = [], []
            for c, home in enumerate(homes):
                first, last = home == 0, home == grid.count - 1
                left, right = sides[2 * c, :, rows], sides[2 * c + 1, :, rows]
                one, two = weights[2 * c], weights[2 * c + 1]
                w_left += [jnp.where(first, zero, left[0]), jnp.where(first, zero, two)]
                w_right += [one, jnp.where(last, one, right[1])]
            w_left = jnp.stack(w_left)[:, None, :]
            w_right = jnp.stack(w_right)[:, None, :]
        left = jnp.concatenate([sides[2 * c, :, :rows] for c in range(CORES)])
        right = []
        for c, home in enumerate(homes):
            turned = step[2 * c : 2 * c + 2][::-1]
            right.append(jnp.where(home == grid.count - 1, turned, sides[2 * c + 1, :, :rows]))
        prior = w_left * (step - left) + w_right * (step - jnp.concatenate(right))
        residual = residual - (gram + prior + damping * step)
    return whole(solution, residual)


def solution(mesh):
    return jax.shard_map(
        on_device,
        mesh=mesh,
        in_specs=(
            P(BOTH, None, None),
            P(BOTH),
            P(BOTH),
            P(BOTH),
            P(BOTH, None),
            P(BOTH, None, None),
        ),
        out_specs=(P(BOTH, None, None), P(BOTH, None, None)),
        check_vma=False,
    )
```

```python
import functools
import math

import jax
import jax.numpy as jnp
from jax import lax
from jax.experimental import pallas as pl
from jax.experimental.pallas import tpu as pltpu
from jax.sharding import PartitionSpec as P

PT_DEV = 16
ITERS = 3
CORES = 2
UNROLL = 16
AREAS = 2
NEAR = 2 * AREAS

damping = 0.5
lowest = 0.5
highest = 8.0
BOTH = ("row", "col")
ONE, TWO, BOTH_AXES = ("y", "x"), ("x", "y"), "x y"


class Grid:
    def __init__(self):
        rows = lax.axis_size("row")
        cols = lax.axis_size("col")
        self.sizes = {"y": rows // CORES, "core": CORES, "z": cols // 2, "x": 2}
        self.count = rows * cols
        self.plane = self.sizes["z"] * CORES * 2

    def coords(self, device):
        cols = self.sizes["z"] * 2
        if isinstance(device, int):
            row, col = device // cols, device % cols
            return {"y": row // 2, "core": row % 2, "z": col // 2, "x": col % 2}
        row, col = lax.div(device, cols), lax.rem(device, cols)
        return {"y": lax.div(row, 2), "core": lax.rem(row, 2), "z": lax.div(col, 2), "x": lax.rem(col, 2)}

    def device(self, at):
        row = at["y"] * 2 + at["core"]
        col = at["z"] * 2 + at["x"]
        return row * self.sizes["z"] * 2 + col

    def spot(self, pose, home):
        at, base = self.coords(lax.div(pose, 2)), self.coords(home)
        away = {a: lax.rem(at[a] - base[a] + n, n) for a, n in self.sizes.items()}
        x, y, z = away["x"], away["y"], at["z"] ^ base["z"]
        if self.sizes["y"] == 2:
            swap = base["core"] == 0
            x, y = jnp.where(swap, y, x), jnp.where(swap, x, y)
        z = jnp.where(z == 0, 0, self.sizes["z"] - z)
        chip = (y * 2 + x) * self.sizes["z"] + z
        spot = (chip * CORES + at["core"]) * 2 + lax.rem(pose, 2)
        area = jnp.where(spot < self.plane, 0, 1)
        return area, spot - area * self.plane

    def send(self, block, axes, distance):
        route = []
        for source in range(self.count):
            at = self.coords(source)
            names = axes if isinstance(axes, str) else axes[at["core"]]
            for name in names.split():
                moved = (at[name] + distance) % self.sizes[name]
                at[name] = at[name] ^ distance if name == "z" else moved
            route.append((source, self.device(at)))
        return lax.ppermute(block, BOTH, route)

    def fetch(self, block, axes, distance):
        return self.send(block, axes, -distance)

    def swap(self, block):
        return self.send(block, "core", 1)


def along_z(grid, block, beside=None):
    depth = grid.sizes["z"]
    moved = [grid.send(block, "z", r) for r in range(1, depth)]
    if beside is not None:
        moved[-1], beside = lax.optimization_barrier((moved[-1], beside))
    return jnp.concatenate([block] + moved[::-1]), beside


def gather_field(grid, low, plan, load, *held):
    wide = grid.sizes["y"]
    if wide == 2:
        base, corner = along_z(grid, low, grid.send(low, BOTH_AXES, 1))
        base, corner, plan, *held = lax.optimization_barrier((base, corner, plan, *held))
        tiles = load(*held)
        sums = base_product(plan, tiles, base)
        over = [grid.send(base, axes, 1) for axes in (ONE, TWO)]
        far, _ = along_z(grid, corner)
        far, *sums = lax.optimization_barrier((far, *sums))
        pieces = [*over, far]
    else:
        base, _ = along_z(grid, low)
        base, plan, *held = lax.optimization_barrier((base, plan, *held))
        tiles = load(*held)
        sums = base_product(plan, tiles, base)
        lines = [base] + [grid.fetch(base, "y", r) for r in range(1, wide)]
        pieces = []
        for line in lines:
            pieces += [line, grid.fetch(line, "x", 1)]
        pieces = pieces[1:]
    return sums, pieces, plan, tiles


def scatter_sum(grid, plan, tiles, rest, low):
    depth, wide = grid.sizes["z"], grid.sizes["y"]
    order = range(depth - 1, 0, -1)
    shape = (depth, 2 * CORES, low.shape[1], tiles.shape[2])

    def narrow(v):
        return v.astype(jnp.bfloat16)

    def widen(v):
        return v.astype(jnp.float32)

    diagonal = jnp.zeros((), jnp.float32)
    if wide == 2:
        one, two, here, *parts = rest
        one, two, *parts = lax.optimization_barrier((one, two, *parts))
        one, two = grid.send(one, ONE, 1), grid.send(two, TWO, 1)
        parts = [grid.send(parts[depth - r - 1], "z", r) for r in order]
        base = base_return(grid, plan, tiles, low)
        *parts, one, two, base = lax.optimization_barrier((*parts, one, two, base))
        base = (base + widen(one) + widen(two)).reshape(shape)
        corner = narrow(here + sum(widen(part) for part in parts))
    else:
        total = jnp.concatenate([base_return(grid, plan, tiles, low), rest[0]])
        total = total.reshape((wide, 2) + shape)
        total = total[:, 0] + widen(grid.send(narrow(total[:, 1]), "x", 1))
        base = total[0]
        for r in range(1, wide):
            base = base + widen(grid.send(narrow(total[r]), "y", r))
        corner = None
    parts = [narrow(base[depth - r]) for r in order]
    if corner is not None:
        *parts, corner = lax.optimization_barrier((*parts, corner))
        diagonal = grid.send(corner, BOTH_AXES, 1)
    parts = [grid.send(part, "z", r) for r, part in zip(order, parts)]
    if corner is not None:
        parts[0], diagonal = lax.optimization_barrier((parts[0], diagonal))
    gram = base[0] + widen(diagonal)
    for part in parts:
        gram = gram + widen(part)
    return gram


def plan_kernel(near, area, pose, point, valid, out):
    tiles, slots = area.shape[1], out.shape[1]
    row_id = lax.broadcasted_iota(jnp.int32, (tiles, tiles), 0)
    col_id = lax.broadcasted_iota(jnp.int32, (tiles, tiles), 1)
    lane = lax.broadcasted_iota(jnp.int32, (tiles, slots), 1)

    def column(row):
        return jnp.sum(jnp.where(row_id == col_id, row, 0.0), axis=1, keepdims=True)

    def half_up(v, unit):
        whole = v.astype(jnp.int32) + (unit - 1)
        return (whole & ~(unit - 1)).astype(jnp.float32)

    def arrange(key, phase):
        key_col, phase_col = column(key), column(phase)
        same = jnp.where((key_col == key) & (real_col > 0.0) & (real > 0.0), 1.0, 0.0)
        count = jnp.sum(same, axis=0, keepdims=True)
        rank = jnp.sum(jnp.where(row_id < col_id, same, 0.0), axis=0, keepdims=True)
        rank_col = jnp.sum(jnp.where(col_id < row_id, same, 0.0), axis=1, keepdims=True)
        room = jnp.where((rank == 0.0) & (real > 0.0), half_up(count, 2), 0.0)
        place = jnp.sum(jnp.where(key < key_col, room, 0.0), axis=1, keepdims=True) + rank_col
        end, gap, bounds = 0.0, 0.0, []
        for k in range(AREAS):
            used = jnp.sum(jnp.where(phase == k, room, 0.0), axis=1, keepdims=True)
            place = place + jnp.where(phase_col == k, gap, 0.0)
            padded = half_up(used, 2 * UNROLL)
            end, gap = end + padded, gap + padded - used
            bounds.append(end)
        place = jnp.where(real_col > 0.0, place, -1.0)
        return jnp.where(place.astype(jnp.int32) == lane, 1.0, 0.0), bounds

    def pick(hit, values):
        return jnp.sum(hit * values, axis=0, keepdims=True)

    real = valid[...].astype(jnp.float32)
    real_col = column(real)
    area_row = area[...].astype(jnp.float32)
    pose_row = pose[...].astype(jnp.float32)
    point_row = point[...].astype(jnp.float32)
    pose_col, point_col = column(pose_row), column(point_row)
    tile_col = column(col_id[:1].astype(jnp.float32))
    points = CORES * PT_DEV
    hit, ends = arrange(area_row * points + point_row, area_row)
    rows = [
        pick(hit, tile_col),
        pick(hit, pose_col),
        pick(hit, jnp.ones_like(tile_col)),
        pick(hit, point_col),
    ]
    turned = AREAS - 1.0 - area_row
    hit, bounds = arrange(turned * 65536.0 + pose_row, turned)
    rows += [
        pick(hit, tile_col),
        pick(hit, point_col - points) + points,
        pick(hit, pose_col),
    ]
    ends += bounds
    spot = lane[:1]
    tail = jnp.zeros_like(rows[0])
    for k, end in enumerate(ends):
        tail = jnp.where(spot == k, end * (0.5 / UNROLL), tail)
    for k in range(near.shape[0]):
        tail = jnp.where(spot == NEAR + k, near[k].astype(jnp.float32), tail)
    for k, row in enumerate(rows + [tail]):
        out[k : k + 1] = row.astype(jnp.int32)


def make_plan(grid, place, near, indices):
    pose, point, valid = indices
    tiles = pose.shape[0]
    area, pose = grid.spot(pose, place)
    slots = tiles + max(AREAS * CORES * PT_DEV, min(tiles, 2 * grid.count)) + 2 * AREAS * UNROLL
    slots = -(-slots // 128) * 128
    rows = [v.reshape(1, tiles) for v in (area, pose, point, valid)]
    vmem = pl.BlockSpec(memory_space=pltpu.VMEM)
    return pl.pallas_call(
        plan_kernel,
        out_shape=jax.ShapeDtypeStruct((8, slots), jnp.int32),
        in_specs=[pl.BlockSpec(memory_space=pltpu.SMEM)] + [vmem] * 4,
        out_specs=vmem,
        compiler_params=pltpu.CompilerParams(vmem_limit_bytes=32 * tiles * slots + 2 * 1024 * 1024),
    )(near, *rows)


def join_kernel(first, second, out, sems):
    half = first.shape[0]
    copies = [
        pltpu.make_async_copy(first, out.at[pl.ds(0, half)], sems.at[0]),
        pltpu.make_async_copy(second, out.at[pl.ds(half, half)], sems.at[1]),
    ]
    for copy in copies:
        copy.start()
    for copy in copies:
        copy.wait()


def join_tiles(first, second):
    shape = (2 * first.shape[0], *first.shape[1:])
    return pl.pallas_call(
        join_kernel,
        out_shape=jax.ShapeDtypeStruct(shape, first.dtype),
        in_specs=[pl.BlockSpec(memory_space=pl.ANY)] * 2,
        out_specs=pl.BlockSpec(memory_space=pltpu.VMEM),
        scratch_shapes=[pltpu.SemaphoreType.DMA((2,))],
        compiler_params=pltpu.CompilerParams(vmem_limit_bytes=2 * 1024 * 1024),
    )(first, second)


NT = (((1,), (1,)), ((), ()))
NN = (((1,), (0,)), ((), ()))
F_TILE, F_POSE, F_REAL, F_POINT, B_TILE, B_POINT, B_POSE, ENDS = range(8)


def forward(plan, tiles, field, acc, begin, end):
    def body(i, _):
        for u in range(UNROLL):
            j = 2 * (i * UNROLL + u)
            block = [
                field[plan[F_POSE, j + h], : acc.shape[1]]
                * plan[F_REAL, j + h].astype(jnp.float32).astype(jnp.bfloat16)
                for h in range(2)
            ]
            tile = [tiles[plan[F_TILE, j + h]] for h in range(2)]
            acc[plan[F_POINT, j]] += lax.dot_general(
                jnp.concatenate(block, axis=1),
                jnp.concatenate(tile, axis=1),
                NT,
                preferred_element_type=jnp.float32,
            )
        return 0

    lax.fori_loop(begin, end, body, 0)


def backward(plan, tiles, low, total, begin, end):
    def body(i, _):
        for u in range(UNROLL):
            j = 2 * (i * UNROLL + u)
            block = [low[plan[B_POINT, j + h]] for h in range(2)]
            tile = [tiles[plan[B_TILE, j + h]] for h in range(2)]
            total[plan[B_POSE, j]] += lax.dot_general(
                jnp.concatenate(block, axis=1),
                jnp.concatenate(tile, axis=0),
                NN,
                preferred_element_type=jnp.float32,
            )
        return 0

    lax.fori_loop(begin, end, body, 0)


def assemble(pieces, field):
    start = 0
    for piece in pieces:
        field[start : start + piece.shape[0]] = piece[...]
        start += piece.shape[0]


def near_side(plan, field, sides, area):
    for side in range(sides.shape[0]):
        spot = NEAR + 2 * side

        @pl.when(plan[ENDS, spot] == area)
        def _():
            sides[side] = field[pl.ds(plan[ENDS, spot + 1], 2)]


def base_forward(plan_in, tiles, field, acc, sides, plan, sem):
    copy = pltpu.make_async_copy(plan_in, plan, sem)
    copy.start()
    acc[...] = jnp.zeros_like(acc)
    sides[...] = jnp.zeros_like(sides)
    copy.wait()
    near_side(plan, field, sides, 0)
    forward(plan, tiles, field, acc, 0, plan[ENDS, 0])


def rest_both(cuts, plan_in, tiles, part, sides_in, *refs):
    pieces, refs = refs[: -len(cuts) - 7], refs[-len(cuts) - 7 :]
    (acc, sides, low), outs, (field, total, plan, sem) = refs[:3], refs[3:-4], refs[-4:]
    copy = pltpu.make_async_copy(plan_in, plan, sem)
    copy.start()
    assemble(pieces, field)
    total[...] = jnp.zeros_like(total)
    acc[...] = part[...]
    sides[...] = sides_in[...]
    points = acc.shape[0]
    low[points] = jnp.zeros(low.shape[1:], jnp.bfloat16)
    copy.wait()
    near_side(plan, field, sides, 1)
    forward(plan, tiles, field, acc, plan[ENDS, 0], plan[ENDS, 1])
    low[:points] = acc[...].astype(jnp.bfloat16)
    backward(plan, tiles, low, total, 0, plan[ENDS, AREAS])
    start = 0
    for size, out in zip(cuts, outs):
        out[...] = total[start : start + size].astype(out.dtype)
        start += size


def base_backward(plan_in, tiles, low, base, plan, sem):
    copy = pltpu.make_async_copy(plan_in, plan, sem)
    copy.start()
    base[...] = jnp.zeros_like(base)
    copy.wait()
    backward(plan, tiles, low, base, plan[ENDS, AREAS], plan[ENDS, AREAS + 1])


def call(kernel, outs, scratch, args, kinds, tiles, share, aliases={}):
    place = {
        "a": pl.BlockSpec(memory_space=pl.ANY),
        "v": pl.BlockSpec(memory_space=pltpu.VMEM),
    }
    size = sum(math.prod(v.shape) * jnp.dtype(v.dtype).itemsize for v in scratch)
    scratch = scratch + [pltpu.SMEM(args[0].shape, jnp.int32), pltpu.SemaphoreType.DMA]
    return pl.pallas_call(
        kernel,
        out_shape=outs,
        in_specs=[place[kind] for kind in kinds],
        out_specs=[place["v"]] * len(outs),
        scratch_shapes=scratch,
        input_output_aliases=aliases,
        compiler_params=pltpu.CompilerParams(vmem_limit_bytes=size + 3 * 1024 * 1024),
        cost_estimate=pl.CostEstimate(
            flops=int(share * 4 * tiles.size * 128),
            bytes_accessed=tiles.size * 2,
            transcendentals=0,
        ),
    )(*args)


def array(lead, like, kind):
    return jax.ShapeDtypeStruct((lead, *like[1:]), kind)


def base_product(plan, tiles, base):
    rows = tiles.shape[1] // CORES
    acc = (0, rows, tiles.shape[1])
    return call(
        base_forward,
        [
            array(CORES * PT_DEV, acc, jnp.float32),
            jax.ShapeDtypeStruct((2 * CORES, 2, *base.shape[1:]), jnp.bfloat16),
        ],
        [],
        [plan, tiles, base],
        "avv",
        tiles,
        0.125,
    )


def rest_product(grid, plan, tiles, sums, pieces):
    plane = grid.plane
    rest = 2 * grid.count - plane
    if grid.sizes["y"] == 2:
        group = 2 * CORES
        cuts = [plane, plane, group] + [group] * (grid.sizes["z"] - 1)
        kinds = [jnp.bfloat16, jnp.bfloat16, jnp.float32] + [jnp.bfloat16] * (grid.sizes["z"] - 1)
    else:
        cuts, kinds = [rest], [jnp.float32]
    rows, points = sums[0].shape[1:]
    like = (0, rows, tiles.shape[2])
    _, sides, low, *outs = call(
        functools.partial(rest_both, cuts),
        [
            *[jax.ShapeDtypeStruct(v.shape, v.dtype) for v in sums],
            array(CORES * PT_DEV + 1, (0, rows, points), jnp.bfloat16),
            *[array(cut, like, kind) for cut, kind in zip(cuts, kinds)],
        ],
        [pltpu.VMEM((rest, *pieces[0].shape[1:]), jnp.bfloat16), pltpu.VMEM((rest, *like[1:]), jnp.float32)],
        [plan, tiles, *sums, *pieces],
        "avvv" + "v" * len(pieces),
        tiles,
        0.75,
        {2: 0, 3: 1},
    )
    return outs, low, sides


def base_return(grid, plan, tiles, low):
    (base,) = call(
        base_backward,
        [array(grid.plane, (0, low.shape[1], tiles.shape[2]), jnp.float32)],
        [],
        [plan, tiles, low],
        "avv",
        tiles,
        0.125,
    )
    return base


def in_order(core, mine, theirs, axis):
    low, high = jnp.where(core == 0, mine, theirs), jnp.where(core == 0, theirs, mine)
    return jnp.concatenate([low, high], axis=axis)


def on_device(jac_tiles, tile_pose, tile_point, tile_valid, prior_weight, right_side):
    grid = Grid()
    place = lax.axis_index(BOTH)
    at = grid.coords(place)
    core = at["core"]
    homes = [grid.device(at | {"core": c}) for c in range(CORES)]
    params, rhs = right_side.shape[1:]
    rows = rhs // CORES

    def half(v, which):
        return lax.dynamic_slice_in_dim(v, which * rows, rows, 1)

    def whole(*values):
        v = jnp.stack(values).reshape((-1, CORES, 2) + values[0].shape[1:])
        mine = lax.dynamic_index_in_dim(v, core, 1, keepdims=False)
        theirs = grid.swap(lax.dynamic_index_in_dim(v, 1 - core, 1, keepdims=False))
        return tuple(jnp.swapaxes(in_order(core, mine, theirs, 2), 2, 3))

    turned = jnp.swapaxes(right_side, 1, 2)
    names = jnp.stack([tile_pose, tile_point, tile_valid]).astype(jnp.float32)
    width = -(-names.shape[1] // params)
    names = jnp.pad(names, ((0, 0), (0, width * params - names.shape[1])))
    extra = jnp.concatenate([prior_weight, names.reshape(3 * width, params)])
    extra = jnp.pad(extra, ((0, -extra.shape[0] % 16), (0, 0))).reshape(2, -1, params)
    pack = lax.optimization_barrier(jnp.concatenate([half(turned, 1 - core), extra], axis=1))
    theirs = grid.swap(pack)
    theirs, sent_tiles = lax.optimization_barrier((theirs, jac_tiles))
    other_tiles = grid.swap(sent_tiles)
    right_side = in_order(core, half(turned, core), theirs[:, :rows], 0)
    notes = [v[:, rows:].reshape(-1, params) for v in (pack, theirs)]
    weights = in_order(core, notes[0][:2], notes[1][:2], 0)
    names = [v[2 : 2 + 3 * width].reshape(3, -1)[:, : tile_pose.shape[0]] for v in notes]
    shift = jnp.array([[0.0], [PT_DEV], [0.0]], jnp.float32)
    indices = jnp.concatenate([names[0], names[1] + shift], axis=1).astype(jnp.int32)
    near = []
    for home in homes:
        near += grid.spot(2 * jnp.maximum(home - 1, 0), place)
        near += grid.spot(2 * jnp.minimum(home + 1, grid.count - 1), place)
    plan = make_plan(grid, place, jnp.stack(near), indices)
    tiles = None

    def load(*arrived):
        return join_tiles(jac_tiles, *arrived) if arrived else tiles

    zero = jnp.zeros((params,), jnp.float32)
    theta = (highest + lowest) / 2.0
    delta = (highest - lowest) / 2.0
    sigma = theta / delta
    ratio = 1.0 / sigma
    step = right_side / theta
    solution = jnp.zeros(right_side.shape, jnp.float32)
    residual = right_side
    for turn in range(ITERS):
        if turn > 0:
            new_ratio = 1.0 / (2.0 * sigma - ratio)
            step = new_ratio * ratio * step + 2.0 * new_ratio / delta * residual
            ratio = new_ratio
        solution = solution + step
        low = step.astype(jnp.bfloat16)
        if turn == 0:
            extra = jnp.broadcast_to(weights[:, None, :], (2 * CORES, 16, params))
            low = jnp.concatenate([low, extra.astype(jnp.bfloat16)], axis=1)
        sums, pieces, plan, tiles = gather_field(grid, low, plan, load, *([other_tiles] if turn == 0 else []))
        rest, point_sums, sides = rest_product(grid, plan, tiles, sums, pieces)
        gram = scatter_sum(grid, plan, tiles, rest, point_sums)
        sides = sides.astype(jnp.float32)
        if turn == 0:
            w_left, w_right = [], []
            for c, home in enumerate(homes):
                first, last = home == 0, home == grid.count - 1
                left, right = sides[2 * c, :, rows], sides[2 * c + 1, :, rows]
                one, two = weights[2 * c], weights[2 * c + 1]
                w_left += [jnp.where(first, zero, left[0]), jnp.where(first, zero, two)]
                w_right += [one, jnp.where(last, one, right[1])]
            w_left = jnp.stack(w_left)[:, None, :]
            w_right = jnp.stack(w_right)[:, None, :]
        left = jnp.concatenate([sides[2 * c, :, :rows] for c in range(CORES)])
        right = []
        for c, home in enumerate(homes):
            turned = step[2 * c : 2 * c + 2][::-1]
            right.append(jnp.where(home == grid.count - 1, turned, sides[2 * c + 1, :, :rows]))
        prior = w_left * (step - left) + w_right * (step - jnp.concatenate(right))
        residual = residual - (gram + prior + damping * step)
    return whole(solution, residual)


def solution(mesh):
    return jax.shard_map(
        on_device,
        mesh=mesh,
        in_specs=(
            P(BOTH, None, None),
            P(BOTH),
            P(BOTH),
            P(BOTH),
            P(BOTH, None),
            P(BOTH, None, None),
        ),
        out_specs=(P(BOTH, None, None), P(BOTH, None, None)),
        check_vma=False,
    )
```
